32 devices in a mesh: tm: 8 (over y, x, core), tile: 4 (over z).
Axes of the slice: x: 2, y: 2, z: 4, core: 2. Of those that a mesh axis runs over, the one named last changes fastest.
Arguments:
- seg_gain: bfloat16 [8, 1024, 1024], P('tm', 'tile'), may hold values from -0.1875 to 0.1875
- seg_offset: float32 [8, 1024], P('tm', 'tile'), may hold values from -6 to 6
- seg_noise: bfloat16 [8, 1024, 1024], P('tm', 'tile'), as said below
- end_mean: bfloat16 [2, 1024], P(None, 'tile'), may hold values from -6 to 6
- end_cov: bfloat16 [2, 1024, 1024], P(None, 'tile'), as said below
- step_gain: bfloat16 [64, 1024, 1024], P('tm', 'tile'), may hold values from -0.1875 to 0.1875
- step_offset: float32 [64, 1024], P('tm', 'tile'), may hold values from -6 to 6
- step_var: float32 [64, 1024], P('tm', 'tile'), may hold values from 0.1 to 1.5
- obs_tiles: int32 [64, 4], P('tm'), may hold values from 0 to 7
- obs_count: int32 [64], P('tm'), may hold values from 1 to 4, as said below
- obs_value: float32 [64, 4, 128], P('tm'), may hold values from -10 to 10
- obs_noise: float32 [1024], replicated, may hold values from 0.2 to 2
Outputs:
- start_cov: bfloat16 [8, 1024, 1024], P('tm', 'tile')
- start_mean: bfloat16 [8, 1024], P('tm', 'tile')
- step_mean: float32 [64, 1024], P('tm', 'tile')
- step_spread: float32 [64, 1024], P('tm', 'tile')
- innovation: float32 [64, 4, 128], P('tm')
The draws below stay inside these ranges and needn't reach their ends.
Inputs may be any that keep to these rules, and one draw needn't show every extreme that they name: `end_cov`: each matrix is symmetric and positive definite. `seg_noise`: each matrix is symmetric and positive definite. `obs_count`: some step has 4 live slots and some has 1.
All inputs are finite; a program needn't handle non-finite values.
Results may differ from the reference program's by a relative error of at most 0.015.
Values may be sent and summed in bfloat16 or wider, within the bound.
No kernel may reach another device: no remote copies, remote signals or barrier semaphores. Data moves between devices by JAX's collectives and lax.ppermute only.
A program may use at most 64 MiB of HBM per device.

```python
import math
import jax
import jax.numpy as jnp
from jax import lax

D = 1024
STEPS_SEG = 8
TILE_STATES = 128
SLOTS = 4
GROUP_SEGS = 4
SEGS = 8
GROUPS = 2
STEPS = 64
NTILES = 8


def correlated_blocks(key, count, amp_low, amp_high, diag_low, diag_high, length, reach, mixing):
    first_key, second_key, third_key, fourth_key = jax.random.split(key, 4)
    amplitude = jax.random.uniform(first_key, (count, D), jnp.float32, amp_low, amp_high)
    places = jnp.arange(D, dtype=jnp.float32)
    distance = jnp.abs(places[:, None] - places[None, :])
    kernel = jnp.exp(-distance / length)
    smooth = amplitude[:, :, None] * amplitude[:, None, :] * kernel[None, :, :]
    raw = jax.random.uniform(second_key, (count, D, D), jnp.float32, -1.0, 1.0) * (reach / D)
    paired = raw + jnp.swapaxes(raw, 1, 2)
    diagonal = jax.random.uniform(third_key, (count, D), jnp.float32, diag_low, diag_high)
    identity = jnp.eye(D, dtype=jnp.float32)
    result = smooth + paired * (1.0 - identity)[None, :, :] + identity[None, :, :] * diagonal[:, :, None]
    if mixing > 0.0:
        inner_width = D // 4
        factor = jax.random.normal(fourth_key, (count, D, inner_width), jnp.float32)
        wishart = jnp.einsum('gik,gjk->gij', factor, factor, precision=lax.Precision.HIGHEST)
        result = result + wishart * (mixing / inner_width)
    return result


def draw_end_cov(key, part):
    result = correlated_blocks(jax.random.fold_in(key, 11), GROUPS, 0.7, 1.5, 1.2, 2.0, D / 16.0, 0.5, 1.0)
    return result.astype(jnp.bfloat16)


def draw_seg_noise(key, part):
    result = correlated_blocks(jax.random.fold_in(key, 13), SEGS, 0.5, 1.2, 0.6, 1.4, D / 32.0, 0.2, 0.0)
    return result.astype(jnp.bfloat16)


def draw_obs_count(key, part):
    counts = jax.random.randint(jax.random.fold_in(key, 17), (STEPS,), 1, SLOTS + 1)
    counts = counts.at[0].set(SLOTS)
    counts = counts.at[1].set(1)
    return counts.astype(jnp.int32)


def touch_ends(drawn, rng, least, top_value):
    longest = drawn.shape.index(max(drawn.shape))
    spots = []
    for shift in (0, 1):
        where = [jax.random.randint(jax.random.fold_in(rng, axis), (), 0, length) for axis, length in enumerate(drawn.shape)]
        where[longest] = (where[longest] + shift) % drawn.shape[longest]
        spots.append(tuple(where))
    return drawn.at[spots[0]].set(least).at[spots[1]].set(top_value)


def block_scale(rng, shape, cuts, least, largest):
    def one(axis_at, shards_of):
        steps = jax.random.uniform(jax.random.fold_in(jax.random.fold_in(rng, 6), axis_at), (shards_of,), jnp.float32, least / len(cuts), largest / len(cuts))
        return jnp.repeat(jnp.exp(steps), shape[axis_at] // shards_of).reshape((-1,) + (1,) * (len(shape) - axis_at - 1))

    factor_of = one(*cuts[0])
    for cut in cuts[1:]:
        factor_of = factor_of * one(*cut)
    return factor_of


def bell_draw(key, dims, scale, limit, shards=(), kind=jnp.bfloat16):
    values = scale * jax.random.normal(key, dims, jnp.float32)
    if shards:
        values = values * block_scale(key, dims, shards, -0.22, 0.18)
    return jnp.clip(values, -limit, limit).astype(kind)


def setup_inputs(seed: int = 0) -> dict:
    key_of = jax.random.split(jax.random.key(seed), 13)
    return {
        "seg_gain": bell_draw(key_of[0], (SEGS, D, D), D ** -0.5, 0.1875, ((0, 8), (1, 4))),
        "seg_offset": bell_draw(key_of[1], (SEGS, D), 1.0, 6.0, ((0, 8), (1, 4)), jnp.float32),
        "seg_noise": draw_seg_noise(jax.random.fold_in(key_of[12], 71), 0),
        "end_mean": bell_draw(key_of[3], (GROUPS, D), 1.0, 6.0, ((1, 4),)),
        "end_cov": draw_end_cov(jax.random.fold_in(key_of[12], 71), 0),
        "step_gain": bell_draw(key_of[5], (STEPS, D, D), D ** -0.5, 0.1875, ((0, 8), (1, 4))),
        "step_offset": bell_draw(key_of[6], (STEPS, D), 1.0, 6.0, ((0, 8), (1, 4)), jnp.float32),
        "step_var": jnp.clip(jnp.exp(math.log(1.5) - 2.7080502 * jax.random.uniform(key_of[7], (STEPS, D), jnp.float32) ** block_scale(key_of[7], (STEPS, D), ((0, 8), (1, 4)), -0.2, 0.2)), 0.1, 1.5),
        "obs_tiles": touch_ends(jax.random.randint(key_of[8], (STEPS, SLOTS), 0, NTILES), jax.random.fold_in(key_of[8], 1), 0, NTILES - 1).astype(jnp.int32),
        "obs_count": draw_obs_count(jax.random.fold_in(key_of[12], 71), 0),
        "obs_value": bell_draw(key_of[10], (STEPS, SLOTS, TILE_STATES), 2.0, 10.0, ((0, 8),), jnp.float32),
        "obs_noise": jnp.clip(jnp.exp(jax.random.uniform(key_of[11], (D,), jnp.float32, math.log(0.2), math.log(2.0))), 0.2, 2.0),
    }


def apply_element(gain_mat, offset_vec, noise_mat, mean_vec, cov_mat):
    product = jnp.dot(gain_mat, cov_mat, preferred_element_type=jnp.float32).astype(jnp.bfloat16)
    new_cov = (jnp.dot(product, gain_mat.T, preferred_element_type=jnp.float32) + noise_mat.astype(jnp.float32)).astype(jnp.bfloat16)
    new_mean = (jnp.dot(gain_mat, mean_vec, preferred_element_type=jnp.float32) + offset_vec).astype(jnp.bfloat16)
    return new_mean, new_cov


def segment_moments(inputs):
    gains, offsets, variances, mean_vec, cov_mat = inputs
    gains_wide = gains.astype(jnp.float32)
    partial_value = jnp.einsum("kij,jl->kil", gains_wide, cov_mat.astype(jnp.float32), precision=lax.Precision.HIGHEST)
    spread = jnp.sum(partial_value * gains_wide, axis=2) + variances
    means = jnp.einsum("kij,j->ki", gains_wide, mean_vec.astype(jnp.float32), precision=lax.Precision.HIGHEST) + offsets
    return means, spread


def reference(seg_gain, seg_offset, seg_noise, end_mean, end_cov, step_gain, step_offset, step_var, obs_tiles, obs_count, obs_value, obs_noise):
    ends_mean = [None] * SEGS
    ends_cov = [None] * SEGS
    starts_mean = [None] * SEGS
    starts_cov = [None] * SEGS
    for group_index in range(GROUPS):
        mean_vec = end_mean[group_index]
        cov_mat = end_cov[group_index]
        for place_index in reversed(range(GROUP_SEGS)):
            segment = group_index * GROUP_SEGS + place_index
            ends_mean[segment] = mean_vec
            ends_cov[segment] = cov_mat
            mean_vec, cov_mat = apply_element(seg_gain[segment], seg_offset[segment], seg_noise[segment], mean_vec, cov_mat)
            starts_mean[segment] = mean_vec
            starts_cov[segment] = cov_mat
    start_cov = jnp.stack(starts_cov)
    start_mean = jnp.stack(starts_mean)
    inputs = (step_gain.reshape(SEGS, STEPS_SEG, D, D), step_offset.reshape(SEGS, STEPS_SEG, D), step_var.reshape(SEGS, STEPS_SEG, D), jnp.stack(ends_mean), jnp.stack(ends_cov))
    means, spread = lax.map(segment_moments, inputs)
    step_mean = means.reshape(STEPS, D)
    step_spread = spread.reshape(STEPS, D)
    tile_mean = step_mean.reshape(STEPS, NTILES, TILE_STATES)
    tile_spread = step_spread.reshape(STEPS, NTILES, TILE_STATES) + obs_noise.reshape(1, NTILES, TILE_STATES)
    onehot = (obs_tiles[:, :, None] == jnp.arange(NTILES, dtype=jnp.int32)[None, None, :]).astype(jnp.float32)
    picked_mean = jnp.einsum("ksn,kno->kso", onehot, tile_mean, precision=lax.Precision.HIGHEST)
    picked_spread = jnp.einsum("ksn,kno->kso", onehot, tile_spread, precision=lax.Precision.HIGHEST)
    live = jnp.arange(SLOTS, dtype=jnp.int32)[None, :] < obs_count[:, None]
    innovation = jnp.where(live[:, :, None], (obs_value - picked_mean) / picked_spread, jnp.float32(0.0))
    return start_cov, start_mean, step_mean, step_spread, innovation
```

```python
import functools
import jax
import jax.numpy as jnp
from jax import lax
from jax.experimental import pallas as pl
from jax.experimental.pallas import tpu as pltpu
from jax.sharding import PartitionSpec as P

TILE_STATES = 128
SLOTS = 4
GROUP_SEGS = 4


def shifted(block, axis, distance):
    devices = range(lax.axis_size(axis))
    route = [(i - distance, i) for i in devices if i - distance in devices]
    return lax.ppermute(block, axis, route)


def general_shards(
    seg_gain,
    seg_offset,
    seg_noise,
    end_mean,
    end_cov,
    step_gain,
    step_offset,
    step_var,
    obs_tiles,
    obs_count,
    obs_value,
    obs_noise,
):
    position = lax.axis_index("tm")
    slot_place = position % GROUP_SEGS
    group_index = position // GROUP_SEGS
    gain_rows = seg_gain[0]
    offset_rows = seg_offset[0]
    noise_rows = seg_noise[0].astype(jnp.float32)
    row_count = gain_rows.shape[0]
    state_count = gain_rows.shape[1]
    cur_mean = lax.dynamic_index_in_dim(end_mean, group_index, 0, keepdims=False)
    cur_cov = lax.dynamic_index_in_dim(end_cov, group_index, 0, keepdims=False)
    kept_mean = jnp.zeros((state_count,), jnp.bfloat16)
    kept_cov = jnp.zeros((state_count, state_count), jnp.bfloat16)
    out_mean = jnp.zeros((row_count,), jnp.bfloat16)
    out_cov = jnp.zeros((row_count, state_count), jnp.bfloat16)
    for depth_step in range(GROUP_SEGS):
        whole_mean, whole_cov = (
            lax.all_gather(cur_mean, "tile", axis=0, tiled=True),
            lax.all_gather(cur_cov, "tile", axis=0, tiled=True),
        )
        is_mine = slot_place == GROUP_SEGS - 1 - depth_step
        kept_mean = jnp.where(is_mine, whole_mean, kept_mean)
        kept_cov = jnp.where(is_mine, whole_cov, kept_cov)
        product = jnp.dot(gain_rows, whole_cov, preferred_element_type=jnp.float32).astype(
            jnp.bfloat16
        )
        col_block = jnp.einsum(
            "pd,rd->pr",
            lax.all_gather(product, "tile", axis=0, tiled=True),
            gain_rows,
            preferred_element_type=jnp.float32,
        )
        spread_rows = lax.all_to_all(col_block, "tile", split_axis=0, concat_axis=1, tiled=True)
        new_cov = (spread_rows + noise_rows).astype(jnp.bfloat16)
        new_mean = (
            jnp.dot(gain_rows, whole_mean, preferred_element_type=jnp.float32) + offset_rows
        ).astype(jnp.bfloat16)
        out_mean = jnp.where(is_mine, new_mean, out_mean)
        out_cov = jnp.where(is_mine, new_cov, out_cov)
        if depth_step < GROUP_SEGS - 1:
            got_mean, got_cov = shifted((new_mean, new_cov), "tm", -1)
            takes_next = slot_place == GROUP_SEGS - 2 - depth_step
            cur_mean = jnp.where(takes_next, got_mean, cur_mean)
            cur_cov = jnp.where(takes_next, got_cov, cur_cov)
    partial_value = jnp.einsum(
        "krd,de->kre", step_gain, kept_cov, preferred_element_type=jnp.float32
    )
    local_spread = jnp.sum(partial_value * step_gain, axis=2) + step_var
    local_mean = (
        jnp.einsum("krd,d->kr", step_gain, kept_mean, preferred_element_type=jnp.float32)
        + step_offset
    )
    full_mean, full_spread = (
        lax.all_gather(local_mean, "tile", axis=1, tiled=True),
        lax.all_gather(local_spread, "tile", axis=1, tiled=True),
    )
    step_count = full_mean.shape[0]
    tile_total = state_count // TILE_STATES
    tile_mean = full_mean.reshape(step_count, tile_total, TILE_STATES)
    tile_spread = full_spread.reshape(step_count, tile_total, TILE_STATES) + obs_noise.reshape(
        1, tile_total, TILE_STATES
    )
    onehot = (
        obs_tiles[:, :, None] == jnp.arange(tile_total, dtype=jnp.int32)[None, None, :]
    ).astype(jnp.float32)
    picked_mean = jnp.einsum("ksn,kno->kso", onehot, tile_mean, precision=lax.Precision.HIGHEST)
    picked_spread = jnp.einsum("ksn,kno->kso", onehot, tile_spread, precision=lax.Precision.HIGHEST)
    live_slots = jnp.arange(SLOTS, dtype=jnp.int32)[None, :] < obs_count[:, None]
    innovation = jnp.where(
        live_slots[:, :, None], (obs_value - picked_mean) / picked_spread, jnp.float32(0.0)
    )
    return (out_cov[None], out_mean[None], local_mean, local_spread, innovation)


BLOCK = 256
RING = 4
TAIL = 16
VMEM = 12 * 1024 * 1024
ALL_VMEM = 56 * 1024 * 1024
NT = (((1,), (1,)), ((), ()))
F32 = jnp.float32
BF16 = jnp.bfloat16


def cols(index):
    return pl.ds(pl.multiple_of(index * BLOCK, BLOCK), BLOCK)


def spot(z, shift):
    return lax.rem(z + shift, RING)


def dot(a, b):
    return jnp.dot(a, b, preferred_element_type=F32)


def dot_nt(a, b):
    return lax.dot_general(a, b, NT, preferred_element_type=F32)


def owns_far(row):
    return (row == 0) | (row == RING - 1)


def lay_out(z, parcels, full, mean):
    for a in range(RING):
        at = spot(z, a)
        row, near, far = cols(at), cols(spot(z, a + 1)), cols(spot(z, a + 2))
        full[row, row] = parcels[a][:BLOCK, :BLOCK]
        beside = parcels[a][:BLOCK, BLOCK : 2 * BLOCK]
        full[row, near] = beside
        full[near, row] = beside.T
        mean[:, row] = parcels[a][BLOCK:, :BLOCK]

        @pl.when(owns_far(at))
        def _(a=a, row=row, far=far):
            block = parcels[a][:BLOCK, 2 * BLOCK :]
            full[row, far] = block
            full[far, row] = block.T


def keep_parcels(z, parcels, half, half_mean):
    for a in range(RING):
        at = spot(z, a)
        half_mean[:, cols(at)] = parcels[a][BLOCK:, :BLOCK]
        half[at, 2 * BLOCK :, :] = parcels[a][:BLOCK, :BLOCK]
        half[spot(z, a + 1), BLOCK : 2 * BLOCK, :] = parcels[a][:BLOCK, BLOCK : 2 * BLOCK] * 2

        @pl.when(owns_far(at))
        def _(a=a):
            half[spot(z, a + 2), :BLOCK, :] = parcels[a][:BLOCK, 2 * BLOCK :] * 2


def pack_kernel(where, end_cov, noise, end_mean, offset, parcel, sems):
    z, seg, group = where[0], where[1], where[2]

    def fetch(source, tail):
        copies = []
        for j in range(3):
            target = parcel.at[pl.ds(0, BLOCK), pl.ds(j * BLOCK, BLOCK)]
            copies.append(pltpu.make_async_copy(source.at[:, cols(spot(z, j))], target, sems.at[j]))
        for copy in copies:
            copy.start()
        parcel[BLOCK:, :] = jnp.zeros((TAIL, 3 * BLOCK), BF16)
        parcel[BLOCK:, :BLOCK] = tail.astype(BF16)
        for copy in copies:
            copy.wait()

    @pl.when(seg == 1)
    def _():
        high = offset[...].astype(BF16).astype(F32)
        first = lax.broadcasted_iota(jnp.int32, (TAIL, BLOCK), 0) == 0
        fetch(noise, jnp.where(first, high, offset[...] - high))

    @pl.when(seg != 1)
    def _():
        mean = jnp.zeros((1, BLOCK), F32)
        for g in range(end_mean.shape[0]):
            mean = jnp.where(group == g, end_mean[g : g + 1, :].astype(F32), mean)
        fetch(end_cov.at[group], jnp.broadcast_to(mean, (TAIL, BLOCK)))


def pairs_kernel(at_seg, where, g0, g1, g2, p0, p1, p2, p3, noise, offset, *refs):
    if at_seg == GROUP_SEGS - 1:
        half, half_mean, parcel, mean_row, full, mean = refs
    else:
        early, _, _, half, half_mean, parcel, mean_row, full, mean = refs
    z, seg = where[0], where[1]
    parcels = (p0, p1, p2, p3)

    @pl.when(seg == at_seg)
    def _():
        lay_out(z, parcels, full, mean)
        product = dot(g0[...], full[...]).astype(BF16)
        for j, gain in enumerate((g0, g1, g2)):
            block = dot_nt(product, gain[...]) + noise[:, cols(spot(z, j))].astype(F32)
            parcel[:BLOCK, j * BLOCK : (j + 1) * BLOCK] = block.astype(BF16)
        new_mean = (dot_nt(mean[...], g0[...]) + offset[...]).astype(BF16)
        parcel[BLOCK:, :BLOCK] = new_mean
        parcel[BLOCK:, BLOCK:] = jnp.zeros((TAIL, 2 * BLOCK), BF16)
        mean_row[...] = new_mean
        keep_parcels(z, parcels, half, half_mean)

    if at_seg < GROUP_SEGS - 1:

        @pl.when(seg == GROUP_SEGS - 1)
        def _():
            parcel[...] = early[...]


def hand_kernel(where, event, gain, out, sem):
    @pl.when(where[1] < 2)
    def _():
        copy = pltpu.make_async_copy(gain, out, sem)
        copy.start()
        copy.wait()


def stack_kernel(where, event, g0, g1, g2, g3, n0, n1, n2, n3, lift):
    z, seg = where[0], where[1]
    states = g0.shape[1]

    @pl.when(seg == 1)
    def _():
        for a, gain in enumerate((g0, g1, g2, g3)):
            lift[cols(spot(z, a)), :] = gain[...]
        lay_out(z, (n0, n1, n2, n3), lift.at[pl.ds(states, states)], lift.at[pl.ds(2 * states, TAIL)])


def turn_kernel(where, event, t0, t1, t2, t3, out):
    @pl.when(where[1] == 1)
    def _():
        for a, parcel in enumerate((t0, t1, t2, t3)):
            out[a] = parcel[...]


def ahead_kernel(where, lift, gain, step_gain, left, base, through, beside):
    seg = where[1]
    states = gain.shape[1]

    @pl.when(seg == 0)
    def _():
        through[...] = dot(gain[...], lift[:states, :]).astype(BF16)
        beside[...] = dot(gain[...], lift[states : 2 * states, :])

        def one(k, carry):
            rows = step_gain[k]
            left[k] = dot(rows, lift[:states, :]).astype(BF16)
            value = dot(rows, lift[states : 2 * states, :]) * rows.astype(F32)
            base[pl.ds(k, 1), :] = row_sums(value)
            return carry

        lax.fori_loop(0, step_gain.shape[0], one, 0)


def row_sums(value):
    total = value[:, :128]
    for at in range(128, value.shape[1], 128):
        total = total + value[:, at : at + 128]
    return jnp.sum(total.T, axis=0, keepdims=True)


def moments_kernel(where, ends_1, ends_0, lift, left, base, gain, offset, var, parcel, kept, kept_mean, half, half_mean, out_mean, out_spread, out, parcel_on):
    z, seg = where[0], where[1]
    states = gain.shape[2]

    @pl.when(seg == 1)
    def _():
        keep_parcels(z, [ends_1.at[a] for a in range(RING)], half, half_mean)

    @pl.when(seg == 0)
    def _():
        keep_parcels(z, [ends_0.at[a] for a in range(RING)], half, half_mean)
        tail = lift[2 * states :, :].astype(F32)
        half_mean[...] = (dot_nt(half_mean[...], lift[:states, :]) + tail[0:1] + tail[1:2]).astype(BF16)

    @pl.when(seg > 1)
    def _():
        parcel_on[...] = parcel[...]

    def steps(rows_of, more):
        def one(k, carry):
            total = jnp.zeros((BLOCK, BLOCK), F32)
            for b in range(RING):
                blocks = (b + 2, b + 3, b) if b in (1, 2) else (b + 3, b)
                parts = [rows_of[k, :, (r % RING) * BLOCK : (r % RING + 1) * BLOCK] for r in blocks]
                value = dot(jnp.concatenate(parts, axis=1), half[b, (3 - len(blocks)) * BLOCK :, :])
                total = total + value * parts[-1].astype(F32)
            spread = row_sums(total) + var[pl.ds(k, 1), :]
            if more is not None:
                spread = spread + more[pl.ds(k, 1), :]
            means = dot_nt(half_mean[...], gain[k])[0:1] + offset[pl.ds(k, 1), :]
            out[0, pl.ds(k, 1), :] = means
            out[1, pl.ds(k, 1), :] = spread
            out_mean[pl.ds(k, 1), :] = means
            out_spread[pl.ds(k, 1), :] = spread
            return carry

        lax.fori_loop(0, gain.shape[0], one, 0, unroll=2)

    @pl.when(seg == 0)
    def _():
        steps(left, base)

    @pl.when(seg != 0)
    def _():
        steps(gain, None)


def last_kernel(where, g0, g1, g2, g3, ends_1, ends_0, lift, through, beside, noise, offset, means, rows, mean_row, full, mean):
    z, seg = where[0], where[1]
    states = g0.shape[1]

    def finish(product):
        for a, gain in enumerate((g0, g1, g2, g3)):
            column = cols(spot(z, a))
            rows[:, column] = (dot_nt(product, gain[...]) + noise[:, column].astype(F32)).astype(BF16)
        mean_row[...] = (dot_nt(means[...], g0[...]) + offset[...]).astype(BF16)

    @pl.when(seg == 0)
    def _():
        lay_out(z, [ends_0.at[a] for a in range(RING)], full, mean)
        product = dot(through[...], full[...]).astype(BF16)
        finish((dot_nt(product, lift[:states, :]) + beside[...]).astype(BF16))

    @pl.when(seg == 1)
    def _():
        lay_out(z, [ends_1.at[a] for a in range(RING)], full, mean)
        finish(dot(g0[...], full[...]).astype(BF16))


def innovation_kernel(where, tiles, counts, s0, s1, s2, s3, value, noise, own, far, near, mean_1, mean_2, mean_3, _, out, mean_row, rows_out, full, rows, sem):
    z, seg = where[0], where[1]
    copy = pltpu.make_async_copy(rows, rows_out, sem)

    @pl.when(seg > 1)
    def _():
        rows[:, cols(z)] = own[:BLOCK, :BLOCK]
        rows[:, cols(spot(z, 1))] = own[:BLOCK, BLOCK : 2 * BLOCK]
        rows[:, cols(spot(z, 3))] = near[:BLOCK, BLOCK : 2 * BLOCK].T

        @pl.when(owns_far(z))
        def _():
            rows[:, cols(spot(z, 2))] = own[:BLOCK, 2 * BLOCK :]

        @pl.when(jnp.logical_not(owns_far(z)))
        def _():
            rows[:, cols(spot(z, 2))] = far[:BLOCK, 2 * BLOCK :].T

        copy.start()

    mean = mean_1[0:1].astype(F32)
    for at, source in ((2, mean_2), (3, mean_3)):
        mean = jnp.where(seg == at, source[0:1].astype(F32), mean)
    mean_row[...] = mean.astype(BF16)
    for a, part in enumerate((s0, s1, s2, s3)):
        full[:, :, cols(spot(z, a))] = part[...]
    full[1] = full[1] + noise[...]
    for k in range(value.shape[0]):
        for j in range(SLOTS):
            at = pl.ds(pl.multiple_of(tiles[j, k] * TILE_STATES, TILE_STATES), TILE_STATES)
            result = (value[k, j : j + 1, :] - full[0, k : k + 1, at]) / full[1, k : k + 1, at]
            out[k, j : j + 1, :] = jnp.where(j < counts[k], result, 0.0)

    @pl.when(seg > 1)
    def _():
        copy.wait()


def smem():
    return pl.BlockSpec(memory_space=pltpu.SMEM)


def vmem():
    return pl.BlockSpec(memory_space=pltpu.VMEM)


def params():
    return pltpu.CompilerParams(vmem_limit_bytes=VMEM)


def cost(flops, moved):
    return pl.CostEstimate(flops=int(flops), bytes_accessed=int(moved), transcendentals=0)


def shape(dims, kind=BF16):
    return jax.ShapeDtypeStruct(dims, kind)


def ring_shards(groups, seg_gain, seg_offset, seg_noise, end_mean, end_cov, step_gain, step_offset, step_var, obs_tiles, obs_count, obs_value, obs_noise):
    position = lax.axis_index("tm")
    z = lax.axis_index("tile")
    where = jnp.stack([z, position % GROUP_SEGS, position // GROUP_SEGS]).astype(jnp.int32)
    gain, noise = seg_gain[0], seg_noise[0]
    states = gain.shape[1]
    steps = step_gain.shape[0]
    parcel_shape = shape((BLOCK + TAIL, 3 * BLOCK))

    def route(block, moves):
        table = []
        for g in range(groups):
            for (source, start), (target, end) in moves:
                table.append(((g * GROUP_SEGS + source) * RING + start, (g * GROUP_SEGS + target) * RING + end))
        return lax.ppermute(block, ("tm", "tile"), table)

    def send(block, pairs, shift):
        return route(block, [((a, (to + shift) % RING), (b, to)) for a, b in pairs for to in range(RING)])

    def exchange(block, pairs, own=None):
        others = [send(block, pairs, a) for a in (2, 1, 3)]
        return [send(block, pairs, 0) if own is None else own, others[1], others[0], others[2]]

    def within(segments, steps):
        return [((a, start), (a, to)) for a in segments for start, to in steps]

    def call(kernel, name, out_shape, operands, scratch, flops, aliases={}):
        moved = sum(x.size * x.dtype.itemsize for x in list(operands) + list(out_shape))
        return pl.pallas_call(
            kernel,
            out_shape=out_shape,
            in_specs=[smem()] + [vmem()] * len(operands),
            out_specs=(vmem(),) * len(out_shape),
            scratch_shapes=scratch,
            input_output_aliases=aliases,
            compiler_params=params(),
            cost_estimate=cost(flops, moved),
            name=name,
        )(where, *operands)

    def pack(kernel, name, out_shape, far_operands, near_operands, sems, limit):
        return pl.pallas_call(
            kernel,
            out_shape=out_shape,
            in_specs=[smem()] + [pl.BlockSpec(memory_space=pl.ANY)] * len(far_operands) + [vmem()] * len(near_operands),
            out_specs=vmem(),
            scratch_shapes=[sems],
            compiler_params=pltpu.CompilerParams(vmem_limit_bytes=limit),
            cost_estimate=cost(0, 1e6),
            name=name,
        )(where, *far_operands, *near_operands)

    full_and_mean = [pltpu.VMEM((states, states), BF16), pltpu.VMEM((TAIL, states), BF16)]
    row_shape, mean_shape = shape((BLOCK, states)), shape((TAIL, BLOCK))
    half_shapes = (shape((RING, 3 * BLOCK, BLOCK)), shape((TAIL, states)))

    back, on = ((1, 0), (2, 1), (3, 2), (0, 3)), ((0, 1), (1, 2), (2, 3), (3, 0))
    gain_1 = route(gain, within((3, 2, 1, 0), back))
    gain_2 = route(gain, within((3, 2), ((2, 0), (1, 3))) + within((1, 0), on))
    parcel = pack(pack_kernel, "pack", parcel_shape, (end_cov, noise), (end_mean, seg_offset), pltpu.SemaphoreType.DMA((3,)), ALL_VMEM)
    first = exchange(parcel, ((3, 3), (1, 1)), parcel)
    held = pack(hand_kernel, "hand", row_shape, (first[2], gain), (), pltpu.SemaphoreType.DMA, VMEM)
    gains = [gain, gain_1, route(held, within((1, 0), ((0, 2), (1, 3), (2, 0), (3, 1)))), gain_2]

    flops = 4 * BLOCK * states * states
    *kept, parcel_3, mean_3 = call(
        functools.partial(pairs_kernel, 3),
        "pairs_3",
        (*half_shapes, parcel_shape, mean_shape),
        (gain, gain_1, gain_2, *first, noise, seg_offset),
        full_and_mean,
        flops,
    )
    second = exchange(parcel_3, ((3, 2),))
    *kept, parcel_2, mean_2 = call(
        functools.partial(pairs_kernel, 2),
        "pairs_2",
        (*half_shapes, parcel_shape, mean_shape),
        (gain, gain_1, gain_2, *second, noise, seg_offset, parcel_3, *kept),
        full_and_mean,
        flops,
        {11: 0, 12: 1},
    )
    third = exchange(parcel_2, ((2, 1),))
    (lift,) = call(stack_kernel, "stack", (shape((2 * states + TAIL, states)),), (parcel_2, *gains, *first), [], 0)
    lift = send(lift, ((1, 0),), 0)
    left, base, through, beside = call(
        ahead_kernel,
        "ahead",
        (shape(step_gain.shape), shape((steps, BLOCK), F32), row_shape, shape((BLOCK, states), F32)),
        (lift, gain, step_gain),
        [],
        4 * (steps + 1) * BLOCK * states * states,
    )
    (ends_1,) = call(turn_kernel, "turn", (shape((RING, *parcel_shape.shape)),), (base, *third), [], 0)
    ends_0 = send(ends_1, ((1, 0),), 0)
    out_steps = shape((steps, BLOCK), F32)
    _, means, step_mean, step_spread, stats, parcel_on = call(
        moments_kernel,
        "moments",
        (*half_shapes, out_steps, out_steps, shape((2, steps, BLOCK), F32), parcel_shape),
        (ends_1, ends_0, lift, left, base, step_gain, step_offset, step_var, parcel_2, *kept),
        [],
        2 * steps * BLOCK * states * states,
        {10: 0, 11: 1},
    )
    everyone = tuple((s, s) for s in range(GROUP_SEGS))
    all_stats = [stats] + [send(stats, everyone, a) for a in range(1, RING)]
    near, far = send(parcel_on, ((3, 3), (2, 2)), 3), route(parcel_on, within((3, 2), ((0, 2), (3, 1))))
    rows, mean_1 = call(
        last_kernel,
        "last",
        (row_shape, mean_shape),
        (*gains, ends_1, ends_0, lift, through, beside, noise, seg_offset, means),
        full_and_mean,
        flops,
    )
    innovation, out_mean, out_cov = pl.pallas_call(
        innovation_kernel,
        out_shape=(shape(obs_value.shape, F32), shape((1, BLOCK)), row_shape),
        in_specs=[smem()] * 3 + [vmem()] * 12 + [pl.BlockSpec(memory_space=pl.ANY)],
        out_specs=(vmem(), vmem(), pl.BlockSpec(memory_space=pl.ANY)),
        scratch_shapes=[pltpu.VMEM((2, steps, states), F32), pltpu.VMEM(row_shape.shape, BF16), pltpu.SemaphoreType.DMA],
        input_output_aliases={15: 2},
        compiler_params=params(),
        cost_estimate=cost(0, 2e5),
        name="innovation",
    )(where, obs_tiles.T, obs_count, *all_stats, obs_value, obs_noise.reshape(1, states), parcel_2, far, near, mean_1, mean_2, mean_3, rows)
    return out_cov[None], out_mean, step_mean, step_spread, innovation


def solution(mesh):
    in_specs = (
        P("tm", "tile", None),
        P("tm", "tile"),
        P("tm", "tile", None),
        P(None, "tile"),
        P(None, "tile", None),
        P("tm", "tile", None),
        P("tm", "tile"),
        P("tm", "tile"),
        P("tm", None),
        P("tm"),
        P("tm", None, None),
        P(),
    )
    out_specs = (
        P("tm", "tile", None),
        P("tm", "tile"),
        P("tm", "tile"),
        P("tm", "tile"),
        P("tm", None, None),
    )
    if mesh.shape["tile"] == RING:
        shards = functools.partial(ring_shards, mesh.shape["tm"] // GROUP_SEGS)
    else:
        shards = general_shards
    return jax.shard_map(shards, mesh=mesh, in_specs=in_specs, out_specs=out_specs, check_vma=False)
```

```python
import functools
import jax
import jax.numpy as jnp
from jax import lax
from jax.experimental import pallas as pl
from jax.experimental.pallas import tpu as pltpu
from jax.sharding import PartitionSpec as P

TILE_STATES = 128
SLOTS = 4
GROUP_SEGS = 4


def shifted(block, axis, distance):
    devices = range(lax.axis_size(axis))
    route = [(i - distance, i) for i in devices if i - distance in devices]
    return lax.ppermute(block, axis, route)


def general_shards(
    seg_gain,
    seg_offset,
    seg_noise,
    end_mean,
    end_cov,
    step_gain,
    step_offset,
    step_var,
    obs_tiles,
    obs_count,
    obs_value,
    obs_noise,
):
    position = lax.axis_index("tm")
    slot_place = position % GROUP_SEGS
    group_index = position // GROUP_SEGS
    gain_rows = seg_gain[0]
    offset_rows = seg_offset[0]
    noise_rows = seg_noise[0].astype(jnp.float32)
    row_count = gain_rows.shape[0]
    state_count = gain_rows.shape[1]
    cur_mean = lax.dynamic_index_in_dim(end_mean, group_index, 0, keepdims=False)
    cur_cov = lax.dynamic_index_in_dim(end_cov, group_index, 0, keepdims=False)
    kept_mean = jnp.zeros((state_count,), jnp.bfloat16)
    kept_cov = jnp.zeros((state_count, state_count), jnp.bfloat16)
    out_mean = jnp.zeros((row_count,), jnp.bfloat16)
    out_cov = jnp.zeros((row_count, state_count), jnp.bfloat16)
    for depth_step in range(GROUP_SEGS):
        whole_mean, whole_cov = (
            lax.all_gather(cur_mean, "tile", axis=0, tiled=True),
            lax.all_gather(cur_cov, "tile", axis=0, tiled=True),
        )
        is_mine = slot_place == GROUP_SEGS - 1 - depth_step
        kept_mean = jnp.where(is_mine, whole_mean, kept_mean)
        kept_cov = jnp.where(is_mine, whole_cov, kept_cov)
        product = jnp.dot(gain_rows, whole_cov, preferred_element_type=jnp.float32).astype(
            jnp.bfloat16
        )
        col_block = jnp.einsum(
            "pd,rd->pr",
            lax.all_gather(product, "tile", axis=0, tiled=True),
            gain_rows,
            preferred_element_type=jnp.float32,
        )
        spread_rows = lax.all_to_all(col_block, "tile", split_axis=0, concat_axis=1, tiled=True)
        new_cov = (spread_rows + noise_rows).astype(jnp.bfloat16)
        new_mean = (
            jnp.dot(gain_rows, whole_mean, preferred_element_type=jnp.float32) + offset_rows
        ).astype(jnp.bfloat16)
        out_mean = jnp.where(is_mine, new_mean, out_mean)
        out_cov = jnp.where(is_mine, new_cov, out_cov)
        if depth_step < GROUP_SEGS - 1:
            got_mean, got_cov = shifted((new_mean, new_cov), "tm", -1)
            takes_next = slot_place == GROUP_SEGS - 2 - depth_step
            cur_mean = jnp.where(takes_next, got_mean, cur_mean)
            cur_cov = jnp.where(takes_next, got_cov, cur_cov)
    partial_value = jnp.einsum(
        "krd,de->kre", step_gain, kept_cov, preferred_element_type=jnp.float32
    )
    local_spread = jnp.sum(partial_value * step_gain, axis=2) + step_var
    local_mean = (
        jnp.einsum("krd,d->kr", step_gain, kept_mean, preferred_element_type=jnp.float32)
        + step_offset
    )
    full_mean, full_spread = (
        lax.all_gather(local_mean, "tile", axis=1, tiled=True),
        lax.all_gather(local_spread, "tile", axis=1, tiled=True),
    )
    step_count = full_mean.shape[0]
    tile_total = state_count // TILE_STATES
    tile_mean = full_mean.reshape(step_count, tile_total, TILE_STATES)
    tile_spread = full_spread.reshape(step_count, tile_total, TILE_STATES) + obs_noise.reshape(
        1, tile_total, TILE_STATES
    )
    onehot = (
        obs_tiles[:, :, None] == jnp.arange(tile_total, dtype=jnp.int32)[None, None, :]
    ).astype(jnp.float32)
    picked_mean = jnp.einsum("ksn,kno->kso", onehot, tile_mean, precision=lax.Precision.HIGHEST)
    picked_spread = jnp.einsum("ksn,kno->kso", onehot, tile_spread, precision=lax.Precision.HIGHEST)
    live_slots = jnp.arange(SLOTS, dtype=jnp.int32)[None, :] < obs_count[:, None]
    innovation = jnp.where(
        live_slots[:, :, None], (obs_value - picked_mean) / picked_spread, jnp.float32(0.0)
    )
    return (out_cov[None], out_mean[None], local_mean, local_spread, innovation)


BLOCK = 256
RING = 4
TAIL = 16
VMEM = 12 * 1024 * 1024
ALL_VMEM = 56 * 1024 * 1024
NT = (((1,), (1,)), ((), ()))
F32 = jnp.float32
BF16 = jnp.bfloat16


def cols(index):
    return pl.ds(pl.multiple_of(index * BLOCK, BLOCK), BLOCK)


def spot(z, shift):
    return lax.rem(z + shift, RING)


def dot(a, b):
    return jnp.dot(a, b, preferred_element_type=F32)


def dot_nt(a, b):
    return lax.dot_general(a, b, NT, preferred_element_type=F32)


def owns_far(row):
    return (row == 0) | (row == RING - 1)


def each_parcel(parcels, body):
    for a, entry in enumerate(parcels):
        if isinstance(entry, tuple):
            condition, one, other = entry
            pl.when(condition)(functools.partial(body, a, one))
            pl.when(jnp.logical_not(condition))(functools.partial(body, a, other))
        else:
            body(a, entry)


def by_relay(z, own, after, across, before, handed):
    return own, (z < RING - 1, after, handed), across, (z > 0, before, handed)


def lay_out(z, parcels, full, mean):
    def body(a, parcel):
        at = spot(z, a)
        row, near, far = cols(at), cols(spot(z, a + 1)), cols(spot(z, a + 2))
        full[row, row] = parcel[:BLOCK, :BLOCK]
        beside = parcel[:BLOCK, BLOCK : 2 * BLOCK]
        full[row, near] = beside
        full[near, row] = beside.T
        mean[:, row] = parcel[BLOCK:, :BLOCK]

        @pl.when(owns_far(at))
        def _():
            block = parcel[:BLOCK, 2 * BLOCK :]
            full[row, far] = block
            full[far, row] = block.T

    each_parcel(parcels, body)


def keep_parcels(z, parcels, half, half_mean):
    def body(a, parcel):
        at = spot(z, a)
        half_mean[:, cols(at)] = parcel[BLOCK:, :BLOCK]
        half[at, 2 * BLOCK :, :] = parcel[:BLOCK, :BLOCK]
        half[spot(z, a + 1), BLOCK : 2 * BLOCK, :] = parcel[:BLOCK, BLOCK : 2 * BLOCK] * 2

        @pl.when(owns_far(at))
        def _():
            half[spot(z, a + 2), :BLOCK, :] = parcel[:BLOCK, 2 * BLOCK :] * 2

    each_parcel(parcels, body)


def keep_whole(full, mean, half, half_mean):
    half_mean[...] = mean[...]
    for b in range(RING):
        column = slice(b * BLOCK, (b + 1) * BLOCK)
        for j in range(3):
            if j < 2 or b in (1, 2):
                row = (b - j) % RING * BLOCK
                block = full[row : row + BLOCK, column]
                half[b, (2 - j) * BLOCK : (3 - j) * BLOCK, :] = block * 2 if j else block


def fetch(source, z, tail, parcel, sems):
    copies = []
    for j in range(3):
        target = parcel.at[pl.ds(0, BLOCK), pl.ds(j * BLOCK, BLOCK)]
        copies.append(pltpu.make_async_copy(source.at[:, cols(spot(z, j))], target, sems.at[j]))
    for copy in copies:
        copy.start()
    parcel[BLOCK:, :] = jnp.zeros((TAIL, 3 * BLOCK), BF16)
    parcel[BLOCK:, :BLOCK] = tail.astype(BF16)
    for copy in copies:
        copy.wait()


def group_mean(group, end_mean):
    mean = jnp.zeros((1, BLOCK), F32)
    for g in range(end_mean.shape[0]):
        mean = jnp.where(group == g, end_mean[g : g + 1, :].astype(F32), mean)
    return jnp.broadcast_to(mean, (TAIL, BLOCK))


def pack_kernel(where, end_cov, noise, end_mean, offset, parcel, sems):
    z, seg, group = where[0], where[1], where[2]

    @pl.when(seg == 1)
    def _():
        high = offset[...].astype(BF16).astype(F32)
        first = lax.broadcasted_iota(jnp.int32, (TAIL, BLOCK), 0) == 0
        fetch(noise, z, jnp.where(first, high, offset[...] - high), parcel, sems)

    @pl.when(seg != 1)
    def _():
        fetch(end_cov.at[group], z, group_mean(group, end_mean), parcel, sems)


def pairs_kernel(at_seg, where, g0, g1, g2, noise, offset, *refs):
    z, seg, group = where[0], where[1], where[2]
    if at_seg == GROUP_SEGS - 1:
        end_cov, end_mean, *others, half, half_mean, parcel, mean_row, full, mean, own = refs
        parcels = (own, *others)
    else:
        *parcels, early, _, _, half, half_mean, parcel, mean_row, beside, far, full, mean = refs

    @pl.when(seg == at_seg)
    def _():
        if at_seg == GROUP_SEGS - 1:
            for j in range(3):
                own[:BLOCK, j * BLOCK : (j + 1) * BLOCK] = end_cov[group, :, cols(spot(z, j))]
            own[BLOCK:, :BLOCK] = group_mean(group, end_mean).astype(BF16)
        lay_out(z, parcels, full, mean)
        product = dot(g0[...], full[...]).astype(BF16)
        for j, gain in enumerate((g0, g1, g2)):
            block = dot_nt(product, gain[...]) + noise[:, cols(spot(z, j))].astype(F32)
            parcel[:BLOCK, j * BLOCK : (j + 1) * BLOCK] = block.astype(BF16)
        new_mean = (dot_nt(mean[...], g0[...]) + offset[...]).astype(BF16)
        parcel[BLOCK:, :BLOCK] = new_mean
        parcel[BLOCK:, BLOCK:] = jnp.zeros((TAIL, 2 * BLOCK), BF16)
        mean_row[...] = new_mean
        keep_whole(full, mean, half, half_mean)

    if at_seg < GROUP_SEGS - 1:
        @pl.when(seg == GROUP_SEGS - 1)
        def _():
            parcel[...] = early[...]

        beside[...] = parcel[:BLOCK, BLOCK : 2 * BLOCK]
        far[...] = parcel[:BLOCK, 2 * BLOCK :]


def hand_kernel(at_seg, where, event, gain, out, sem):
    @pl.when(where[1] == at_seg)
    def _():
        copy = pltpu.make_async_copy(gain, out, sem)
        copy.start()
        copy.wait()


def stack_kernel(where, event, g0, g1, g2, g3, n0, n1, n2, n3, lift):
    z, seg = where[0], where[1]
    states = g0.shape[1]

    @pl.when(seg == 1)
    def _():
        for a, gain in enumerate((g0, g1, g2, g3)):
            lift[cols(spot(z, a)), :] = gain[...]
        lay_out(z, (n0, n1, n2, n3), lift.at[pl.ds(states, states)], lift.at[pl.ds(2 * states, TAIL)])


def turn_kernel(where, near, far, t0, t1, t2, t3, t4, out):
    def body(a, parcel):
        out[a] = parcel[...]

    @pl.when(where[1] == 1)
    def _():
        each_parcel(by_relay(where[0], t0, t1, t2, t3, t4), body)


def ahead_kernel(where, event, lift, gain, step_gain, block_1, block_2, left, base, through, beside, block_1_on, block_2_on):
    seg = where[1]
    states = gain.shape[1]

    @pl.when(seg > 1)
    def _():
        block_1_on[...] = block_1[...]
        block_2_on[...] = block_2[...]

    @pl.when(seg == 0)
    def _():
        through[...] = dot(gain[...], lift[:states, :]).astype(BF16)
        beside[...] = dot(gain[...], lift[states : 2 * states, :])

        def one(k, carry):
            rows = step_gain[k]
            left[k] = dot(rows, lift[:states, :]).astype(BF16)
            value = dot(rows, lift[states : 2 * states, :]) * rows.astype(F32)
            base[pl.ds(k, 1), :] = row_sums(value)
            return carry

        lax.fori_loop(0, step_gain.shape[0], one, 0)


def row_sums(value):
    total = value[:, :128]
    for at in range(128, value.shape[1], 128):
        total = total + value[:, at : at + 128]
    return jnp.sum(total.T, axis=0, keepdims=True)


def moments_kernel(where, ends_1, ends_0, lift, left, base, gain, offset, var, kept, kept_mean, half, half_mean, out_mean, out_spread, out):
    z, seg = where[0], where[1]
    states = gain.shape[2]

    @pl.when(seg == 1)
    def _():
        keep_parcels(z, [ends_1.at[a] for a in range(RING)], half, half_mean)

    @pl.when(seg == 0)
    def _():
        keep_parcels(z, [ends_0.at[a] for a in range(RING)], half, half_mean)
        tail = lift[2 * states :, :].astype(F32)
        half_mean[...] = (dot_nt(half_mean[...], lift[:states, :]) + tail[0:1] + tail[1:2]).astype(BF16)

    def steps(rows_of, more):
        def one(k, carry):
            total = jnp.zeros((BLOCK, BLOCK), F32)
            for b in range(RING):
                blocks = (b + 2, b + 3, b) if b in (1, 2) else (b + 3, b)
                parts = [rows_of[k, :, (r % RING) * BLOCK : (r % RING + 1) * BLOCK] for r in blocks]
                value = dot(jnp.concatenate(parts, axis=1), half[b, (3 - len(blocks)) * BLOCK :, :])
                total = total + value * parts[-1].astype(F32)
            spread = row_sums(total) + var[pl.ds(k, 1), :]
            if more is not None:
                spread = spread + more[pl.ds(k, 1), :]
            means = dot_nt(half_mean[...], gain[k])[0:1] + offset[pl.ds(k, 1), :]
            out[0, pl.ds(k, 1), :] = means
            out[1, pl.ds(k, 1), :] = spread
            out_mean[pl.ds(k, 1), :] = means
            out_spread[pl.ds(k, 1), :] = spread
            return carry

        lax.fori_loop(0, gain.shape[0], one, 0, unroll=2)

    @pl.when(seg == 0)
    def _():
        steps(left, base)

    @pl.when(seg != 0)
    def _():
        steps(gain, None)


def last_kernel(where, g0, a1, a2, a3, b1, b2, b3, ends_1, ends_0, lift, through, beside, noise, offset, means, rows, mean_row, full, mean):
    z, seg = where[0], where[1]
    states = g0.shape[1]

    def finish(product, gains):
        for a, gain in enumerate(gains):
            column = cols(spot(z, a))
            rows[:, column] = (dot_nt(product, gain[...]) + noise[:, column].astype(F32)).astype(BF16)
        mean_row[...] = (dot_nt(means[...], g0[...]) + offset[...]).astype(BF16)

    @pl.when(seg == 0)
    def _():
        lay_out(z, [ends_0.at[a] for a in range(RING)], full, mean)
        product = dot(through[...], full[...]).astype(BF16)
        finish((dot_nt(product, lift[:states, :]) + beside[...]).astype(BF16), (g0, b1, b2, b3))

    @pl.when(seg == 1)
    def _():
        lay_out(z, [ends_1.at[a] for a in range(RING)], full, mean)
        finish(dot(g0[...], full[...]).astype(BF16), (g0, a1, a2, a3))


def innovation_kernel(where, tiles, counts, s0, s1, s2, s3, value, noise, own, far, near, mean_1, mean_2, mean_3, _, out, mean_row, rows_out, full, rows, sem):
    z, seg = where[0], where[1]
    copy = pltpu.make_async_copy(rows, rows_out, sem)

    @pl.when(seg > 1)
    def _():
        rows[:, cols(z)] = own[:BLOCK, :BLOCK]
        rows[:, cols(spot(z, 1))] = own[:BLOCK, BLOCK : 2 * BLOCK]
        rows[:, cols(spot(z, 3))] = near[...].T

        @pl.when(owns_far(z))
        def _():
            rows[:, cols(spot(z, 2))] = own[:BLOCK, 2 * BLOCK :]

        @pl.when(jnp.logical_not(owns_far(z)))
        def _():
            rows[:, cols(spot(z, 2))] = far[...].T

        copy.start()

    mean = mean_1[0:1].astype(F32)
    for at, source in ((2, mean_2), (3, mean_3)):
        mean = jnp.where(seg == at, source[0:1].astype(F32), mean)
    mean_row[...] = mean.astype(BF16)
    for a, part in enumerate((s0, s1, s2, s3)):
        full[:, :, cols(spot(z, a))] = part[...]
    full[1] = full[1] + noise[...]
    for k in range(value.shape[0]):
        for j in range(SLOTS):
            at = pl.ds(pl.multiple_of(tiles[j, k] * TILE_STATES, TILE_STATES), TILE_STATES)
            result = (value[k, j : j + 1, :] - full[0, k : k + 1, at]) / full[1, k : k + 1, at]
            out[k, j : j + 1, :] = jnp.where(j < counts[k], result, 0.0)

    @pl.when(seg > 1)
    def _():
        copy.wait()


def smem():
    return pl.BlockSpec(memory_space=pltpu.SMEM)


def vmem():
    return pl.BlockSpec(memory_space=pltpu.VMEM)


def params():
    return pltpu.CompilerParams(vmem_limit_bytes=VMEM)


def cost(flops, moved):
    return pl.CostEstimate(flops=int(flops), bytes_accessed=int(moved), transcendentals=0)


def shape(dims, kind=BF16):
    return jax.ShapeDtypeStruct(dims, kind)


def ring_shards(groups, seg_gain, seg_offset, seg_noise, end_mean, end_cov, step_gain, step_offset, step_var, obs_tiles, obs_count, obs_value, obs_noise):
    position = lax.axis_index("tm")
    z = lax.axis_index("tile")
    where = jnp.stack([z, position % GROUP_SEGS, position // GROUP_SEGS]).astype(jnp.int32)
    gain, noise = seg_gain[0], seg_noise[0]
    states = gain.shape[1]
    steps = step_gain.shape[0]
    parcel_shape = shape((BLOCK + TAIL, 3 * BLOCK))

    def route(block, moves):
        table = []
        for g in range(groups):
            for (source, start), (target, end) in moves:
                table.append(((g * GROUP_SEGS + source) * RING + start, (g * GROUP_SEGS + target) * RING + end))
        return lax.ppermute(block, ("tm", "tile"), table)

    def send(block, pairs, shift):
        return route(block, [((a, (to + shift) % RING), (b, to)) for a, b in pairs for to in range(RING)])

    def exchange(block, pairs, own=None):
        others = [send(block, pairs, a) for a in (2, 1, 3)]
        return [send(block, pairs, 0) if own is None else own, others[1], others[0], others[2]]

    def within(segments, steps):
        return [((a, start), (a, to)) for a in segments for start, to in steps]

    def call(kernel, name, out_shape, operands, scratch, flops, aliases={}):
        moved = sum(x.size * x.dtype.itemsize for x in list(operands) + list(out_shape))
        return pl.pallas_call(
            kernel,
            out_shape=out_shape,
            in_specs=[smem()] + [vmem()] * len(operands),
            out_specs=(vmem(),) * len(out_shape),
            scratch_shapes=scratch,
            input_output_aliases=aliases,
            compiler_params=params(),
            cost_estimate=cost(flops, moved),
            name=name,
        )(where, *operands)

    def pack(kernel, name, out_shape, far_operands, near_operands, sems, limit):
        return pl.pallas_call(
            kernel,
            out_shape=out_shape,
            in_specs=[smem()] + [pl.BlockSpec(memory_space=pl.ANY)] * len(far_operands) + [vmem()] * len(near_operands),
            out_specs=jax.tree.map(lambda _: vmem(), out_shape),
            scratch_shapes=[sems],
            compiler_params=pltpu.CompilerParams(vmem_limit_bytes=limit),
            cost_estimate=cost(0, 1e6),
            name=name,
        )(where, *far_operands, *near_operands)

    full_and_mean = [pltpu.VMEM((states, states), BF16), pltpu.VMEM((TAIL, states), BF16)]
    row_shape, mean_shape, block_shape = shape((BLOCK, states)), shape((TAIL, BLOCK)), shape((BLOCK, BLOCK))
    half_shapes = (shape((RING, 3 * BLOCK, BLOCK)), shape((TAIL, states)))

    back, two_on, on = ((1, 0), (2, 1), (3, 2), (0, 3)), ((0, 2), (1, 3), (2, 0), (3, 1)), ((0, 1), (1, 2), (2, 3), (3, 0))
    pair_gains = [route(gain, within((3, 2, 1), back)), route(gain, within((3, 2), ((2, 0), (1, 3))) + within((1,), on))]
    parcel = pack(pack_kernel, "pack", parcel_shape, (end_cov, noise), (end_mean, seg_offset), pltpu.SemaphoreType.DMA((3,)), ALL_VMEM)
    first = [send(parcel, ((0 if a == 2 else 3, 3), (1, 1)), a) for a in range(1, RING)]

    def hand(segment, event):
        kernel = functools.partial(hand_kernel, segment)
        return pack(kernel, f"hand_{segment}", row_shape, (event, gain), (), pltpu.SemaphoreType.DMA, VMEM)

    gains_1 = [pair_gains[0], route(hand(1, first[1]), within((1,), two_on)), pair_gains[1]]

    flops = 4 * BLOCK * states * states
    *kept, parcel_3, mean_3 = call(
        functools.partial(pairs_kernel, 3),
        "pairs_3",
        (*half_shapes, parcel_shape, mean_shape),
        (gain, *pair_gains, noise, seg_offset, end_cov, end_mean, *first),
        full_and_mean + [pltpu.VMEM(parcel_shape.shape, BF16)],
        flops,
    )
    second = exchange(parcel_3, ((3, 2),))

    *kept, parcel_2, mean_2, beside_block, far_block = call(
        functools.partial(pairs_kernel, 2),
        "pairs_2",
        (*half_shapes, parcel_shape, mean_shape, block_shape, block_shape),
        (gain, *pair_gains, noise, seg_offset, *second, parcel_3, *kept),
        full_and_mean,
        flops,
        {11: 0, 12: 1},
    )
    own = send(parcel_2, ((2, 1),), 0)
    across = send(parcel_2, ((2, 1),), 2)
    sides = [
        route(parcel_2, [((2, start), (1, to)) for start, to in moves])
        for moves in (((1, 0), (2, 1), (3, 2)), ((0, 1), (1, 2), (2, 3)))
    ]
    third = [own, sides[0], across, sides[1], route(across, within((1,), ((2, 3), (1, 0))))]
    (lift,) = call(stack_kernel, "stack", (shape((2 * states + TAIL, states)),), (parcel_2, gain, *gains_1, parcel, *first), [], 0)
    lift = send(lift, ((1, 0),), 0)
    gain_0 = hand(0, lift)
    left, base, through, beside, beside_block, far_block = call(
        ahead_kernel,
        "ahead",
        (shape(step_gain.shape), shape((steps, BLOCK), F32), row_shape, shape((BLOCK, states), F32), block_shape, block_shape),
        (gain_0, lift, gain, step_gain, beside_block, far_block),
        [],
        4 * (steps + 1) * BLOCK * states * states,
    )
    gains_0 = [route(gain_0, within((0,), moves)) for moves in (back, two_on, on)]
    near, far = route(beside_block, within((3, 2), on)), route(far_block, within((3, 2), ((0, 2), (3, 1))))
    (ends_1,) = call(turn_kernel, "turn", (shape((RING, *parcel_shape.shape)),), (near, far, *third), [], 0)
    ends_0 = send(ends_1, ((1, 0),), 0)
    out_steps = shape((steps, BLOCK), F32)
    _, means, step_mean, step_spread, stats = call(
        moments_kernel,
        "moments",
        (*half_shapes, out_steps, out_steps, shape((2, steps, BLOCK), F32)),
        (ends_1, ends_0, lift, left, base, step_gain, step_offset, step_var, *kept),
        [],
        2 * steps * BLOCK * states * states,
        {9: 0, 10: 1},
    )
    everyone = tuple((s, s) for s in range(GROUP_SEGS))
    all_stats = [stats] + [send(stats, everyone, a) for a in range(1, RING)]
    rows, mean_1 = call(
        last_kernel,
        "last",
        (row_shape, mean_shape),
        (gain, *gains_1, *gains_0, ends_1, ends_0, lift, through, beside, noise, seg_offset, means),
        full_and_mean,
        flops,
    )
    innovation, out_mean, out_cov = pl.pallas_call(
        innovation_kernel,
        out_shape=(shape(obs_value.shape, F32), shape((1, BLOCK)), row_shape),
        in_specs=[smem()] * 3 + [vmem()] * 12 + [pl.BlockSpec(memory_space=pl.ANY)],
        out_specs=(vmem(), vmem(), pl.BlockSpec(memory_space=pl.ANY)),
        scratch_shapes=[pltpu.VMEM((2, steps, states), F32), pltpu.VMEM(row_shape.shape, BF16), pltpu.SemaphoreType.DMA],
        input_output_aliases={15: 2},
        compiler_params=params(),
        cost_estimate=cost(0, 2e5),
        name="innovation",
    )(where, obs_tiles.T, obs_count, *all_stats, obs_value, obs_noise.reshape(1, states), parcel_2, far, near, mean_1, mean_2, mean_3, rows)
    return out_cov[None], out_mean, step_mean, step_spread, innovation


def solution(mesh):
    in_specs = (
        P("tm", "tile", None),
        P("tm", "tile"),
        P("tm", "tile", None),
        P(None, "tile"),
        P(None, "tile", None),
        P("tm", "tile", None),
        P("tm", "tile"),
        P("tm", "tile"),
        P("tm", None),
        P("tm"),
        P("tm", None, None),
        P(),
    )
    out_specs = (
        P("tm", "tile", None),
        P("tm", "tile"),
        P("tm", "tile"),
        P("tm", "tile"),
        P("tm", None, None),
    )
    if mesh.shape["tile"] == RING:
        shards = functools.partial(ring_shards, mesh.shape["tm"] // GROUP_SEGS)
    else:
        shards = general_shards
    return jax.shard_map(shards, mesh=mesh, in_specs=in_specs, out_specs=out_specs, check_vma=False)
```

```python
import functools
import jax
import jax.numpy as jnp
from jax import lax
from jax.experimental import pallas as pl
from jax.experimental.pallas import tpu as pltpu
from jax.sharding import PartitionSpec as P

TILE_STATES = 128
SLOTS = 4
GROUP_SEGS = 4


def shifted(block, axis, distance):
    devices = range(lax.axis_size(axis))
    route = [(i - distance, i) for i in devices if i - distance in devices]
    return lax.ppermute(block, axis, route)


def general_shards(
    seg_gain,
    seg_offset,
    seg_noise,
    end_mean,
    end_cov,
    step_gain,
    step_offset,
    step_var,
    obs_tiles,
    obs_count,
    obs_value,
    obs_noise,
):
    position = lax.axis_index("tm")
    slot_place = position % GROUP_SEGS
    group_index = position // GROUP_SEGS
    gain_rows = seg_gain[0]
    offset_rows = seg_offset[0]
    noise_rows = seg_noise[0].astype(jnp.float32)
    row_count = gain_rows.shape[0]
    state_count = gain_rows.shape[1]
    cur_mean = lax.dynamic_index_in_dim(end_mean, group_index, 0, keepdims=False)
    cur_cov = lax.dynamic_index_in_dim(end_cov, group_index, 0, keepdims=False)
    kept_mean = jnp.zeros((state_count,), jnp.bfloat16)
    kept_cov = jnp.zeros((state_count, state_count), jnp.bfloat16)
    out_mean = jnp.zeros((row_count,), jnp.bfloat16)
    out_cov = jnp.zeros((row_count, state_count), jnp.bfloat16)
    for depth_step in range(GROUP_SEGS):
        whole_mean, whole_cov = (
            lax.all_gather(cur_mean, "tile", axis=0, tiled=True),
            lax.all_gather(cur_cov, "tile", axis=0, tiled=True),
        )
        is_mine = slot_place == GROUP_SEGS - 1 - depth_step
        kept_mean = jnp.where(is_mine, whole_mean, kept_mean)
        kept_cov = jnp.where(is_mine, whole_cov, kept_cov)
        product = jnp.dot(gain_rows, whole_cov, preferred_element_type=jnp.float32).astype(
            jnp.bfloat16
        )
        col_block = jnp.einsum(
            "pd,rd->pr",
            lax.all_gather(product, "tile", axis=0, tiled=True),
            gain_rows,
            preferred_element_type=jnp.float32,
        )
        spread_rows = lax.all_to_all(col_block, "tile", split_axis=0, concat_axis=1, tiled=True)
        new_cov = (spread_rows + noise_rows).astype(jnp.bfloat16)
        new_mean = (
            jnp.dot(gain_rows, whole_mean, preferred_element_type=jnp.float32) + offset_rows
        ).astype(jnp.bfloat16)
        out_mean = jnp.where(is_mine, new_mean, out_mean)
        out_cov = jnp.where(is_mine, new_cov, out_cov)
        if depth_step < GROUP_SEGS - 1:
            got_mean, got_cov = shifted((new_mean, new_cov), "tm", -1)
            takes_next = slot_place == GROUP_SEGS - 2 - depth_step
            cur_mean = jnp.where(takes_next, got_mean, cur_mean)
            cur_cov = jnp.where(takes_next, got_cov, cur_cov)
    partial_value = jnp.einsum(
        "krd,de->kre", step_gain, kept_cov, preferred_element_type=jnp.float32
    )
    local_spread = jnp.sum(partial_value * step_gain, axis=2) + step_var
    local_mean = (
        jnp.einsum("krd,d->kr", step_gain, kept_mean, preferred_element_type=jnp.float32)
        + step_offset
    )
    full_mean, full_spread = (
        lax.all_gather(local_mean, "tile", axis=1, tiled=True),
        lax.all_gather(local_spread, "tile", axis=1, tiled=True),
    )
    step_count = full_mean.shape[0]
    tile_total = state_count // TILE_STATES
    tile_mean = full_mean.reshape(step_count, tile_total, TILE_STATES)
    tile_spread = full_spread.reshape(step_count, tile_total, TILE_STATES) + obs_noise.reshape(
        1, tile_total, TILE_STATES
    )
    onehot = (
        obs_tiles[:, :, None] == jnp.arange(tile_total, dtype=jnp.int32)[None, None, :]
    ).astype(jnp.float32)
    picked_mean = jnp.einsum("ksn,kno->kso", onehot, tile_mean, precision=lax.Precision.HIGHEST)
    picked_spread = jnp.einsum("ksn,kno->kso", onehot, tile_spread, precision=lax.Precision.HIGHEST)
    live_slots = jnp.arange(SLOTS, dtype=jnp.int32)[None, :] < obs_count[:, None]
    innovation = jnp.where(
        live_slots[:, :, None], (obs_value - picked_mean) / picked_spread, jnp.float32(0.0)
    )
    return (out_cov[None], out_mean[None], local_mean, local_spread, innovation)


BLOCK = 256
RING = 4
TAIL = 16
VMEM = 12 * 1024 * 1024
ALL_VMEM = 56 * 1024 * 1024
NT = (((1,), (1,)), ((), ()))
F32 = jnp.float32
BF16 = jnp.bfloat16


def cols(index):
    return pl.ds(pl.multiple_of(index * BLOCK, BLOCK), BLOCK)


def spot(z, shift):
    return lax.rem(z + shift, RING)


def dot(a, b):
    return jnp.dot(a, b, preferred_element_type=F32)


def dot_nt(a, b):
    return lax.dot_general(a, b, NT, preferred_element_type=F32)


def owns_far(row):
    return (row == 0) | (row == RING - 1)


def each_parcel(parcels, body):
    for a, entry in enumerate(parcels):
        if isinstance(entry, tuple):
            condition, one, other = entry
            pl.when(condition)(functools.partial(body, a, one))
            pl.when(jnp.logical_not(condition))(functools.partial(body, a, other))
        else:
            body(a, entry)


def by_relay(z, own, after, across, before, handed):
    return own, after, across, (z > 0, before, handed)


def lay_out(z, parcels, full, mean):
    def body(a, parcel):
        at = spot(z, a)
        row, near, far = cols(at), cols(spot(z, a + 1)), cols(spot(z, a + 2))
        full[row, row] = parcel[:BLOCK, :BLOCK]
        beside = parcel[:BLOCK, BLOCK : 2 * BLOCK]
        full[row, near] = beside
        full[near, row] = beside.T
        mean[:, row] = parcel[BLOCK:, :BLOCK]

        @pl.when(owns_far(at))
        def _():
            block = parcel[:BLOCK, 2 * BLOCK :]
            full[row, far] = block
            full[far, row] = block.T

    each_parcel(parcels, body)


def keep_parcels(z, parcels, half, half_mean):
    def body(a, parcel):
        at = spot(z, a)
        half_mean[:, cols(at)] = parcel[BLOCK:, :BLOCK]
        half[at, 2 * BLOCK :, :] = parcel[:BLOCK, :BLOCK]
        half[spot(z, a + 1), BLOCK : 2 * BLOCK, :] = parcel[:BLOCK, BLOCK : 2 * BLOCK] * 2

        @pl.when(owns_far(at))
        def _():
            half[spot(z, a + 2), :BLOCK, :] = parcel[:BLOCK, 2 * BLOCK :] * 2

    each_parcel(parcels, body)


def keep_whole(full, mean, half, half_mean):
    half_mean[...] = mean[...]
    for b in range(RING):
        column = slice(b * BLOCK, (b + 1) * BLOCK)
        for j in range(3):
            if j < 2 or b in (1, 2):
                row = (b - j) % RING * BLOCK
                block = full[row : row + BLOCK, column]
                half[b, (2 - j) * BLOCK : (3 - j) * BLOCK, :] = block * 2 if j else block


def fetch(source, z, tail, parcel, sems):
    copies = []
    for j in range(3):
        target = parcel.at[pl.ds(0, BLOCK), pl.ds(j * BLOCK, BLOCK)]
        copies.append(pltpu.make_async_copy(source.at[:, cols(spot(z, j))], target, sems.at[j]))
    for copy in copies:
        copy.start()
    parcel[BLOCK:, :] = jnp.zeros((TAIL, 3 * BLOCK), BF16)
    parcel[BLOCK:, :BLOCK] = tail.astype(BF16)
    for copy in copies:
        copy.wait()


def group_mean(group, end_mean):
    mean = jnp.zeros((1, BLOCK), F32)
    for g in range(end_mean.shape[0]):
        mean = jnp.where(group == g, end_mean[g : g + 1, :].astype(F32), mean)
    return jnp.broadcast_to(mean, (TAIL, BLOCK))


def pack_kernel(where, end_cov, noise, end_mean, offset, parcel, sems):
    z, seg, group = where[0], where[1], where[2]

    @pl.when(seg == 1)
    def _():
        high = offset[...].astype(BF16).astype(F32)
        first = lax.broadcasted_iota(jnp.int32, (TAIL, BLOCK), 0) == 0
        fetch(noise, z, jnp.where(first, high, offset[...] - high), parcel, sems)

    @pl.when(seg != 1)
    def _():
        fetch(end_cov.at[group], z, group_mean(group, end_mean), parcel, sems)


def pairs_kernel(at_seg, where, g0, g1, g2, noise, offset, *refs):
    z, seg, group = where[0], where[1], where[2]
    if at_seg == GROUP_SEGS - 1:
        end_cov, end_mean, *others, half, half_mean, parcel, mean_row, full, mean, own = refs
        parcels = (own, *others)
    else:
        *parcels, early, _, _, half, half_mean, parcel, mean_row, beside, far, full, mean = refs

    @pl.when(seg == at_seg)
    def _():
        if at_seg == GROUP_SEGS - 1:
            for j in range(3):
                own[:BLOCK, j * BLOCK : (j + 1) * BLOCK] = end_cov[group, :, cols(spot(z, j))]
            own[BLOCK:, :BLOCK] = group_mean(group, end_mean).astype(BF16)
        lay_out(z, parcels, full, mean)
        product = dot(g0[...], full[...]).astype(BF16)
        for j, gain in enumerate((g0, g1, g2)):
            block = dot_nt(product, gain[...]) + noise[:, cols(spot(z, j))].astype(F32)
            parcel[:BLOCK, j * BLOCK : (j + 1) * BLOCK] = block.astype(BF16)
        new_mean = (dot_nt(mean[...], g0[...]) + offset[...]).astype(BF16)
        parcel[BLOCK:, :BLOCK] = new_mean
        parcel[BLOCK:, BLOCK:] = jnp.zeros((TAIL, 2 * BLOCK), BF16)
        mean_row[...] = new_mean
        keep_whole(full, mean, half, half_mean)

    if at_seg < GROUP_SEGS - 1:
        @pl.when(seg == GROUP_SEGS - 1)
        def _():
            parcel[...] = early[...]

        beside[...] = parcel[:BLOCK, BLOCK : 2 * BLOCK]
        far[...] = parcel[:BLOCK, 2 * BLOCK :]


def hand_kernel(at_seg, where, event, gain, out, sem):
    @pl.when(where[1] == at_seg)
    def _():
        copy = pltpu.make_async_copy(gain, out, sem)
        copy.start()
        copy.wait()


def stack_kernel(where, event, g0, g1, g2, g3, n0, n1, n2, n3, lift):
    z, seg = where[0], where[1]
    states = g0.shape[1]

    @pl.when(seg == 1)
    def _():
        for a, gain in enumerate((g0, g1, g2, g3)):
            lift[cols(spot(z, a)), :] = gain[...]
        lay_out(z, (n0, n1, n2, n3), lift.at[pl.ds(states, states)], lift.at[pl.ds(2 * states, TAIL)])


def turn_kernel(where, near, far, t0, t1, t2, t3, t4, out):
    def body(a, parcel):
        out[a] = parcel[...]

    @pl.when(where[1] == 1)
    def _():
        each_parcel(by_relay(where[0], t0, t1, t2, t3, t4), body)


def ahead_kernel(where, event, lift, gain, step_gain, block_1, block_2, left, base, through, beside, block_1_on, block_2_on):
    seg = where[1]
    states = gain.shape[1]

    @pl.when(seg > 1)
    def _():
        block_1_on[...] = block_1[...]
        block_2_on[...] = block_2[...]

    @pl.when(seg == 0)
    def _():
        through[...] = dot(gain[...], lift[:states, :]).astype(BF16)
        beside[...] = dot(gain[...], lift[states : 2 * states, :])

        def one(k, carry):
            rows = step_gain[k]
            left[k] = dot(rows, lift[:states, :]).astype(BF16)
            value = dot(rows, lift[states : 2 * states, :]) * rows.astype(F32)
            base[pl.ds(k, 1), :] = row_sums(value)
            return carry

        lax.fori_loop(0, step_gain.shape[0], one, 0)


def row_sums(value):
    total = value[:, :128]
    for at in range(128, value.shape[1], 128):
        total = total + value[:, at : at + 128]
    return jnp.sum(total.T, axis=0, keepdims=True)


def moments_kernel(where, ends_1, ends_0, lift, left, base, gain, offset, var, kept, kept_mean, half, half_mean, out_mean, out_spread, out):
    z, seg = where[0], where[1]
    states = gain.shape[2]

    @pl.when(seg == 1)
    def _():
        keep_parcels(z, [ends_1.at[a] for a in range(RING)], half, half_mean)

    @pl.when(seg == 0)
    def _():
        keep_parcels(z, [ends_0.at[a] for a in range(RING)], half, half_mean)
        tail = lift[2 * states :, :].astype(F32)
        half_mean[...] = (dot_nt(half_mean[...], lift[:states, :]) + tail[0:1] + tail[1:2]).astype(BF16)

    def steps(rows_of, more):
        def one(k, carry):
            total = jnp.zeros((BLOCK, BLOCK), F32)
            for b in range(RING):
                blocks = (b + 2, b + 3, b) if b in (1, 2) else (b + 3, b)
                parts = [rows_of[k, :, (r % RING) * BLOCK : (r % RING + 1) * BLOCK] for r in blocks]
                value = dot(jnp.concatenate(parts, axis=1), half[b, (3 - len(blocks)) * BLOCK :, :])
                total = total + value * parts[-1].astype(F32)
            spread = row_sums(total) + var[pl.ds(k, 1), :]
            if more is not None:
                spread = spread + more[pl.ds(k, 1), :]
            means = dot_nt(half_mean[...], gain[k])[0:1] + offset[pl.ds(k, 1), :]
            out[0, pl.ds(k, 1), :] = means
            out[1, pl.ds(k, 1), :] = spread
            out_mean[pl.ds(k, 1), :] = means
            out_spread[pl.ds(k, 1), :] = spread
            return carry

        lax.fori_loop(0, gain.shape[0], one, 0, unroll=4)

    @pl.when(seg == 0)
    def _():
        steps(left, base)

    @pl.when(seg != 0)
    def _():
        steps(gain, None)


def last_kernel(where, g0, a1, a2, a3, b1, b2, b3, ends_1, ends_0, lift, through, beside, noise, offset, means, rows, mean_row, full, mean):
    z, seg = where[0], where[1]
    states = g0.shape[1]

    def finish(product, gains):
        for a, gain in enumerate(gains):
            column = cols(spot(z, a))
            rows[:, column] = (dot_nt(product, gain[...]) + noise[:, column].astype(F32)).astype(BF16)
        mean_row[...] = (dot_nt(means[...], g0[...]) + offset[...]).astype(BF16)

    @pl.when(seg == 0)
    def _():
        lay_out(z, [ends_0.at[a] for a in range(RING)], full, mean)
        product = dot(through[...], full[...]).astype(BF16)
        finish((dot_nt(product, lift[:states, :]) + beside[...]).astype(BF16), (g0, b1, b2, b3))

    @pl.when(seg == 1)
    def _():
        lay_out(z, [ends_1.at[a] for a in range(RING)], full, mean)
        finish(dot(g0[...], full[...]).astype(BF16), (g0, a1, a2, a3))


def innovation_kernel(where, tiles, counts, s0, s1, s2, s3, value, noise, own, far, near, mean_1, mean_2, mean_3, _, out, mean_row, rows_out, full, rows, sem):
    z, seg = where[0], where[1]
    copy = pltpu.make_async_copy(rows, rows_out, sem)

    @pl.when(seg > 1)
    def _():
        rows[:, cols(z)] = own[:BLOCK, :BLOCK]
        rows[:, cols(spot(z, 1))] = own[:BLOCK, BLOCK : 2 * BLOCK]
        rows[:, cols(spot(z, 3))] = near[...].T

        @pl.when(owns_far(z))
        def _():
            rows[:, cols(spot(z, 2))] = own[:BLOCK, 2 * BLOCK :]

        @pl.when(jnp.logical_not(owns_far(z)))
        def _():
            rows[:, cols(spot(z, 2))] = far[...].T

        copy.start()

    mean = mean_1[0:1].astype(F32)
    for at, source in ((2, mean_2), (3, mean_3)):
        mean = jnp.where(seg == at, source[0:1].astype(F32), mean)
    mean_row[...] = mean.astype(BF16)
    for a, part in enumerate((s0, s1, s2, s3)):
        full[:, :, cols(spot(z, a))] = part[...]
    full[1] = full[1] + noise[...]
    for k in range(value.shape[0]):
        for j in range(SLOTS):
            at = pl.ds(pl.multiple_of(tiles[j, k] * TILE_STATES, TILE_STATES), TILE_STATES)
            result = (value[k, j : j + 1, :] - full[0, k : k + 1, at]) / full[1, k : k + 1, at]
            out[k, j : j + 1, :] = jnp.where(j < counts[k], result, 0.0)

    @pl.when(seg > 1)
    def _():
        copy.wait()


def smem():
    return pl.BlockSpec(memory_space=pltpu.SMEM)


def vmem():
    return pl.BlockSpec(memory_space=pltpu.VMEM)


def params():
    return pltpu.CompilerParams(vmem_limit_bytes=VMEM)


def cost(flops, moved):
    return pl.CostEstimate(flops=int(flops), bytes_accessed=int(moved), transcendentals=0)


def shape(dims, kind=BF16):
    return jax.ShapeDtypeStruct(dims, kind)


def ring_shards(groups, seg_gain, seg_offset, seg_noise, end_mean, end_cov, step_gain, step_offset, step_var, obs_tiles, obs_count, obs_value, obs_noise):
    position = lax.axis_index("tm")
    z = lax.axis_index("tile")
    where = jnp.stack([z, position % GROUP_SEGS, position // GROUP_SEGS]).astype(jnp.int32)
    gain, noise = seg_gain[0], seg_noise[0]
    states = gain.shape[1]
    steps = step_gain.shape[0]
    parcel_shape = shape((BLOCK + TAIL, 3 * BLOCK))

    def route(block, moves):
        table = []
        for g in range(groups):
            for (source, start), (target, end) in moves:
                table.append(((g * GROUP_SEGS + source) * RING + start, (g * GROUP_SEGS + target) * RING + end))
        return lax.ppermute(block, ("tm", "tile"), table)

    def send(block, pairs, shift):
        return route(block, [((a, (to + shift) % RING), (b, to)) for a, b in pairs for to in range(RING)])

    def exchange(block, pairs, own=None):
        others = [send(block, pairs, a) for a in (2, 1, 3)]
        return [send(block, pairs, 0) if own is None else own, others[1], others[0], others[2]]

    def within(segments, steps):
        return [((a, start), (a, to)) for a in segments for start, to in steps]

    def call(kernel, name, out_shape, operands, scratch, flops, aliases={}):
        moved = sum(x.size * x.dtype.itemsize for x in list(operands) + list(out_shape))
        return pl.pallas_call(
            kernel,
            out_shape=out_shape,
            in_specs=[smem()] + [vmem()] * len(operands),
            out_specs=(vmem(),) * len(out_shape),
            scratch_shapes=scratch,
            input_output_aliases=aliases,
            compiler_params=params(),
            cost_estimate=cost(flops, moved),
            name=name,
        )(where, *operands)

    def pack(kernel, name, out_shape, far_operands, near_operands, sems, limit):
        return pl.pallas_call(
            kernel,
            out_shape=out_shape,
            in_specs=[smem()] + [pl.BlockSpec(memory_space=pl.ANY)] * len(far_operands) + [vmem()] * len(near_operands),
            out_specs=jax.tree.map(lambda _: vmem(), out_shape),
            scratch_shapes=[sems],
            compiler_params=pltpu.CompilerParams(vmem_limit_bytes=limit),
            cost_estimate=cost(0, 1e6),
            name=name,
        )(where, *far_operands, *near_operands)

    full_and_mean = [pltpu.VMEM((states, states), BF16), pltpu.VMEM((TAIL, states), BF16)]
    row_shape, mean_shape, block_shape = shape((BLOCK, states)), shape((TAIL, BLOCK)), shape((BLOCK, BLOCK))
    half_shapes = (shape((RING, 3 * BLOCK, BLOCK)), shape((TAIL, states)))

    back, two_on, on = ((1, 0), (2, 1), (3, 2), (0, 3)), ((0, 2), (1, 3), (2, 0), (3, 1)), ((0, 1), (1, 2), (2, 3), (3, 0))
    pair_gains = [route(gain, within((3, 2, 1), back)), route(gain, within((3, 2), ((2, 0), (1, 3))) + within((1,), on))]
    parcel = pack(pack_kernel, "pack", parcel_shape, (end_cov, noise), (end_mean, seg_offset), pltpu.SemaphoreType.DMA((3,)), ALL_VMEM)
    first = [send(parcel, ((0 if a == 2 else 3, 3), (1, 1)), a) for a in range(1, RING)]

    def hand(segment, event):
        kernel = functools.partial(hand_kernel, segment)
        return pack(kernel, f"hand_{segment}", row_shape, (event, gain), (), pltpu.SemaphoreType.DMA, VMEM)

    gains_1 = [pair_gains[0], route(hand(1, first[1]), within((1,), two_on)), pair_gains[1]]

    flops = 4 * BLOCK * states * states
    *kept, parcel_3, mean_3 = call(
        functools.partial(pairs_kernel, 3),
        "pairs_3",
        (*half_shapes, parcel_shape, mean_shape),
        (gain, *pair_gains, noise, seg_offset, end_cov, end_mean, *first),
        full_and_mean + [pltpu.VMEM(parcel_shape.shape, BF16)],
        flops,
    )
    second = exchange(parcel_3, ((3, 2),))

    *kept, parcel_2, mean_2, beside_block, far_block = call(
        functools.partial(pairs_kernel, 2),
        "pairs_2",
        (*half_shapes, parcel_shape, mean_shape, block_shape, block_shape),
        (gain, *pair_gains, noise, seg_offset, *second, parcel_3, *kept),
        full_and_mean,
        flops,
        {11: 0, 12: 1},
    )
    own = send(parcel_2, ((2, 1),), 0)
    across = send(parcel_2, ((2, 1),), 2)
    sides = [
        route(parcel_2, [((2, start), (1, to)) for start, to in moves])
        for moves in (((1, 0), (2, 1), (3, 2), (0, 3)), ((0, 1), (1, 2), (2, 3)))
    ]
    third = [own, sides[0], across, sides[1], route(across, within((1,), ((1, 0),)))]
    (lift,) = call(stack_kernel, "stack", (shape((2 * states + TAIL, states)),), (parcel_2, gain, *gains_1, parcel, *first), [], 0)
    lift = send(lift, ((1, 0),), 0)
    gain_0 = hand(0, lift)
    left, base, through, beside, beside_block, far_block = call(
        ahead_kernel,
        "ahead",
        (shape(step_gain.shape), shape((steps, BLOCK), F32), row_shape, shape((BLOCK, states), F32), block_shape, block_shape),
        (gain_0, lift, gain, step_gain, beside_block, far_block),
        [],
        4 * (steps + 1) * BLOCK * states * states,
    )
    gains_0 = [route(gain_0, within((0,), moves)) for moves in (back, two_on, on)]
    near, far = route(beside_block, within((3, 2), on)), route(far_block, within((3, 2), ((0, 2), (3, 1))))
    (ends_1,) = call(turn_kernel, "turn", (shape((RING, *parcel_shape.shape)),), (near, far, *third), [], 0)
    ends_0 = send(ends_1, ((1, 0),), 0)
    out_steps = shape((steps, BLOCK), F32)
    _, means, step_mean, step_spread, stats = call(
        moments_kernel,
        "moments",
        (*half_shapes, out_steps, out_steps, shape((2, steps, BLOCK), F32)),
        (ends_1, ends_0, lift, left, base, step_gain, step_offset, step_var, *kept),
        [],
        2 * steps * BLOCK * states * states,
        {9: 0, 10: 1},
    )
    everyone = tuple((s, s) for s in range(GROUP_SEGS))
    all_stats = [stats] + [send(stats, everyone, a) for a in range(1, RING)]
    rows, mean_1 = call(
        last_kernel,
        "last",
        (row_shape, mean_shape),
        (gain, *gains_1, *gains_0, ends_1, ends_0, lift, through, beside, noise, seg_offset, means),
        full_and_mean,
        flops,
    )
    innovation, out_mean, out_cov = pl.pallas_call(
        innovation_kernel,
        out_shape=(shape(obs_value.shape, F32), shape((1, BLOCK)), row_shape),
        in_specs=[smem()] * 3 + [vmem()] * 12 + [pl.BlockSpec(memory_space=pl.ANY)],
        out_specs=(vmem(), vmem(), pl.BlockSpec(memory_space=pl.ANY)),
        scratch_shapes=[pltpu.VMEM((2, steps, states), F32), pltpu.VMEM(row_shape.shape, BF16), pltpu.SemaphoreType.DMA],
        input_output_aliases={15: 2},
        compiler_params=params(),
        cost_estimate=cost(0, 2e5),
        name="innovation",
    )(where, obs_tiles.T, obs_count, *all_stats, obs_value, obs_noise.reshape(1, states), parcel_2, far, near, mean_1, mean_2, mean_3, rows)
    return out_cov[None], out_mean, step_mean, step_spread, innovation


def solution(mesh):
    in_specs = (
        P("tm", "tile", None),
        P("tm", "tile"),
        P("tm", "tile", None),
        P(None, "tile"),
        P(None, "tile", None),
        P("tm", "tile", None),
        P("tm", "tile"),
        P("tm", "tile"),
        P("tm", None),
        P("tm"),
        P("tm", None, None),
        P(),
    )
    out_specs = (
        P("tm", "tile", None),
        P("tm", "tile"),
        P("tm", "tile"),
        P("tm", "tile"),
        P("tm", None, None),
    )
    if mesh.shape["tile"] == RING:
        shards = functools.partial(ring_shards, mesh.shape["tm"] // GROUP_SEGS)
    else:
        shards = general_shards
    return jax.shard_map(shards, mesh=mesh, in_specs=in_specs, out_specs=out_specs, check_vma=False)
```

```python
import functools
import jax
import jax.numpy as jnp
from jax import lax
from jax.experimental import pallas as pl
from jax.experimental.pallas import tpu as pltpu
from jax.sharding import PartitionSpec as P

TILE_STATES = 128
SLOTS = 4
GROUP_SEGS = 4


def shifted(block, axis, distance):
    devices = range(lax.axis_size(axis))
    route = [(i - distance, i) for i in devices if i - distance in devices]
    return lax.ppermute(block, axis, route)


def general_shards(
    seg_gain,
    seg_offset,
    seg_noise,
    end_mean,
    end_cov,
    step_gain,
    step_offset,
    step_var,
    obs_tiles,
    obs_count,
    obs_value,
    obs_noise,
):
    position = lax.axis_index("tm")
    slot_place = position % GROUP_SEGS
    group_index = position // GROUP_SEGS
    gain_rows = seg_gain[0]
    offset_rows = seg_offset[0]
    noise_rows = seg_noise[0].astype(jnp.float32)
    row_count = gain_rows.shape[0]
    state_count = gain_rows.shape[1]
    cur_mean = lax.dynamic_index_in_dim(end_mean, group_index, 0, keepdims=False)
    cur_cov = lax.dynamic_index_in_dim(end_cov, group_index, 0, keepdims=False)
    kept_mean = jnp.zeros((state_count,), jnp.bfloat16)
    kept_cov = jnp.zeros((state_count, state_count), jnp.bfloat16)
    out_mean = jnp.zeros((row_count,), jnp.bfloat16)
    out_cov = jnp.zeros((row_count, state_count), jnp.bfloat16)
    for depth_step in range(GROUP_SEGS):
        whole_mean, whole_cov = (
            lax.all_gather(cur_mean, "tile", axis=0, tiled=True),
            lax.all_gather(cur_cov, "tile", axis=0, tiled=True),
        )
        is_mine = slot_place == GROUP_SEGS - 1 - depth_step
        kept_mean = jnp.where(is_mine, whole_mean, kept_mean)
        kept_cov = jnp.where(is_mine, whole_cov, kept_cov)
        product = jnp.dot(gain_rows, whole_cov, preferred_element_type=jnp.float32).astype(
            jnp.bfloat16
        )
        col_block = jnp.einsum(
            "pd,rd->pr",
            lax.all_gather(product, "tile", axis=0, tiled=True),
            gain_rows,
            preferred_element_type=jnp.float32,
        )
        spread_rows = lax.all_to_all(col_block, "tile", split_axis=0, concat_axis=1, tiled=True)
        new_cov = (spread_rows + noise_rows).astype(jnp.bfloat16)
        new_mean = (
            jnp.dot(gain_rows, whole_mean, preferred_element_type=jnp.float32) + offset_rows
        ).astype(jnp.bfloat16)
        out_mean = jnp.where(is_mine, new_mean, out_mean)
        out_cov = jnp.where(is_mine, new_cov, out_cov)
        if depth_step < GROUP_SEGS - 1:
            got_mean, got_cov = shifted((new_mean, new_cov), "tm", -1)
            takes_next = slot_place == GROUP_SEGS - 2 - depth_step
            cur_mean = jnp.where(takes_next, got_mean, cur_mean)
            cur_cov = jnp.where(takes_next, got_cov, cur_cov)
    partial_value = jnp.einsum(
        "krd,de->kre", step_gain, kept_cov, preferred_element_type=jnp.float32
    )
    local_spread = jnp.sum(partial_value * step_gain, axis=2) + step_var
    local_mean = (
        jnp.einsum("krd,d->kr", step_gain, kept_mean, preferred_element_type=jnp.float32)
        + step_offset
    )
    full_mean, full_spread = (
        lax.all_gather(local_mean, "tile", axis=1, tiled=True),
        lax.all_gather(local_spread, "tile", axis=1, tiled=True),
    )
    step_count = full_mean.shape[0]
    tile_total = state_count // TILE_STATES
    tile_mean = full_mean.reshape(step_count, tile_total, TILE_STATES)
    tile_spread = full_spread.reshape(step_count, tile_total, TILE_STATES) + obs_noise.reshape(
        1, tile_total, TILE_STATES
    )
    onehot = (
        obs_tiles[:, :, None] == jnp.arange(tile_total, dtype=jnp.int32)[None, None, :]
    ).astype(jnp.float32)
    picked_mean = jnp.einsum("ksn,kno->kso", onehot, tile_mean, precision=lax.Precision.HIGHEST)
    picked_spread = jnp.einsum("ksn,kno->kso", onehot, tile_spread, precision=lax.Precision.HIGHEST)
    live_slots = jnp.arange(SLOTS, dtype=jnp.int32)[None, :] < obs_count[:, None]
    innovation = jnp.where(
        live_slots[:, :, None], (obs_value - picked_mean) / picked_spread, jnp.float32(0.0)
    )
    return (out_cov[None], out_mean[None], local_mean, local_spread, innovation)


BLOCK = 256
RING = 4
TAIL = 16
VMEM = 12 * 1024 * 1024
ALL_VMEM = 56 * 1024 * 1024
NT = (((1,), (1,)), ((), ()))
F32 = jnp.float32
BF16 = jnp.bfloat16


def cols(index):
    return pl.ds(pl.multiple_of(index * BLOCK, BLOCK), BLOCK)


def spot(z, shift):
    return lax.rem(z + shift, RING)


def dot(a, b):
    return jnp.dot(a, b, preferred_element_type=F32)


def dot_nt(a, b):
    return lax.dot_general(a, b, NT, preferred_element_type=F32)


def owns_far(row):
    return (row == 0) | (row == RING - 1)


def each_parcel(parcels, body):
    for a, entry in enumerate(parcels):
        if isinstance(entry, tuple):
            condition, one, other = entry
            pl.when(condition)(functools.partial(body, a, one))
            pl.when(jnp.logical_not(condition))(functools.partial(body, a, other))
        else:
            body(a, entry)


def by_relay(z, own, after, across, before, handed):
    return own, after, across, (z > 0, before, handed)


def lay_out(z, parcels, full, mean):
    def body(a, parcel):
        at = spot(z, a)
        row, near, far = cols(at), cols(spot(z, a + 1)), cols(spot(z, a + 2))
        full[row, row] = parcel[:BLOCK, :BLOCK]
        beside = parcel[:BLOCK, BLOCK : 2 * BLOCK]
        full[row, near] = beside
        full[near, row] = beside.T
        mean[:, row] = parcel[BLOCK:, :BLOCK]

        @pl.when(owns_far(at))
        def _():
            block = parcel[:BLOCK, 2 * BLOCK :]
            full[row, far] = block
            full[far, row] = block.T

    each_parcel(parcels, body)


def keep_parcels(z, parcels, half, half_mean):
    def body(a, parcel):
        at = spot(z, a)
        half_mean[:, cols(at)] = parcel[BLOCK:, :BLOCK]
        half[at, 2 * BLOCK :, :] = parcel[:BLOCK, :BLOCK]
        half[spot(z, a + 1), BLOCK : 2 * BLOCK, :] = parcel[:BLOCK, BLOCK : 2 * BLOCK] * 2

        @pl.when(owns_far(at))
        def _():
            half[spot(z, a + 2), :BLOCK, :] = parcel[:BLOCK, 2 * BLOCK :] * 2

    each_parcel(parcels, body)


def keep_whole(full, mean, half, half_mean):
    half_mean[...] = mean[...]
    for b in range(RING):
        column = slice(b * BLOCK, (b + 1) * BLOCK)
        for j in range(3):
            if j < 2 or b in (1, 2):
                row = (b - j) % RING * BLOCK
                block = full[row : row + BLOCK, column]
                half[b, (2 - j) * BLOCK : (3 - j) * BLOCK, :] = block * 2 if j else block


def fetch(source, z, tail, parcel, sems):
    copies = []
    for j in range(3):
        target = parcel.at[pl.ds(0, BLOCK), pl.ds(j * BLOCK, BLOCK)]
        copies.append(pltpu.make_async_copy(source.at[:, cols(spot(z, j))], target, sems.at[j]))
    for copy in copies:
        copy.start()
    parcel[BLOCK:, :] = jnp.zeros((TAIL, 3 * BLOCK), BF16)
    parcel[BLOCK:, :BLOCK] = tail.astype(BF16)
    for copy in copies:
        copy.wait()


def group_mean(group, end_mean):
    mean = jnp.zeros((1, BLOCK), F32)
    for g in range(end_mean.shape[0]):
        mean = jnp.where(group == g, end_mean[g : g + 1, :].astype(F32), mean)
    return jnp.broadcast_to(mean, (TAIL, BLOCK))


def pack_kernel(where, end_cov, noise, end_mean, offset, parcel, sems):
    z, seg, group = where[0], where[1], where[2]

    @pl.when(seg == 1)
    def _():
        high = offset[...].astype(BF16).astype(F32)
        first = lax.broadcasted_iota(jnp.int32, (TAIL, BLOCK), 0) == 0
        fetch(noise, z, jnp.where(first, high, offset[...] - high), parcel, sems)

    @pl.when(seg != 1)
    def _():
        fetch(end_cov.at[group], z, group_mean(group, end_mean), parcel, sems)


def pairs_kernel(at_seg, where, g0, g1, g2, noise, offset, *refs):
    z, seg, group = where[0], where[1], where[2]
    if at_seg == GROUP_SEGS - 1:
        end_cov, end_mean, *others, half, half_mean, parcel, mean_row, full, mean, own = refs
        parcels = (own, *others)
    else:
        *parcels, early, _, _, half, half_mean, parcel, mean_row, beside, far, full, mean = refs

    @pl.when(seg == at_seg)
    def _():
        if at_seg == GROUP_SEGS - 1:
            for j in range(3):
                own[:BLOCK, j * BLOCK : (j + 1) * BLOCK] = end_cov[group, :, cols(spot(z, j))]
            own[BLOCK:, :BLOCK] = group_mean(group, end_mean).astype(BF16)
        lay_out(z, parcels, full, mean)
        product = dot(g0[...], full[...]).astype(BF16)
        for j, gain in enumerate((g0, g1, g2)):
            block = dot_nt(product, gain[...]) + noise[:, cols(spot(z, j))].astype(F32)
            parcel[:BLOCK, j * BLOCK : (j + 1) * BLOCK] = block.astype(BF16)
        new_mean = (dot_nt(mean[...], g0[...]) + offset[...]).astype(BF16)
        parcel[BLOCK:, :BLOCK] = new_mean
        parcel[BLOCK:, BLOCK:] = jnp.zeros((TAIL, 2 * BLOCK), BF16)
        mean_row[...] = new_mean
        keep_whole(full, mean, half, half_mean)

    if at_seg < GROUP_SEGS - 1:
        @pl.when(seg == GROUP_SEGS - 1)
        def _():
            parcel[...] = early[...]

        beside[...] = parcel[:BLOCK, BLOCK : 2 * BLOCK]
        far[...] = parcel[:BLOCK, 2 * BLOCK :]


def hand_kernel(at_seg, where, event, gain, out, sem):
    @pl.when(where[1] == at_seg)
    def _():
        copy = pltpu.make_async_copy(gain, out, sem)
        copy.start()
        copy.wait()


def stack_kernel(where, event, g0, g1, g2, g3, n0, n1, n2, n3, lift):
    z, seg = where[0], where[1]
    states = g0.shape[1]

    @pl.when(seg == 1)
    def _():
        for a, gain in enumerate((g0, g1, g2, g3)):
            lift[cols(spot(z, a)), :] = gain[...]
        lay_out(z, (n0, n1, n2, n3), lift.at[pl.ds(states, states)], lift.at[pl.ds(2 * states, TAIL)])


def turn_kernel(where, near, far, t0, t1, t2, t3, t4, out):
    def body(a, parcel):
        out[a] = parcel[...]

    @pl.when(where[1] == 1)
    def _():
        each_parcel(by_relay(where[0], t0, t1, t2, t3, t4), body)


def ahead_kernel(where, event, lift, gain, step_gain, block_1, block_2, left, base, through, beside, block_1_on, block_2_on):
    seg = where[1]
    states = gain.shape[1]

    @pl.when(seg > 1)
    def _():
        block_1_on[...] = block_1[...]
        block_2_on[...] = block_2[...]

    @pl.when(seg == 0)
    def _():
        through[...] = dot(gain[...], lift[:states, :]).astype(BF16)
        beside[...] = dot(gain[...], lift[states : 2 * states, :])

        def one(k, carry):
            rows = step_gain[k]
            left[k] = dot(rows, lift[:states, :]).astype(BF16)
            value = dot(rows, lift[states : 2 * states, :]) * rows.astype(F32)
            base[pl.ds(k, 1), :] = row_sums(value)
            return carry

        lax.fori_loop(0, step_gain.shape[0], one, 0, unroll=4)


def row_sums(value):
    total = value[:, :128]
    for at in range(128, value.shape[1], 128):
        total = total + value[:, at : at + 128]
    return jnp.sum(total.T, axis=0, keepdims=True)


def moments_kernel(where, ends_1, ends_0, lift, left, base, gain, offset, var, kept, kept_mean, half, half_mean, out_mean, out_spread, out):
    z, seg = where[0], where[1]
    states = gain.shape[2]

    @pl.when(seg == 1)
    def _():
        keep_parcels(z, [ends_1.at[a] for a in range(RING)], half, half_mean)

    @pl.when(seg == 0)
    def _():
        keep_parcels(z, [ends_0.at[a] for a in range(RING)], half, half_mean)
        tail = lift[2 * states :, :].astype(F32)
        half_mean[...] = (dot_nt(half_mean[...], lift[:states, :]) + tail[0:1] + tail[1:2]).astype(BF16)

    def steps(rows_of, more):
        def one(k, carry):
            total = jnp.zeros((BLOCK, BLOCK), F32)
            for b in range(RING):
                blocks = (b + 2, b + 3, b) if b in (1, 2) else (b + 3, b)
                parts = [rows_of[k, :, (r % RING) * BLOCK : (r % RING + 1) * BLOCK] for r in blocks]
                value = dot(jnp.concatenate(parts, axis=1), half[b, (3 - len(blocks)) * BLOCK :, :])
                total = total + value * parts[-1].astype(F32)
            spread = row_sums(total) + var[pl.ds(k, 1), :]
            if more is not None:
                spread = spread + more[pl.ds(k, 1), :]
            means = dot_nt(half_mean[...], gain[k])[0:1] + offset[pl.ds(k, 1), :]
            out[0, pl.ds(k, 1), :] = means
            out[1, pl.ds(k, 1), :] = spread
            out_mean[pl.ds(k, 1), :] = means
            out_spread[pl.ds(k, 1), :] = spread
            return carry

        lax.fori_loop(0, gain.shape[0], one, 0, unroll=4)

    @pl.when(seg == 0)
    def _():
        steps(left, base)

    @pl.when(seg != 0)
    def _():
        steps(gain, None)


def last_kernel(where, g0, a1, a2, a3, ends_1, ends_0, lift, through, beside, noise, offset, means, rows, mean_row, product, full, mean):
    z, seg = where[0], where[1]
    states = g0.shape[1]
    mean_row[...] = (dot_nt(means[...], g0[...]) + offset[...]).astype(BF16)

    @pl.when(seg == 0)
    def _():
        lay_out(z, [ends_0.at[a] for a in range(RING)], full, mean)
        half_way = dot(through[...], full[...]).astype(BF16)
        product[...] = (dot_nt(half_way, lift[:states, :]) + beside[...]).astype(BF16)

    @pl.when(seg == 1)
    def _():
        lay_out(z, [ends_1.at[a] for a in range(RING)], full, mean)
        finish(z, dot(g0[...], full[...]).astype(BF16), (g0, a1, a2, a3), noise, rows)


def finish(z, product, gains, noise, rows):
    for a, gain in enumerate(gains):
        column = cols(spot(z, a))
        rows[:, column] = (dot_nt(product, gain[...]) + noise[:, column].astype(F32)).astype(BF16)


def innovation_kernel(where, tiles, counts, s0, s1, s2, s3, value, noise, own, far, near, mean_1, mean_2, mean_3, product, g0, b1, b2, b3, cov_noise, _, out, mean_row, rows_out, full, rows, sem):
    z, seg = where[0], where[1]
    copy = pltpu.make_async_copy(rows, rows_out, sem)

    @pl.when(seg == 0)
    def _():
        finish(z, product[...], (g0, b1, b2, b3), cov_noise, rows)
        copy.start()

    @pl.when(seg > 1)
    def _():
        rows[:, cols(z)] = own[:BLOCK, :BLOCK]
        rows[:, cols(spot(z, 1))] = own[:BLOCK, BLOCK : 2 * BLOCK]
        rows[:, cols(spot(z, 3))] = near[...].T

        @pl.when(owns_far(z))
        def _():
            rows[:, cols(spot(z, 2))] = own[:BLOCK, 2 * BLOCK :]

        @pl.when(jnp.logical_not(owns_far(z)))
        def _():
            rows[:, cols(spot(z, 2))] = far[...].T

        copy.start()

    mean = mean_1[0:1].astype(F32)
    for at, source in ((2, mean_2), (3, mean_3)):
        mean = jnp.where(seg == at, source[0:1].astype(F32), mean)
    mean_row[...] = mean.astype(BF16)
    for a, part in enumerate((s0, s1, s2, s3)):
        full[:, :, cols(spot(z, a))] = part[...]
    full[1] = full[1] + noise[...]
    for k in range(value.shape[0]):
        for j in range(SLOTS):
            at = pl.ds(pl.multiple_of(tiles[j, k] * TILE_STATES, TILE_STATES), TILE_STATES)
            result = (value[k, j : j + 1, :] - full[0, k : k + 1, at]) / full[1, k : k + 1, at]
            out[k, j : j + 1, :] = jnp.where(j < counts[k], result, 0.0)

    @pl.when(seg != 1)
    def _():
        copy.wait()


def smem():
    return pl.BlockSpec(memory_space=pltpu.SMEM)


def vmem():
    return pl.BlockSpec(memory_space=pltpu.VMEM)


def params():
    return pltpu.CompilerParams(vmem_limit_bytes=VMEM)


def cost(flops, moved):
    return pl.CostEstimate(flops=int(flops), bytes_accessed=int(moved), transcendentals=0)


def shape(dims, kind=BF16):
    return jax.ShapeDtypeStruct(dims, kind)


def ring_shards(groups, seg_gain, seg_offset, seg_noise, end_mean, end_cov, step_gain, step_offset, step_var, obs_tiles, obs_count, obs_value, obs_noise):
    position = lax.axis_index("tm")
    z = lax.axis_index("tile")
    where = jnp.stack([z, position % GROUP_SEGS, position // GROUP_SEGS]).astype(jnp.int32)
    gain, noise = seg_gain[0], seg_noise[0]
    states = gain.shape[1]
    steps = step_gain.shape[0]
    parcel_shape = shape((BLOCK + TAIL, 3 * BLOCK))

    def route(block, moves):
        table = []
        for g in range(groups):
            for (source, start), (target, end) in moves:
                table.append(((g * GROUP_SEGS + source) * RING + start, (g * GROUP_SEGS + target) * RING + end))
        return lax.ppermute(block, ("tm", "tile"), table)

    def send(block, pairs, shift):
        return route(block, [((a, (to + shift) % RING), (b, to)) for a, b in pairs for to in range(RING)])

    def exchange(block, pairs, own=None):
        others = [send(block, pairs, a) for a in (2, 1, 3)]
        return [send(block, pairs, 0) if own is None else own, others[1], others[0], others[2]]

    def within(segments, steps):
        return [((a, start), (a, to)) for a in segments for start, to in steps]

    def call(kernel, name, out_shape, operands, scratch, flops, aliases={}):
        moved = sum(x.size * x.dtype.itemsize for x in list(operands) + list(out_shape))
        return pl.pallas_call(
            kernel,
            out_shape=out_shape,
            in_specs=[smem()] + [vmem()] * len(operands),
            out_specs=(vmem(),) * len(out_shape),
            scratch_shapes=scratch,
            input_output_aliases=aliases,
            compiler_params=params(),
            cost_estimate=cost(flops, moved),
            name=name,
        )(where, *operands)

    def pack(kernel, name, out_shape, far_operands, near_operands, sems, limit):
        return pl.pallas_call(
            kernel,
            out_shape=out_shape,
            in_specs=[smem()] + [pl.BlockSpec(memory_space=pl.ANY)] * len(far_operands) + [vmem()] * len(near_operands),
            out_specs=jax.tree.map(lambda _: vmem(), out_shape),
            scratch_shapes=[sems],
            compiler_params=pltpu.CompilerParams(vmem_limit_bytes=limit),
            cost_estimate=cost(0, 1e6),
            name=name,
        )(where, *far_operands, *near_operands)

    full_and_mean = [pltpu.VMEM((states, states), BF16), pltpu.VMEM((TAIL, states), BF16)]
    row_shape, mean_shape, block_shape = shape((BLOCK, states)), shape((TAIL, BLOCK)), shape((BLOCK, BLOCK))
    half_shapes = (shape((RING, 3 * BLOCK, BLOCK)), shape((TAIL, states)))

    back, two_on, on = ((1, 0), (2, 1), (3, 2), (0, 3)), ((0, 2), (1, 3), (2, 0), (3, 1)), ((0, 1), (1, 2), (2, 3), (3, 0))
    pair_gains = [route(gain, within((3, 2, 1), back)), route(gain, within((3, 2), ((2, 0), (1, 3))) + within((1,), on))]
    parcel = pack(pack_kernel, "pack", parcel_shape, (end_cov, noise), (end_mean, seg_offset), pltpu.SemaphoreType.DMA((3,)), ALL_VMEM)
    first = [send(parcel, ((0 if a == 2 else 3, 3), (1, 1)), a) for a in range(1, RING)]

    def hand(segment, event):
        kernel = functools.partial(hand_kernel, segment)
        return pack(kernel, f"hand_{segment}", row_shape, (event, gain), (), pltpu.SemaphoreType.DMA, VMEM)

    gains_1 = [pair_gains[0], route(hand(1, first[1]), within((1,), two_on)), pair_gains[1]]

    flops = 4 * BLOCK * states * states
    *kept, parcel_3, mean_3 = call(
        functools.partial(pairs_kernel, 3),
        "pairs_3",
        (*half_shapes, parcel_shape, mean_shape),
        (gain, *pair_gains, noise, seg_offset, end_cov, end_mean, *first),
        full_and_mean + [pltpu.VMEM(parcel_shape.shape, BF16)],
        flops,
    )
    second = exchange(parcel_3, ((3, 2),))

    *kept, parcel_2, mean_2, beside_block, far_block = call(
        functools.partial(pairs_kernel, 2),
        "pairs_2",
        (*half_shapes, parcel_shape, mean_shape, block_shape, block_shape),
        (gain, *pair_gains, noise, seg_offset, *second, parcel_3, *kept),
        full_and_mean,
        flops,
        {11: 0, 12: 1},
    )
    own = send(parcel_2, ((2, 1),), 0)
    across = send(parcel_2, ((2, 1),), 2)
    sides = [
        route(parcel_2, [((2, start), (1, to)) for start, to in moves])
        for moves in (((1, 0), (2, 1), (3, 2), (0, 3)), ((0, 1), (1, 2), (2, 3)))
    ]
    third = [own, sides[0], across, sides[1], route(across, within((1,), ((1, 0),)))]
    (lift,) = call(stack_kernel, "stack", (shape((2 * states + TAIL, states)),), (parcel_2, gain, *gains_1, parcel, *first), [], 0)
    lift = send(lift, ((1, 0),), 0)
    gain_0 = hand(0, lift)
    left, base, through, beside, beside_block, far_block = call(
        ahead_kernel,
        "ahead",
        (shape(step_gain.shape), shape((steps, BLOCK), F32), row_shape, shape((BLOCK, states), F32), block_shape, block_shape),
        (gain_0, lift, gain, step_gain, beside_block, far_block),
        [],
        4 * (steps + 1) * BLOCK * states * states,
    )
    gains_0 = [route(gain_0, within((0,), moves)) for moves in (back, two_on, on)]
    near, far = route(beside_block, within((3, 2), on)), route(far_block, within((3, 2), ((0, 2), (3, 1))))
    (ends_1,) = call(turn_kernel, "turn", (shape((RING, *parcel_shape.shape)),), (near, far, *third), [], 0)
    ends_0 = send(ends_1, ((1, 0),), 0)
    out_steps = shape((steps, BLOCK), F32)
    _, means, step_mean, step_spread, stats = call(
        moments_kernel,
        "moments",
        (*half_shapes, out_steps, out_steps, shape((2, steps, BLOCK), F32)),
        (ends_1, ends_0, lift, left, base, step_gain, step_offset, step_var, *kept),
        [],
        2 * steps * BLOCK * states * states,
        {9: 0, 10: 1},
    )
    everyone = tuple((s, s) for s in range(GROUP_SEGS))
    all_stats = [stats] + [send(stats, everyone, a) for a in range(1, RING)]
    rows, mean_1, product = call(
        last_kernel,
        "last",
        (row_shape, mean_shape, row_shape),
        (gain, *gains_1, ends_1, ends_0, lift, through, beside, noise, seg_offset, means),
        full_and_mean,
        flops,
    )
    innovation, out_mean, out_cov = pl.pallas_call(
        innovation_kernel,
        out_shape=(shape(obs_value.shape, F32), shape((1, BLOCK)), row_shape),
        in_specs=[smem()] * 3 + [vmem()] * 18 + [pl.BlockSpec(memory_space=pl.ANY)],
        out_specs=(vmem(), vmem(), pl.BlockSpec(memory_space=pl.ANY)),
        scratch_shapes=[pltpu.VMEM((2, steps, states), F32), pltpu.VMEM(row_shape.shape, BF16), pltpu.SemaphoreType.DMA],
        input_output_aliases={21: 2},
        compiler_params=params(),
        cost_estimate=cost(0, 2e5),
        name="innovation",
    )(where, obs_tiles.T, obs_count, *all_stats, obs_value, obs_noise.reshape(1, states), parcel_2, far, near, mean_1, mean_2, mean_3, product, gain, *gains_0, noise, rows)
    return out_cov[None], out_mean, step_mean, step_spread, innovation


def solution(mesh):
    in_specs = (
        P("tm", "tile", None),
        P("tm", "tile"),
        P("tm", "tile", None),
        P(None, "tile"),
        P(None, "tile", None),
        P("tm", "tile", None),
        P("tm", "tile"),
        P("tm", "tile"),
        P("tm", None),
        P("tm"),
        P("tm", None, None),
        P(),
    )
    out_specs = (
        P("tm", "tile", None),
        P("tm", "tile"),
        P("tm", "tile"),
        P("tm", "tile"),
        P("tm", None, None),
    )
    if mesh.shape["tile"] == RING:
        shards = functools.partial(ring_shards, mesh.shape["tm"] // GROUP_SEGS)
    else:
        shards = general_shards
    return jax.shard_map(shards, mesh=mesh, in_specs=in_specs, out_specs=out_specs, check_vma=False)
```

```python
import functools
import jax
import jax.numpy as jnp
from jax import lax
from jax.experimental import pallas as pl
from jax.experimental.pallas import tpu as pltpu
from jax.sharding import PartitionSpec as P

TILE_STATES = 128
SLOTS = 4
GROUP_SEGS = 4


def shifted(block, axis, distance):
    devices = range(lax.axis_size(axis))
    route = [(i - distance, i) for i in devices if i - distance in devices]
    return lax.ppermute(block, axis, route)


def general_shards(
    seg_gain,
    seg_offset,
    seg_noise,
    end_mean,
    end_cov,
    step_gain,
    step_offset,
    step_var,
    obs_tiles,
    obs_count,
    obs_value,
    obs_noise,
):
    position = lax.axis_index("tm")
    slot_place = position % GROUP_SEGS
    group_index = position // GROUP_SEGS
    gain_rows = seg_gain[0]
    offset_rows = seg_offset[0]
    noise_rows = seg_noise[0].astype(jnp.float32)
    row_count = gain_rows.shape[0]
    state_count = gain_rows.shape[1]
    cur_mean = lax.dynamic_index_in_dim(end_mean, group_index, 0, keepdims=False)
    cur_cov = lax.dynamic_index_in_dim(end_cov, group_index, 0, keepdims=False)
    kept_mean = jnp.zeros((state_count,), jnp.bfloat16)
    kept_cov = jnp.zeros((state_count, state_count), jnp.bfloat16)
    out_mean = jnp.zeros((row_count,), jnp.bfloat16)
    out_cov = jnp.zeros((row_count, state_count), jnp.bfloat16)
    for depth_step in range(GROUP_SEGS):
        whole_mean, whole_cov = (
            lax.all_gather(cur_mean, "tile", axis=0, tiled=True),
            lax.all_gather(cur_cov, "tile", axis=0, tiled=True),
        )
        is_mine = slot_place == GROUP_SEGS - 1 - depth_step
        kept_mean = jnp.where(is_mine, whole_mean, kept_mean)
        kept_cov = jnp.where(is_mine, whole_cov, kept_cov)
        product = jnp.dot(gain_rows, whole_cov, preferred_element_type=jnp.float32).astype(
            jnp.bfloat16
        )
        col_block = jnp.einsum(
            "pd,rd->pr",
            lax.all_gather(product, "tile", axis=0, tiled=True),
            gain_rows,
            preferred_element_type=jnp.float32,
        )
        spread_rows = lax.all_to_all(col_block, "tile", split_axis=0, concat_axis=1, tiled=True)
        new_cov = (spread_rows + noise_rows).astype(jnp.bfloat16)
        new_mean = (
            jnp.dot(gain_rows, whole_mean, preferred_element_type=jnp.float32) + offset_rows
        ).astype(jnp.bfloat16)
        out_mean = jnp.where(is_mine, new_mean, out_mean)
        out_cov = jnp.where(is_mine, new_cov, out_cov)
        if depth_step < GROUP_SEGS - 1:
            got_mean, got_cov = shifted((new_mean, new_cov), "tm", -1)
            takes_next = slot_place == GROUP_SEGS - 2 - depth_step
            cur_mean = jnp.where(takes_next, got_mean, cur_mean)
            cur_cov = jnp.where(takes_next, got_cov, cur_cov)
    partial_value = jnp.einsum(
        "krd,de->kre", step_gain, kept_cov, preferred_element_type=jnp.float32
    )
    local_spread = jnp.sum(partial_value * step_gain, axis=2) + step_var
    local_mean = (
        jnp.einsum("krd,d->kr", step_gain, kept_mean, preferred_element_type=jnp.float32)
        + step_offset
    )
    full_mean, full_spread = (
        lax.all_gather(local_mean, "tile", axis=1, tiled=True),
        lax.all_gather(local_spread, "tile", axis=1, tiled=True),
    )
    step_count = full_mean.shape[0]
    tile_total = state_count // TILE_STATES
    tile_mean = full_mean.reshape(step_count, tile_total, TILE_STATES)
    tile_spread = full_spread.reshape(step_count, tile_total, TILE_STATES) + obs_noise.reshape(
        1, tile_total, TILE_STATES
    )
    onehot = (
        obs_tiles[:, :, None] == jnp.arange(tile_total, dtype=jnp.int32)[None, None, :]
    ).astype(jnp.float32)
    picked_mean = jnp.einsum("ksn,kno->kso", onehot, tile_mean, precision=lax.Precision.HIGHEST)
    picked_spread = jnp.einsum("ksn,kno->kso", onehot, tile_spread, precision=lax.Precision.HIGHEST)
    live_slots = jnp.arange(SLOTS, dtype=jnp.int32)[None, :] < obs_count[:, None]
    innovation = jnp.where(
        live_slots[:, :, None], (obs_value - picked_mean) / picked_spread, jnp.float32(0.0)
    )
    return (out_cov[None], out_mean[None], local_mean, local_spread, innovation)


BLOCK = 256
RING = 4
TAIL = 16
VMEM = 12 * 1024 * 1024
ALL_VMEM = 56 * 1024 * 1024
NT = (((1,), (1,)), ((), ()))
F32 = jnp.float32
BF16 = jnp.bfloat16


def cols(index):
    return pl.ds(pl.multiple_of(index * BLOCK, BLOCK), BLOCK)


def spot(z, shift):
    return lax.rem(z + shift, RING)


def dot(a, b):
    return jnp.dot(a, b, preferred_element_type=F32)


def dot_nt(a, b):
    return lax.dot_general(a, b, NT, preferred_element_type=F32)


def owns_far(row):
    return (row == 0) | (row == RING - 1)


def each_parcel(parcels, body):
    for a, entry in enumerate(parcels):
        if isinstance(entry, tuple):
            condition, one, other = entry
            pl.when(condition)(functools.partial(body, a, one))
            pl.when(jnp.logical_not(condition))(functools.partial(body, a, other))
        else:
            body(a, entry)


def by_relay(z, own, after, across, before, handed):
    return own, after, across, (z > 0, before, handed)


def lay_out(z, parcels, full, mean):
    def body(a, parcel):
        at = spot(z, a)
        row, near, far = cols(at), cols(spot(z, a + 1)), cols(spot(z, a + 2))
        full[row, row] = parcel[:BLOCK, :BLOCK]
        beside = parcel[:BLOCK, BLOCK : 2 * BLOCK]
        full[row, near] = beside
        full[near, row] = beside.T
        mean[:, row] = parcel[BLOCK:, :BLOCK]

        @pl.when(owns_far(at))
        def _():
            block = parcel[:BLOCK, 2 * BLOCK :]
            full[row, far] = block
            full[far, row] = block.T

    each_parcel(parcels, body)


def keep_parcels(z, parcels, half, half_mean):
    def body(a, parcel):
        at = spot(z, a)
        half_mean[:, cols(at)] = parcel[BLOCK:, :BLOCK]
        half[at, 2 * BLOCK :, :] = parcel[:BLOCK, :BLOCK]
        half[spot(z, a + 1), BLOCK : 2 * BLOCK, :] = parcel[:BLOCK, BLOCK : 2 * BLOCK] * 2

        @pl.when(owns_far(at))
        def _():
            half[spot(z, a + 2), :BLOCK, :] = parcel[:BLOCK, 2 * BLOCK :] * 2

    each_parcel(parcels, body)


def keep_whole(full, mean, half, half_mean):
    half_mean[...] = mean[...]
    for b in range(RING):
        column = slice(b * BLOCK, (b + 1) * BLOCK)
        for j in range(3):
            if j < 2 or b in (1, 2):
                row = (b - j) % RING * BLOCK
                block = full[row : row + BLOCK, column]
                half[b, (2 - j) * BLOCK : (3 - j) * BLOCK, :] = block * 2 if j else block


def fetch(source, z, tail, parcel, sems):
    copies = []
    for j in range(3):
        target = parcel.at[pl.ds(0, BLOCK), pl.ds(j * BLOCK, BLOCK)]
        copies.append(pltpu.make_async_copy(source.at[:, cols(spot(z, j))], target, sems.at[j]))
    for copy in copies:
        copy.start()
    parcel[BLOCK:, :] = jnp.zeros((TAIL, 3 * BLOCK), BF16)
    parcel[BLOCK:, :BLOCK] = tail.astype(BF16)
    for copy in copies:
        copy.wait()


def group_mean(group, end_mean):
    mean = jnp.zeros((1, BLOCK), F32)
    for g in range(end_mean.shape[0]):
        mean = jnp.where(group == g, end_mean[g : g + 1, :].astype(F32), mean)
    return jnp.broadcast_to(mean, (TAIL, BLOCK))


def pack_kernel(where, end_cov, noise, end_mean, offset, parcel, sems):
    z, seg, group = where[0], where[1], where[2]

    @pl.when(seg == 1)
    def _():
        high = offset[...].astype(BF16).astype(F32)
        first = lax.broadcasted_iota(jnp.int32, (TAIL, BLOCK), 0) == 0
        fetch(noise, z, jnp.where(first, high, offset[...] - high), parcel, sems)

    @pl.when(seg != 1)
    def _():
        fetch(end_cov.at[group], z, group_mean(group, end_mean), parcel, sems)


def pairs_kernel(at_seg, where, g0, g1, g2, noise, offset, *refs):
    z, seg, group = where[0], where[1], where[2]
    if at_seg == GROUP_SEGS - 1:
        end_cov, end_mean, *others, half, half_mean, parcel, mean_row, full, mean, own = refs
        parcels = (own, *others)
    else:
        *parcels, early, _, _, half, half_mean, parcel, mean_row, beside, far, full, mean = refs

    @pl.when(seg == at_seg)
    def _():
        if at_seg == GROUP_SEGS - 1:
            for j in range(3):
                own[:BLOCK, j * BLOCK : (j + 1) * BLOCK] = end_cov[group, :, cols(spot(z, j))]
            own[BLOCK:, :BLOCK] = group_mean(group, end_mean).astype(BF16)
        lay_out(z, parcels, full, mean)
        product = dot(g0[...], full[...]).astype(BF16)
        for j, gain in enumerate((g0, g1, g2)):
            block = dot_nt(product, gain[...]) + noise[:, cols(spot(z, j))].astype(F32)
            parcel[:BLOCK, j * BLOCK : (j + 1) * BLOCK] = block.astype(BF16)
        new_mean = (dot_nt(mean[...], g0[...]) + offset[...]).astype(BF16)
        parcel[BLOCK:, :BLOCK] = new_mean
        parcel[BLOCK:, BLOCK:] = jnp.zeros((TAIL, 2 * BLOCK), BF16)
        mean_row[...] = new_mean
        keep_whole(full, mean, half, half_mean)

    if at_seg < GROUP_SEGS - 1:
        @pl.when(seg == GROUP_SEGS - 1)
        def _():
            parcel[...] = early[...]

        beside[...] = parcel[:BLOCK, BLOCK : 2 * BLOCK]
        far[...] = parcel[:BLOCK, 2 * BLOCK :]


def hand_kernel(at_seg, where, event, gain, out, sem):
    @pl.when(where[1] == at_seg)
    def _():
        copy = pltpu.make_async_copy(gain, out, sem)
        copy.start()
        copy.wait()


def stack_kernel(where, event, g0, g1, g2, g3, n0, n1, n2, n3, lift):
    z, seg = where[0], where[1]
    states = g0.shape[1]

    @pl.when(seg == 1)
    def _():
        for a, gain in enumerate((g0, g1, g2, g3)):
            lift[cols(spot(z, a)), :] = gain[...]
        lay_out(z, (n0, n1, n2, n3), lift.at[pl.ds(states, states)], lift.at[pl.ds(2 * states, TAIL)])


def turn_kernel(where, near, far, b2, t0, t1, t2, t3, t4, out):
    def body(a, parcel):
        out[a] = parcel[...]

    @pl.when(where[1] == 1)
    def _():
        each_parcel(by_relay(where[0], t0, t1, t2, t3, t4), body)


def ahead_kernel(where, event, lift, gain, step_gain, block_1, block_2, left, base, through, beside, block_1_on, block_2_on):
    seg = where[1]
    states = gain.shape[1]

    @pl.when(seg > 1)
    def _():
        block_1_on[...] = block_1[...]
        block_2_on[...] = block_2[...]

    @pl.when(seg == 0)
    def _():
        through[...] = dot(gain[...], lift[:states, :]).astype(BF16)
        beside[...] = dot(gain[...], lift[states : 2 * states, :])

        def one(k, carry):
            rows = step_gain[k]
            left[k] = dot(rows, lift[:states, :]).astype(BF16)
            value = dot(rows, lift[states : 2 * states, :]) * rows.astype(F32)
            base[pl.ds(k, 1), :] = row_sums(value)
            return carry

        lax.fori_loop(0, step_gain.shape[0], one, 0, unroll=4)


def row_sums(value):
    total = value[:, :128]
    for at in range(128, value.shape[1], 128):
        total = total + value[:, at : at + 128]
    return jnp.sum(total.T, axis=0, keepdims=True)


def moments_kernel(where, ends_1, ends_0, lift, left, base, gain, offset, var, kept, kept_mean, half, half_mean, out_mean, out_spread, out):
    z, seg = where[0], where[1]
    states = gain.shape[2]

    @pl.when(seg == 1)
    def _():
        keep_parcels(z, [ends_1.at[a] for a in range(RING)], half, half_mean)

    @pl.when(seg == 0)
    def _():
        keep_parcels(z, [ends_0.at[a] for a in range(RING)], half, half_mean)
        tail = lift[2 * states :, :].astype(F32)
        half_mean[...] = (dot_nt(half_mean[...], lift[:states, :]) + tail[0:1] + tail[1:2]).astype(BF16)

    def steps(rows_of, more):
        def one(k, carry):
            total = jnp.zeros((BLOCK, BLOCK), F32)
            for b in range(RING):
                blocks = (b + 2, b + 3, b) if b in (1, 2) else (b + 3, b)
                parts = [rows_of[k, :, (r % RING) * BLOCK : (r % RING + 1) * BLOCK] for r in blocks]
                value = dot(jnp.concatenate(parts, axis=1), half[b, (3 - len(blocks)) * BLOCK :, :])
                total = total + value * parts[-1].astype(F32)
            spread = row_sums(total) + var[pl.ds(k, 1), :]
            if more is not None:
                spread = spread + more[pl.ds(k, 1), :]
            means = dot_nt(half_mean[...], gain[k])[0:1] + offset[pl.ds(k, 1), :]
            out[0, pl.ds(k, 1), :] = means
            out[1, pl.ds(k, 1), :] = spread
            out_mean[pl.ds(k, 1), :] = means
            out_spread[pl.ds(k, 1), :] = spread
            return carry

        lax.fori_loop(0, gain.shape[0], one, 0, unroll=4)

    @pl.when(seg == 0)
    def _():
        steps(left, base)

    @pl.when(seg != 0)
    def _():
        steps(gain, None)


def last_kernel(where, g0, a1, a2, a3, ends_1, ends_0, lift, through, beside, noise, offset, means, rows, mean_row, product, full, mean):
    z, seg = where[0], where[1]
    states = g0.shape[1]
    mean_row[...] = (dot_nt(means[...], g0[...]) + offset[...]).astype(BF16)

    @pl.when(seg == 0)
    def _():
        lay_out(z, [ends_0.at[a] for a in range(RING)], full, mean)
        half_way = dot(through[...], full[...]).astype(BF16)
        product[...] = (dot_nt(half_way, lift[:states, :]) + beside[...]).astype(BF16)

    @pl.when(seg == 1)
    def _():
        lay_out(z, [ends_1.at[a] for a in range(RING)], full, mean)
        finish(z, dot(g0[...], full[...]).astype(BF16), (g0, a1, a2, a3), noise, rows)


def finish(z, product, gains, noise, rows):
    for a, gain in enumerate(gains):
        column = cols(spot(z, a))
        rows[:, column] = (dot_nt(product, gain[...]) + noise[:, column].astype(F32)).astype(BF16)


def innovation_kernel(where, tiles, counts, s0, s1, s2, s3, value, noise, own, far, near, mean_1, mean_2, mean_3, product, g0, b1, b2, b3, cov_noise, _, out, mean_row, rows_out, full, rows, sem):
    z, seg = where[0], where[1]
    copy = pltpu.make_async_copy(rows, rows_out, sem)

    @pl.when(seg == 0)
    def _():
        finish(z, product[...], (g0, b1, b2, b3), cov_noise, rows)
        copy.start()

    @pl.when(seg > 1)
    def _():
        rows[:, cols(z)] = own[:BLOCK, :BLOCK]
        rows[:, cols(spot(z, 1))] = own[:BLOCK, BLOCK : 2 * BLOCK]
        rows[:, cols(spot(z, 3))] = near[...].T

        @pl.when(owns_far(z))
        def _():
            rows[:, cols(spot(z, 2))] = own[:BLOCK, 2 * BLOCK :]

        @pl.when(jnp.logical_not(owns_far(z)))
        def _():
            rows[:, cols(spot(z, 2))] = far[...].T

        copy.start()

    mean = mean_1[0:1].astype(F32)
    for at, source in ((2, mean_2), (3, mean_3)):
        mean = jnp.where(seg == at, source[0:1].astype(F32), mean)
    mean_row[...] = mean.astype(BF16)
    for a, part in enumerate((s0, s1, s2, s3)):
        full[:, :, cols(spot(z, a))] = part[...]
    full[1] = full[1] + noise[...]
    for k in range(value.shape[0]):
        for j in range(SLOTS):
            at = pl.ds(pl.multiple_of(tiles[j, k] * TILE_STATES, TILE_STATES), TILE_STATES)
            result = (value[k, j : j + 1, :] - full[0, k : k + 1, at]) / full[1, k : k + 1, at]
            out[k, j : j + 1, :] = jnp.where(j < counts[k], result, 0.0)

    @pl.when(seg != 1)
    def _():
        copy.wait()


def smem():
    return pl.BlockSpec(memory_space=pltpu.SMEM)


def vmem():
    return pl.BlockSpec(memory_space=pltpu.VMEM)


def params():
    return pltpu.CompilerParams(vmem_limit_bytes=VMEM)


def cost(flops, moved):
    return pl.CostEstimate(flops=int(flops), bytes_accessed=int(moved), transcendentals=0)


def shape(dims, kind=BF16):
    return jax.ShapeDtypeStruct(dims, kind)


def ring_shards(groups, seg_gain, seg_offset, seg_noise, end_mean, end_cov, step_gain, step_offset, step_var, obs_tiles, obs_count, obs_value, obs_noise):
    position = lax.axis_index("tm")
    z = lax.axis_index("tile")
    where = jnp.stack([z, position % GROUP_SEGS, position // GROUP_SEGS]).astype(jnp.int32)
    gain, noise = seg_gain[0], seg_noise[0]
    states = gain.shape[1]
    steps = step_gain.shape[0]
    parcel_shape = shape((BLOCK + TAIL, 3 * BLOCK))

    def route(block, moves):
        table = []
        for g in range(groups):
            for (source, start), (target, end) in moves:
                table.append(((g * GROUP_SEGS + source) * RING + start, (g * GROUP_SEGS + target) * RING + end))
        return lax.ppermute(block, ("tm", "tile"), table)

    def send(block, pairs, shift):
        return route(block, [((a, (to + shift) % RING), (b, to)) for a, b in pairs for to in range(RING)])

    def exchange(block, pairs, own=None):
        others = [send(block, pairs, a) for a in (2, 1, 3)]
        return [send(block, pairs, 0) if own is None else own, others[1], others[0], others[2]]

    def within(segments, steps):
        return [((a, start), (a, to)) for a in segments for start, to in steps]

    def call(kernel, name, out_shape, operands, scratch, flops, aliases={}):
        moved = sum(x.size * x.dtype.itemsize for x in list(operands) + list(out_shape))
        return pl.pallas_call(
            kernel,
            out_shape=out_shape,
            in_specs=[smem()] + [vmem()] * len(operands),
            out_specs=(vmem(),) * len(out_shape),
            scratch_shapes=scratch,
            input_output_aliases=aliases,
            compiler_params=params(),
            cost_estimate=cost(flops, moved),
            name=name,
        )(where, *operands)

    def pack(kernel, name, out_shape, far_operands, near_operands, sems, limit):
        return pl.pallas_call(
            kernel,
            out_shape=out_shape,
            in_specs=[smem()] + [pl.BlockSpec(memory_space=pl.ANY)] * len(far_operands) + [vmem()] * len(near_operands),
            out_specs=jax.tree.map(lambda _: vmem(), out_shape),
            scratch_shapes=[sems],
            compiler_params=pltpu.CompilerParams(vmem_limit_bytes=limit),
            cost_estimate=cost(0, 1e6),
            name=name,
        )(where, *far_operands, *near_operands)

    full_and_mean = [pltpu.VMEM((states, states), BF16), pltpu.VMEM((TAIL, states), BF16)]
    row_shape, mean_shape, block_shape = shape((BLOCK, states)), shape((TAIL, BLOCK)), shape((BLOCK, BLOCK))
    half_shapes = (shape((RING, 3 * BLOCK, BLOCK)), shape((TAIL, states)))

    back, two_on, on = ((1, 0), (2, 1), (3, 2), (0, 3)), ((0, 2), (1, 3), (2, 0), (3, 1)), ((0, 1), (1, 2), (2, 3), (3, 0))
    pair_gains = [route(gain, within((3, 2, 1), back)), route(gain, within((3, 2), ((2, 0), (1, 3))) + within((1,), on))]
    parcel = pack(pack_kernel, "pack", parcel_shape, (end_cov, noise), (end_mean, seg_offset), pltpu.SemaphoreType.DMA((3,)), ALL_VMEM)
    first = [send(parcel, ((0 if a == 2 else 3, 3), (1, 1)), a) for a in range(1, RING)]

    def hand(segment, event):
        kernel = functools.partial(hand_kernel, segment)
        return pack(kernel, f"hand_{segment}", row_shape, (event, gain), (), pltpu.SemaphoreType.DMA, VMEM)

    gains_1 = [pair_gains[0], route(hand(1, first[1]), within((1,), two_on)), pair_gains[1]]

    flops = 4 * BLOCK * states * states
    *kept, parcel_3, mean_3 = call(
        functools.partial(pairs_kernel, 3),
        "pairs_3",
        (*half_shapes, parcel_shape, mean_shape),
        (gain, *pair_gains, noise, seg_offset, end_cov, end_mean, *first),
        full_and_mean + [pltpu.VMEM(parcel_shape.shape, BF16)],
        flops,
    )
    second = exchange(parcel_3, ((3, 2),))

    *kept, parcel_2, mean_2, beside_block, far_block = call(
        functools.partial(pairs_kernel, 2),
        "pairs_2",
        (*half_shapes, parcel_shape, mean_shape, block_shape, block_shape),
        (gain, *pair_gains, noise, seg_offset, *second, parcel_3, *kept),
        full_and_mean,
        flops,
        {11: 0, 12: 1},
    )
    own = send(parcel_2, ((2, 1),), 0)
    across = send(parcel_2, ((2, 1),), 2)
    sides = [
        route(parcel_2, [((2, start), (1, to)) for start, to in moves])
        for moves in (((1, 0), (2, 1), (3, 2), (0, 3)), ((0, 1), (1, 2), (2, 3)))
    ]
    third = [own, sides[0], across, sides[1], route(across, within((1,), ((1, 0),)))]
    (lift,) = call(stack_kernel, "stack", (shape((2 * states + TAIL, states)),), (parcel_2, gain, *gains_1, parcel, *first), [], 0)
    lift = send(lift, ((1, 0),), 0)
    gain_0 = hand(0, lift)
    left, base, through, beside, beside_block, far_block = call(
        ahead_kernel,
        "ahead",
        (shape(step_gain.shape), shape((steps, BLOCK), F32), row_shape, shape((BLOCK, states), F32), block_shape, block_shape),
        (gain_0, lift, gain, step_gain, beside_block, far_block),
        [],
        4 * (steps + 1) * BLOCK * states * states,
    )
    gains_0 = [route(gain_0, within((0,), moves)) for moves in (back, two_on, on)]
    near, far = route(beside_block, within((3, 2), on)), route(far_block, within((3, 2), ((0, 2), (3, 1))))
    (ends_1,) = call(turn_kernel, "turn", (shape((RING, *parcel_shape.shape)),), (near, far, gains_0[1], *third), [], 0)
    ends_0 = send(ends_1, ((1, 0),), 0)
    out_steps = shape((steps, BLOCK), F32)
    _, means, step_mean, step_spread, stats = call(
        moments_kernel,
        "moments",
        (*half_shapes, out_steps, out_steps, shape((2, steps, BLOCK), F32)),
        (ends_1, ends_0, lift, left, base, step_gain, step_offset, step_var, *kept),
        [],
        2 * steps * BLOCK * states * states,
        {9: 0, 10: 1},
    )
    everyone = tuple((s, s) for s in range(GROUP_SEGS))
    all_stats = [stats] + [send(stats, everyone, a) for a in range(1, RING)]
    rows, mean_1, product = call(
        last_kernel,
        "last",
        (row_shape, mean_shape, row_shape),
        (gain, *gains_1, ends_1, ends_0, lift, through, beside, noise, seg_offset, means),
        full_and_mean,
        flops,
    )
    innovation, out_mean, out_cov = pl.pallas_call(
        innovation_kernel,
        out_shape=(shape(obs_value.shape, F32), shape((1, BLOCK)), row_shape),
        in_specs=[smem()] * 3 + [vmem()] * 18 + [pl.BlockSpec(memory_space=pl.ANY)],
        out_specs=(vmem(), vmem(), pl.BlockSpec(memory_space=pl.ANY)),
        scratch_shapes=[pltpu.VMEM((2, steps, states), F32), pltpu.VMEM(row_shape.shape, BF16), pltpu.SemaphoreType.DMA],
        input_output_aliases={21: 2},
        compiler_params=params(),
        cost_estimate=cost(0, 2e5),
        name="innovation",
    )(where, obs_tiles.T, obs_count, *all_stats, obs_value, obs_noise.reshape(1, states), parcel_2, far, near, mean_1, mean_2, mean_3, product, gain, *gains_0, noise, rows)
    return out_cov[None], out_mean, step_mean, step_spread, innovation


def solution(mesh):
    in_specs = (
        P("tm", "tile", None),
        P("tm", "tile"),
        P("tm", "tile", None),
        P(None, "tile"),
        P(None, "tile", None),
        P("tm", "tile", None),
        P("tm", "tile"),
        P("tm", "tile"),
        P("tm", None),
        P("tm"),
        P("tm", None, None),
        P(),
    )
    out_specs = (
        P("tm", "tile", None),
        P("tm", "tile"),
        P("tm", "tile"),
        P("tm", "tile"),
        P("tm", None, None),
    )
    if mesh.shape["tile"] == RING:
        shards = functools.partial(ring_shards, mesh.shape["tm"] // GROUP_SEGS)
    else:
        shards = general_shards
    return jax.shard_map(shards, mesh=mesh, in_specs=in_specs, out_specs=out_specs, check_vma=False)
```

```python
import functools
import jax
import jax.numpy as jnp
from jax import lax
from jax.experimental import pallas as pl
from jax.experimental.pallas import tpu as pltpu
from jax.sharding import PartitionSpec as P

TILE_STATES = 128
SLOTS = 4
GROUP_SEGS = 4


def shifted(block, axis, distance):
    devices = range(lax.axis_size(axis))
    route = [(i - distance, i) for i in devices if i - distance in devices]
    return lax.ppermute(block, axis, route)


def general_shards(
    seg_gain,
    seg_offset,
    seg_noise,
    end_mean,
    end_cov,
    step_gain,
    step_offset,
    step_var,
    obs_tiles,
    obs_count,
    obs_value,
    obs_noise,
):
    position = lax.axis_index("tm")
    slot_place = position % GROUP_SEGS
    group_index = position // GROUP_SEGS
    gain_rows = seg_gain[0]
    offset_rows = seg_offset[0]
    noise_rows = seg_noise[0].astype(jnp.float32)
    row_count = gain_rows.shape[0]
    state_count = gain_rows.shape[1]
    cur_mean = lax.dynamic_index_in_dim(end_mean, group_index, 0, keepdims=False)
    cur_cov = lax.dynamic_index_in_dim(end_cov, group_index, 0, keepdims=False)
    kept_mean = jnp.zeros((state_count,), jnp.bfloat16)
    kept_cov = jnp.zeros((state_count, state_count), jnp.bfloat16)
    out_mean = jnp.zeros((row_count,), jnp.bfloat16)
    out_cov = jnp.zeros((row_count, state_count), jnp.bfloat16)
    for depth_step in range(GROUP_SEGS):
        whole_mean, whole_cov = (
            lax.all_gather(cur_mean, "tile", axis=0, tiled=True),
            lax.all_gather(cur_cov, "tile", axis=0, tiled=True),
        )
        is_mine = slot_place == GROUP_SEGS - 1 - depth_step
        kept_mean = jnp.where(is_mine, whole_mean, kept_mean)
        kept_cov = jnp.where(is_mine, whole_cov, kept_cov)
        product = jnp.dot(gain_rows, whole_cov, preferred_element_type=jnp.float32).astype(
            jnp.bfloat16
        )
        col_block = jnp.einsum(
            "pd,rd->pr",
            lax.all_gather(product, "tile", axis=0, tiled=True),
            gain_rows,
            preferred_element_type=jnp.float32,
        )
        spread_rows = lax.all_to_all(col_block, "tile", split_axis=0, concat_axis=1, tiled=True)
        new_cov = (spread_rows + noise_rows).astype(jnp.bfloat16)
        new_mean = (
            jnp.dot(gain_rows, whole_mean, preferred_element_type=jnp.float32) + offset_rows
        ).astype(jnp.bfloat16)
        out_mean = jnp.where(is_mine, new_mean, out_mean)
        out_cov = jnp.where(is_mine, new_cov, out_cov)
        if depth_step < GROUP_SEGS - 1:
            got_mean, got_cov = shifted((new_mean, new_cov), "tm", -1)
            takes_next = slot_place == GROUP_SEGS - 2 - depth_step
            cur_mean = jnp.where(takes_next, got_mean, cur_mean)
            cur_cov = jnp.where(takes_next, got_cov, cur_cov)
    partial_value = jnp.einsum(
        "krd,de->kre", step_gain, kept_cov, preferred_element_type=jnp.float32
    )
    local_spread = jnp.sum(partial_value * step_gain, axis=2) + step_var
    local_mean = (
        jnp.einsum("krd,d->kr", step_gain, kept_mean, preferred_element_type=jnp.float32)
        + step_offset
    )
    full_mean, full_spread = (
        lax.all_gather(local_mean, "tile", axis=1, tiled=True),
        lax.all_gather(local_spread, "tile", axis=1, tiled=True),
    )
    step_count = full_mean.shape[0]
    tile_total = state_count // TILE_STATES
    tile_mean = full_mean.reshape(step_count, tile_total, TILE_STATES)
    tile_spread = full_spread.reshape(step_count, tile_total, TILE_STATES) + obs_noise.reshape(
        1, tile_total, TILE_STATES
    )
    onehot = (
        obs_tiles[:, :, None] == jnp.arange(tile_total, dtype=jnp.int32)[None, None, :]
    ).astype(jnp.float32)
    picked_mean = jnp.einsum("ksn,kno->kso", onehot, tile_mean, precision=lax.Precision.HIGHEST)
    picked_spread = jnp.einsum("ksn,kno->kso", onehot, tile_spread, precision=lax.Precision.HIGHEST)
    live_slots = jnp.arange(SLOTS, dtype=jnp.int32)[None, :] < obs_count[:, None]
    innovation = jnp.where(
        live_slots[:, :, None], (obs_value - picked_mean) / picked_spread, jnp.float32(0.0)
    )
    return (out_cov[None], out_mean[None], local_mean, local_spread, innovation)


BLOCK = 256
RING = 4
TAIL = 16
VMEM = 12 * 1024 * 1024
ALL_VMEM = 56 * 1024 * 1024
NT = (((1,), (1,)), ((), ()))
F32 = jnp.float32
BF16 = jnp.bfloat16


def cols(index):
    return pl.ds(pl.multiple_of(index * BLOCK, BLOCK), BLOCK)


def spot(z, shift):
    return lax.rem(z + shift, RING)


def dot(a, b):
    return jnp.dot(a, b, preferred_element_type=F32)


def dot_nt(a, b):
    return lax.dot_general(a, b, NT, preferred_element_type=F32)


def owns_far(row):
    return (row == 0) | (row == RING - 1)


def each_parcel(parcels, body):
    for a, entry in enumerate(parcels):
        if isinstance(entry, tuple):
            condition, one, other = entry
            pl.when(condition)(functools.partial(body, a, one))
            pl.when(jnp.logical_not(condition))(functools.partial(body, a, other))
        else:
            body(a, entry)


def by_relay(z, own, after, across, before, handed):
    return own, after, across, (z > 0, before, handed)


def lay_out(z, parcels, full, mean):
    def body(a, parcel):
        at = spot(z, a)
        row, near, far = cols(at), cols(spot(z, a + 1)), cols(spot(z, a + 2))
        full[row, row] = parcel[:BLOCK, :BLOCK]
        beside = parcel[:BLOCK, BLOCK : 2 * BLOCK]
        full[row, near] = beside
        full[near, row] = beside.T
        mean[:, row] = parcel[BLOCK:, :BLOCK]

        @pl.when(owns_far(at))
        def _():
            block = parcel[:BLOCK, 2 * BLOCK :]
            full[row, far] = block
            full[far, row] = block.T

    each_parcel(parcels, body)


def keep_parcels(z, parcels, half, half_mean):
    def body(a, parcel):
        at = spot(z, a)
        half_mean[:, cols(at)] = parcel[BLOCK:, :BLOCK]
        half[at, 2 * BLOCK :, :] = parcel[:BLOCK, :BLOCK]
        half[spot(z, a + 1), BLOCK : 2 * BLOCK, :] = parcel[:BLOCK, BLOCK : 2 * BLOCK] * 2

        @pl.when(owns_far(at))
        def _():
            half[spot(z, a + 2), :BLOCK, :] = parcel[:BLOCK, 2 * BLOCK :] * 2

    each_parcel(parcels, body)


def keep_whole(full, mean, half, half_mean):
    half_mean[...] = mean[...]
    for b in range(RING):
        column = slice(b * BLOCK, (b + 1) * BLOCK)
        for j in range(3):
            if j < 2 or b in (1, 2):
                row = (b - j) % RING * BLOCK
                block = full[row : row + BLOCK, column]
                half[b, (2 - j) * BLOCK : (3 - j) * BLOCK, :] = block * 2 if j else block


def fetch(source, z, tail, parcel, sems):
    copies = []
    for j in range(3):
        target = parcel.at[pl.ds(0, BLOCK), pl.ds(j * BLOCK, BLOCK)]
        copies.append(pltpu.make_async_copy(source.at[:, cols(spot(z, j))], target, sems.at[j]))
    for copy in copies:
        copy.start()
    parcel[BLOCK:, :] = jnp.zeros((TAIL, 3 * BLOCK), BF16)
    parcel[BLOCK:, :BLOCK] = tail.astype(BF16)
    for copy in copies:
        copy.wait()


def group_mean(group, end_mean):
    mean = jnp.zeros((1, BLOCK), F32)
    for g in range(end_mean.shape[0]):
        mean = jnp.where(group == g, end_mean[g : g + 1, :].astype(F32), mean)
    return jnp.broadcast_to(mean, (TAIL, BLOCK))


def pack_kernel(where, end_cov, noise, end_mean, offset, parcel, sems):
    z, seg, group = where[0], where[1], where[2]

    @pl.when(seg == 1)
    def _():
        high = offset[...].astype(BF16).astype(F32)
        first = lax.broadcasted_iota(jnp.int32, (TAIL, BLOCK), 0) == 0
        fetch(noise, z, jnp.where(first, high, offset[...] - high), parcel, sems)

    @pl.when(seg != 1)
    def _():
        fetch(end_cov.at[group], z, group_mean(group, end_mean), parcel, sems)


def pairs_kernel(at_seg, where, g0, g1, g2, noise, offset, *refs):
    z, seg, group = where[0], where[1], where[2]
    if at_seg == GROUP_SEGS - 1:
        end_cov, end_mean, p1, p2, p3, from_1, across, half, half_mean, parcel, mean_row, full, mean, own = refs
        parcels = (own, (z < RING - 1, p1, across), (z > 0, p2, from_1), (z > 0, p3, across))
    else:
        *parcels, early, _, _, half, half_mean, parcel, mean_row, beside, far, full, mean = refs

    @pl.when(seg == at_seg)
    def _():
        if at_seg == GROUP_SEGS - 1:
            for j in range(3):
                own[:BLOCK, j * BLOCK : (j + 1) * BLOCK] = end_cov[group, :, cols(spot(z, j))]
            own[BLOCK:, :BLOCK] = group_mean(group, end_mean).astype(BF16)
        lay_out(z, parcels, full, mean)
        product = dot(g0[...], full[...]).astype(BF16)
        for j, gain in enumerate((g0, g1, g2)):
            block = dot_nt(product, gain[...]) + noise[:, cols(spot(z, j))].astype(F32)
            parcel[:BLOCK, j * BLOCK : (j + 1) * BLOCK] = block.astype(BF16)
        new_mean = (dot_nt(mean[...], g0[...]) + offset[...]).astype(BF16)
        parcel[BLOCK:, :BLOCK] = new_mean
        parcel[BLOCK:, BLOCK:] = jnp.zeros((TAIL, 2 * BLOCK), BF16)
        mean_row[...] = new_mean
        keep_whole(full, mean, half, half_mean)

    if at_seg < GROUP_SEGS - 1:
        @pl.when(seg == GROUP_SEGS - 1)
        def _():
            parcel[...] = early[...]

        beside[...] = parcel[:BLOCK, BLOCK : 2 * BLOCK]
        far[...] = parcel[:BLOCK, 2 * BLOCK :]


def hand_kernel(at_seg, where, event, gain, out, sem):
    @pl.when(where[1] == at_seg)
    def _():
        copy = pltpu.make_async_copy(gain, out, sem)
        copy.start()
        copy.wait()


def stack_kernel(where, event, g0, g1, g2, g3, n0, n1, n2, n3, lift):
    z, seg = where[0], where[1]
    states = g0.shape[1]

    @pl.when(seg == 1)
    def _():
        for a, gain in enumerate((g0, g1, g2, g3)):
            lift[cols(spot(z, a)), :] = gain[...]
        lay_out(z, (n0, n1, n2, n3), lift.at[pl.ds(states, states)], lift.at[pl.ds(2 * states, TAIL)])


def turn_kernel(where, near, far, b2, t0, t1, t2, t3, t4, out):
    def body(a, parcel):
        out[a] = parcel[...]

    @pl.when(where[1] == 1)
    def _():
        each_parcel(by_relay(where[0], t0, t1, t2, t3, t4), body)


def ahead_kernel(where, event, lift, gain, step_gain, block_1, block_2, left, base, through, beside, block_1_on, block_2_on):
    seg = where[1]
    states = gain.shape[1]

    @pl.when(seg > 1)
    def _():
        block_1_on[...] = block_1[...]
        block_2_on[...] = block_2[...]

    @pl.when(seg == 0)
    def _():
        through[...] = dot(gain[...], lift[:states, :]).astype(BF16)
        beside[...] = dot(gain[...], lift[states : 2 * states, :])

        def one(k, carry):
            rows = step_gain[k]
            left[k] = dot(rows, lift[:states, :]).astype(BF16)
            value = dot(rows, lift[states : 2 * states, :]) * rows.astype(F32)
            base[pl.ds(k, 1), :] = row_sums(value)
            return carry

        lax.fori_loop(0, step_gain.shape[0], one, 0, unroll=4)


def row_sums(value):
    total = value[:, :128]
    for at in range(128, value.shape[1], 128):
        total = total + value[:, at : at + 128]
    return jnp.sum(total.T, axis=0, keepdims=True)


def moments_kernel(where, ends_1, ends_0, lift, left, base, gain, offset, var, kept, kept_mean, half, half_mean, out_mean, out_spread, out):
    z, seg = where[0], where[1]
    states = gain.shape[2]

    @pl.when(seg == 1)
    def _():
        keep_parcels(z, [ends_1.at[a] for a in range(RING)], half, half_mean)

    @pl.when(seg == 0)
    def _():
        keep_parcels(z, [ends_0.at[a] for a in range(RING)], half, half_mean)
        tail = lift[2 * states :, :].astype(F32)
        half_mean[...] = (dot_nt(half_mean[...], lift[:states, :]) + tail[0:1] + tail[1:2]).astype(BF16)

    def steps(rows_of, more):
        def one(k, carry):
            total = jnp.zeros((BLOCK, BLOCK), F32)
            for b in range(RING):
                blocks = (b + 2, b + 3, b) if b in (1, 2) else (b + 3, b)
                parts = [rows_of[k, :, (r % RING) * BLOCK : (r % RING + 1) * BLOCK] for r in blocks]
                value = dot(jnp.concatenate(parts, axis=1), half[b, (3 - len(blocks)) * BLOCK :, :])
                total = total + value * parts[-1].astype(F32)
            spread = row_sums(total) + var[pl.ds(k, 1), :]
            if more is not None:
                spread = spread + more[pl.ds(k, 1), :]
            means = dot_nt(half_mean[...], gain[k])[0:1] + offset[pl.ds(k, 1), :]
            out[0, pl.ds(k, 1), :] = means
            out[1, pl.ds(k, 1), :] = spread
            out_mean[pl.ds(k, 1), :] = means
            out_spread[pl.ds(k, 1), :] = spread
            return carry

        lax.fori_loop(0, gain.shape[0], one, 0, unroll=4)

    @pl.when(seg == 0)
    def _():
        steps(left, base)

    @pl.when(seg != 0)
    def _():
        steps(gain, None)


def last_kernel(where, g0, a1, a2, a3, ends_1, ends_0, lift, through, beside, noise, offset, means, own, far, near, rows, mean_row, product, full, mean):
    z, seg = where[0], where[1]
    states = g0.shape[1]
    mean_row[...] = (dot_nt(means[...], g0[...]) + offset[...]).astype(BF16)

    @pl.when(seg == 0)
    def _():
        lay_out(z, [ends_0.at[a] for a in range(RING)], full, mean)
        half_way = dot(through[...], full[...]).astype(BF16)
        product[...] = (dot_nt(half_way, lift[:states, :]) + beside[...]).astype(BF16)

    @pl.when(seg == 1)
    def _():
        lay_out(z, [ends_1.at[a] for a in range(RING)], full, mean)
        finish(z, dot(g0[...], full[...]).astype(BF16), (g0, a1, a2, a3), noise, rows)

    @pl.when(seg > 1)
    def _():
        rows[:, cols(z)] = own[:BLOCK, :BLOCK]
        rows[:, cols(spot(z, 1))] = own[:BLOCK, BLOCK : 2 * BLOCK]
        rows[:, cols(spot(z, 3))] = near[...].T

        @pl.when(owns_far(z))
        def _():
            rows[:, cols(spot(z, 2))] = own[:BLOCK, 2 * BLOCK :]

        @pl.when(jnp.logical_not(owns_far(z)))
        def _():
            rows[:, cols(spot(z, 2))] = far[...].T


def finish(z, product, gains, noise, rows):
    for a, gain in enumerate(gains):
        column = cols(spot(z, a))
        rows[:, column] = (dot_nt(product, gain[...]) + noise[:, column].astype(F32)).astype(BF16)


def innovation_kernel(where, tiles, counts, s0, s1, s2, s3, value, noise, mean_1, mean_2, mean_3, product, g0, b1, b2, b3, cov_noise, _, out, mean_row, rows_out, full, rows, sem):
    z, seg = where[0], where[1]
    copy = pltpu.make_async_copy(rows, rows_out, sem)

    @pl.when(seg == 0)
    def _():
        finish(z, product[...], (g0, b1, b2, b3), cov_noise, rows)
        copy.start()

    mean = mean_1[0:1].astype(F32)
    for at, source in ((2, mean_2), (3, mean_3)):
        mean = jnp.where(seg == at, source[0:1].astype(F32), mean)
    mean_row[...] = mean.astype(BF16)
    for a, part in enumerate((s0, s1, s2, s3)):
        full[:, :, cols(spot(z, a))] = part[...]
    full[1] = full[1] + noise[...]
    for k in range(value.shape[0]):
        for j in range(SLOTS):
            at = pl.ds(pl.multiple_of(tiles[j, k] * TILE_STATES, TILE_STATES), TILE_STATES)
            result = (value[k, j : j + 1, :] - full[0, k : k + 1, at]) / full[1, k : k + 1, at]
            out[k, j : j + 1, :] = jnp.where(j < counts[k], result, 0.0)

    @pl.when(seg == 0)
    def _():
        copy.wait()


def smem():
    return pl.BlockSpec(memory_space=pltpu.SMEM)


def vmem():
    return pl.BlockSpec(memory_space=pltpu.VMEM)


def params():
    return pltpu.CompilerParams(vmem_limit_bytes=VMEM)


def cost(flops, moved):
    return pl.CostEstimate(flops=int(flops), bytes_accessed=int(moved), transcendentals=0)


def shape(dims, kind=BF16):
    return jax.ShapeDtypeStruct(dims, kind)


def ring_shards(groups, seg_gain, seg_offset, seg_noise, end_mean, end_cov, step_gain, step_offset, step_var, obs_tiles, obs_count, obs_value, obs_noise):
    position = lax.axis_index("tm")
    z = lax.axis_index("tile")
    where = jnp.stack([z, position % GROUP_SEGS, position // GROUP_SEGS]).astype(jnp.int32)
    gain, noise = seg_gain[0], seg_noise[0]
    states = gain.shape[1]
    steps = step_gain.shape[0]
    parcel_shape = shape((BLOCK + TAIL, 3 * BLOCK))

    def route(block, moves):
        table = []
        for g in range(groups):
            for (source, start), (target, end) in moves:
                table.append(((g * GROUP_SEGS + source) * RING + start, (g * GROUP_SEGS + target) * RING + end))
        return lax.ppermute(block, ("tm", "tile"), table)

    def send(block, pairs, shift):
        return route(block, [((a, (to + shift) % RING), (b, to)) for a, b in pairs for to in range(RING)])

    def exchange(block, pairs, own=None):
        others = [send(block, pairs, a) for a in (2, 1, 3)]
        return [send(block, pairs, 0) if own is None else own, others[1], others[0], others[2]]

    def within(segments, steps):
        return [((a, start), (a, to)) for a in segments for start, to in steps]

    def call(kernel, name, out_shape, operands, scratch, flops, aliases={}):
        moved = sum(x.size * x.dtype.itemsize for x in list(operands) + list(out_shape))
        return pl.pallas_call(
            kernel,
            out_shape=out_shape,
            in_specs=[smem()] + [vmem()] * len(operands),
            out_specs=(vmem(),) * len(out_shape),
            scratch_shapes=scratch,
            input_output_aliases=aliases,
            compiler_params=params(),
            cost_estimate=cost(flops, moved),
            name=name,
        )(where, *operands)

    def pack(kernel, name, out_shape, far_operands, near_operands, sems, limit):
        return pl.pallas_call(
            kernel,
            out_shape=out_shape,
            in_specs=[smem()] + [pl.BlockSpec(memory_space=pl.ANY)] * len(far_operands) + [vmem()] * len(near_operands),
            out_specs=jax.tree.map(lambda _: vmem(), out_shape),
            scratch_shapes=[sems],
            compiler_params=pltpu.CompilerParams(vmem_limit_bytes=limit),
            cost_estimate=cost(0, 1e6),
            name=name,
        )(where, *far_operands, *near_operands)

    full_and_mean = [pltpu.VMEM((states, states), BF16), pltpu.VMEM((TAIL, states), BF16)]
    row_shape, mean_shape, block_shape = shape((BLOCK, states)), shape((TAIL, BLOCK)), shape((BLOCK, BLOCK))
    half_shapes = (shape((RING, 3 * BLOCK, BLOCK)), shape((TAIL, states)))

    back, two_on, on = ((1, 0), (2, 1), (3, 2), (0, 3)), ((0, 2), (1, 3), (2, 0), (3, 1)), ((0, 1), (1, 2), (2, 3), (3, 0))
    pair_gains = [route(gain, within((3, 2, 1), back)), route(gain, within((3, 2), ((2, 0), (1, 3))) + within((1,), on))]
    parcel = pack(pack_kernel, "pack", parcel_shape, (end_cov, noise), (end_mean, seg_offset), pltpu.SemaphoreType.DMA((3,)), ALL_VMEM)
    ups, downs = ((0, 1), (1, 2), (2, 3)), ((1, 0), (2, 1), (3, 2))
    first = [
        route(parcel, within((3,), downs) + within((1,), back)),
        route(parcel, [((0, start), (3, to)) for start, to in two_on if to != 0] + within((1,), two_on)),
        route(parcel, within((3,), ups) + within((1,), on)),
    ]
    handed = [route(first[0], within((3,), ((1, 0),))), route(first[1], within((3,), ((1, 0), (2, 3))))]

    def hand(segment, event):
        kernel = functools.partial(hand_kernel, segment)
        return pack(kernel, f"hand_{segment}", row_shape, (event, gain), (), pltpu.SemaphoreType.DMA, VMEM)

    gains_1 = [pair_gains[0], route(hand(1, first[1]), within((1,), two_on)), pair_gains[1]]

    flops = 4 * BLOCK * states * states
    *kept, parcel_3, mean_3 = call(
        functools.partial(pairs_kernel, 3),
        "pairs_3",
        (*half_shapes, parcel_shape, mean_shape),
        (gain, *pair_gains, noise, seg_offset, end_cov, end_mean, *first, *handed),
        full_and_mean + [pltpu.VMEM(parcel_shape.shape, BF16)],
        flops,
    )
    second = exchange(parcel_3, ((3, 2),))

    *kept, parcel_2, mean_2, beside_block, far_block = call(
        functools.partial(pairs_kernel, 2),
        "pairs_2",
        (*half_shapes, parcel_shape, mean_shape, block_shape, block_shape),
        (gain, *pair_gains, noise, seg_offset, *second, parcel_3, *kept),
        full_and_mean,
        flops,
        {11: 0, 12: 1},
    )
    own = send(parcel_2, ((2, 1),), 0)
    across = send(parcel_2, ((2, 1),), 2)
    sides = [
        route(parcel_2, [((2, start), (1, to)) for start, to in moves])
        for moves in (((1, 0), (2, 1), (3, 2), (0, 3)), ((0, 1), (1, 2), (2, 3)))
    ]
    third = [own, sides[0], across, sides[1], route(across, within((1,), ((1, 0),)))]
    (lift,) = call(stack_kernel, "stack", (shape((2 * states + TAIL, states)),), (parcel_2, gain, *gains_1, parcel, *first), [], 0)
    lift = send(lift, ((1, 0),), 0)
    gain_0 = hand(0, lift)
    left, base, through, beside, beside_block, far_block = call(
        ahead_kernel,
        "ahead",
        (shape(step_gain.shape), shape((steps, BLOCK), F32), row_shape, shape((BLOCK, states), F32), block_shape, block_shape),
        (gain_0, lift, gain, step_gain, beside_block, far_block),
        [],
        4 * (steps + 1) * BLOCK * states * states,
    )
    gains_0 = [route(gain_0, within((0,), moves)) for moves in (back, two_on, on)]
    near, far = route(beside_block, within((3, 2), on)), route(far_block, within((3, 2), ((0, 2), (3, 1))))
    (ends_1,) = call(turn_kernel, "turn", (shape((RING, *parcel_shape.shape)),), (near, far, gains_0[1], *third), [], 0)
    ends_0 = send(ends_1, ((1, 0),), 0)
    out_steps = shape((steps, BLOCK), F32)
    _, means, step_mean, step_spread, stats = call(
        moments_kernel,
        "moments",
        (*half_shapes, out_steps, out_steps, shape((2, steps, BLOCK), F32)),
        (ends_1, ends_0, lift, left, base, step_gain, step_offset, step_var, *kept),
        [],
        2 * steps * BLOCK * states * states,
        {9: 0, 10: 1},
    )
    everyone = tuple((s, s) for s in range(GROUP_SEGS))
    all_stats = [stats] + [send(stats, everyone, a) for a in range(1, RING)]
    rows, mean_1, product = call(
        last_kernel,
        "last",
        (row_shape, mean_shape, row_shape),
        (gain, *gains_1, ends_1, ends_0, lift, through, beside, noise, seg_offset, means, parcel_2, far, near),
        full_and_mean,
        flops,
    )
    innovation, out_mean, out_cov = pl.pallas_call(
        innovation_kernel,
        out_shape=(shape(obs_value.shape, F32), shape((1, BLOCK)), row_shape),
        in_specs=[smem()] * 3 + [vmem()] * 15 + [pl.BlockSpec(memory_space=pl.ANY)],
        out_specs=(vmem(), vmem(), pl.BlockSpec(memory_space=pl.ANY)),
        scratch_shapes=[pltpu.VMEM((2, steps, states), F32), pltpu.VMEM(row_shape.shape, BF16), pltpu.SemaphoreType.DMA],
        input_output_aliases={18: 2},
        compiler_params=params(),
        cost_estimate=cost(0, 2e5),
        name="innovation",
    )(where, obs_tiles.T, obs_count, *all_stats, obs_value, obs_noise.reshape(1, states), mean_1, mean_2, mean_3, product, gain, *gains_0, noise, rows)
    return out_cov[None], out_mean, step_mean, step_spread, innovation


def solution(mesh):
    in_specs = (
        P("tm", "tile", None),
        P("tm", "tile"),
        P("tm", "tile", None),
        P(None, "tile"),
        P(None, "tile", None),
        P("tm", "tile", None),
        P("tm", "tile"),
        P("tm", "tile"),
        P("tm", None),
        P("tm"),
        P("tm", None, None),
        P(),
    )
    out_specs = (
        P("tm", "tile", None),
        P("tm", "tile"),
        P("tm", "tile"),
        P("tm", "tile"),
        P("tm", None, None),
    )
    if mesh.shape["tile"] == RING:
        shards = functools.partial(ring_shards, mesh.shape["tm"] // GROUP_SEGS)
    else:
        shards = general_shards
    return jax.shard_map(shards, mesh=mesh, in_specs=in_specs, out_specs=out_specs, check_vma=False)
```

```python
import functools
import jax
import jax.numpy as jnp
from jax import lax
from jax.experimental import pallas as pl
from jax.experimental.pallas import tpu as pltpu
from jax.sharding import PartitionSpec as P

TILE_STATES = 128
SLOTS = 4
GROUP_SEGS = 4


def shifted(block, axis, distance):
    devices = range(lax.axis_size(axis))
    route = [(i - distance, i) for i in devices if i - distance in devices]
    return lax.ppermute(block, axis, route)


def general_shards(
    seg_gain,
    seg_offset,
    seg_noise,
    end_mean,
    end_cov,
    step_gain,
    step_offset,
    step_var,
    obs_tiles,
    obs_count,
    obs_value,
    obs_noise,
):
    position = lax.axis_index("tm")
    slot_place = position % GROUP_SEGS
    group_index = position // GROUP_SEGS
    gain_rows = seg_gain[0]
    offset_rows = seg_offset[0]
    noise_rows = seg_noise[0].astype(jnp.float32)
    row_count = gain_rows.shape[0]
    state_count = gain_rows.shape[1]
    cur_mean = lax.dynamic_index_in_dim(end_mean, group_index, 0, keepdims=False)
    cur_cov = lax.dynamic_index_in_dim(end_cov, group_index, 0, keepdims=False)
    kept_mean = jnp.zeros((state_count,), jnp.bfloat16)
    kept_cov = jnp.zeros((state_count, state_count), jnp.bfloat16)
    out_mean = jnp.zeros((row_count,), jnp.bfloat16)
    out_cov = jnp.zeros((row_count, state_count), jnp.bfloat16)
    for depth_step in range(GROUP_SEGS):
        whole_mean, whole_cov = (
            lax.all_gather(cur_mean, "tile", axis=0, tiled=True),
            lax.all_gather(cur_cov, "tile", axis=0, tiled=True),
        )
        is_mine = slot_place == GROUP_SEGS - 1 - depth_step
        kept_mean = jnp.where(is_mine, whole_mean, kept_mean)
        kept_cov = jnp.where(is_mine, whole_cov, kept_cov)
        product = jnp.dot(gain_rows, whole_cov, preferred_element_type=jnp.float32).astype(
            jnp.bfloat16
        )
        col_block = jnp.einsum(
            "pd,rd->pr",
            lax.all_gather(product, "tile", axis=0, tiled=True),
            gain_rows,
            preferred_element_type=jnp.float32,
        )
        spread_rows = lax.all_to_all(col_block, "tile", split_axis=0, concat_axis=1, tiled=True)
        new_cov = (spread_rows + noise_rows).astype(jnp.bfloat16)
        new_mean = (
            jnp.dot(gain_rows, whole_mean, preferred_element_type=jnp.float32) + offset_rows
        ).astype(jnp.bfloat16)
        out_mean = jnp.where(is_mine, new_mean, out_mean)
        out_cov = jnp.where(is_mine, new_cov, out_cov)
        if depth_step < GROUP_SEGS - 1:
            got_mean, got_cov = shifted((new_mean, new_cov), "tm", -1)
            takes_next = slot_place == GROUP_SEGS - 2 - depth_step
            cur_mean = jnp.where(takes_next, got_mean, cur_mean)
            cur_cov = jnp.where(takes_next, got_cov, cur_cov)
    partial_value = jnp.einsum(
        "krd,de->kre", step_gain, kept_cov, preferred_element_type=jnp.float32
    )
    local_spread = jnp.sum(partial_value * step_gain, axis=2) + step_var
    local_mean = (
        jnp.einsum("krd,d->kr", step_gain, kept_mean, preferred_element_type=jnp.float32)
        + step_offset
    )
    full_mean, full_spread = (
        lax.all_gather(local_mean, "tile", axis=1, tiled=True),
        lax.all_gather(local_spread, "tile", axis=1, tiled=True),
    )
    step_count = full_mean.shape[0]
    tile_total = state_count // TILE_STATES
    tile_mean = full_mean.reshape(step_count, tile_total, TILE_STATES)
    tile_spread = full_spread.reshape(step_count, tile_total, TILE_STATES) + obs_noise.reshape(
        1, tile_total, TILE_STATES
    )
    onehot = (
        obs_tiles[:, :, None] == jnp.arange(tile_total, dtype=jnp.int32)[None, None, :]
    ).astype(jnp.float32)
    picked_mean = jnp.einsum("ksn,kno->kso", onehot, tile_mean, precision=lax.Precision.HIGHEST)
    picked_spread = jnp.einsum("ksn,kno->kso", onehot, tile_spread, precision=lax.Precision.HIGHEST)
    live_slots = jnp.arange(SLOTS, dtype=jnp.int32)[None, :] < obs_count[:, None]
    innovation = jnp.where(
        live_slots[:, :, None], (obs_value - picked_mean) / picked_spread, jnp.float32(0.0)
    )
    return (out_cov[None], out_mean[None], local_mean, local_spread, innovation)


BLOCK = 256
RING = 4
TAIL = 16
VMEM = 12 * 1024 * 1024
ALL_VMEM = 56 * 1024 * 1024
NT = (((1,), (1,)), ((), ()))
F32 = jnp.float32
BF16 = jnp.bfloat16


def cols(index):
    return pl.ds(pl.multiple_of(index * BLOCK, BLOCK), BLOCK)


def spot(z, shift):
    return lax.rem(z + shift, RING)


def dot(a, b):
    return jnp.dot(a, b, preferred_element_type=F32)


def dot_nt(a, b):
    return lax.dot_general(a, b, NT, preferred_element_type=F32)


def owns_far(row):
    return (row == 0) | (row == RING - 1)


def each_parcel(parcels, body):
    for a, entry in enumerate(parcels):
        if isinstance(entry, tuple):
            condition, one, other = entry
            pl.when(condition)(functools.partial(body, a, one))
            pl.when(jnp.logical_not(condition))(functools.partial(body, a, other))
        else:
            body(a, entry)


def by_relay(z, own, after, across, before, handed):
    return own, after, across, (z > 0, before, handed)


def lay_out(z, parcels, full, mean):
    def body(a, parcel):
        at = spot(z, a)
        row, near, far = cols(at), cols(spot(z, a + 1)), cols(spot(z, a + 2))
        full[row, row] = parcel[:BLOCK, :BLOCK]
        beside = parcel[:BLOCK, BLOCK : 2 * BLOCK]
        full[row, near] = beside
        full[near, row] = beside.T
        mean[:, row] = parcel[BLOCK:, :BLOCK]

        @pl.when(owns_far(at))
        def _():
            block = parcel[:BLOCK, 2 * BLOCK :]
            full[row, far] = block
            full[far, row] = block.T

    each_parcel(parcels, body)


def keep_parcels(z, parcels, half, half_mean):
    def body(a, parcel):
        at = spot(z, a)
        half_mean[:, cols(at)] = parcel[BLOCK:, :BLOCK]
        half[at, 2 * BLOCK :, :] = parcel[:BLOCK, :BLOCK]
        half[spot(z, a + 1), BLOCK : 2 * BLOCK, :] = parcel[:BLOCK, BLOCK : 2 * BLOCK] * 2

        @pl.when(owns_far(at))
        def _():
            half[spot(z, a + 2), :BLOCK, :] = parcel[:BLOCK, 2 * BLOCK :] * 2

    each_parcel(parcels, body)


def keep_whole(full, mean, half, half_mean):
    half_mean[...] = mean[...]
    for b in range(RING):
        column = slice(b * BLOCK, (b + 1) * BLOCK)
        for j in range(3):
            if j < 2 or b in (1, 2):
                row = (b - j) % RING * BLOCK
                block = full[row : row + BLOCK, column]
                half[b, (2 - j) * BLOCK : (3 - j) * BLOCK, :] = block * 2 if j else block


def fetch(source, z, tail, parcel, sems):
    copies = []
    for j in range(3):
        target = parcel.at[pl.ds(0, BLOCK), pl.ds(j * BLOCK, BLOCK)]
        copies.append(pltpu.make_async_copy(source.at[:, cols(spot(z, j))], target, sems.at[j]))
    for copy in copies:
        copy.start()
    parcel[BLOCK:, :] = jnp.zeros((TAIL, 3 * BLOCK), BF16)
    parcel[BLOCK:, :BLOCK] = tail.astype(BF16)
    for copy in copies:
        copy.wait()


def group_mean(group, end_mean):
    mean = jnp.zeros((1, BLOCK), F32)
    for g in range(end_mean.shape[0]):
        mean = jnp.where(group == g, end_mean[g : g + 1, :].astype(F32), mean)
    return jnp.broadcast_to(mean, (TAIL, BLOCK))


def pack_kernel(where, end_cov, noise, end_mean, offset, parcel, sems):
    z, seg, group = where[0], where[1], where[2]

    @pl.when(seg == 1)
    def _():
        high = offset[...].astype(BF16).astype(F32)
        first = lax.broadcasted_iota(jnp.int32, (TAIL, BLOCK), 0) == 0
        fetch(noise, z, jnp.where(first, high, offset[...] - high), parcel, sems)

    @pl.when(seg != 1)
    def _():
        fetch(end_cov.at[group], z, group_mean(group, end_mean), parcel, sems)


def pairs_kernel(at_seg, where, g0, g1, g2, noise, offset, *refs):
    z, seg, group = where[0], where[1], where[2]
    if at_seg == GROUP_SEGS - 1:
        end_cov, end_mean, *others, half, half_mean, parcel, mean_row, full, mean, own = refs
        parcels = (own, *others)
    else:
        p2, p1, p3, p0, early, _, _, half, half_mean, parcel, mean_row, beside, far, full, mean = refs
        parcels = (p0, p1, p2, p3)

    @pl.when(seg == at_seg)
    def _():
        if at_seg == GROUP_SEGS - 1:
            for j in range(3):
                own[:BLOCK, j * BLOCK : (j + 1) * BLOCK] = end_cov[group, :, cols(spot(z, j))]
            own[BLOCK:, :BLOCK] = group_mean(group, end_mean).astype(BF16)
        lay_out(z, parcels, full, mean)
        product = dot(g0[...], full[...]).astype(BF16)
        for j, gain in enumerate((g0, g1, g2)):
            block = dot_nt(product, gain[...]) + noise[:, cols(spot(z, j))].astype(F32)
            parcel[:BLOCK, j * BLOCK : (j + 1) * BLOCK] = block.astype(BF16)
        new_mean = (dot_nt(mean[...], g0[...]) + offset[...]).astype(BF16)
        parcel[BLOCK:, :BLOCK] = new_mean
        parcel[BLOCK:, BLOCK:] = jnp.zeros((TAIL, 2 * BLOCK), BF16)
        mean_row[...] = new_mean
        keep_whole(full, mean, half, half_mean)

    if at_seg < GROUP_SEGS - 1:
        @pl.when(seg == GROUP_SEGS - 1)
        def _():
            parcel[...] = early[...]

        beside[...] = parcel[:BLOCK, BLOCK : 2 * BLOCK]
        far[...] = parcel[:BLOCK, 2 * BLOCK :]


def hand_kernel(at_seg, where, event, gain, out, sem):
    @pl.when(where[1] == at_seg)
    def _():
        copy = pltpu.make_async_copy(gain, out, sem)
        copy.start()
        copy.wait()


def stack_kernel(where, event, g0, g1, g2, g3, n0, n1, n2, n3, lift):
    z, seg = where[0], where[1]
    states = g0.shape[1]

    @pl.when(seg == 1)
    def _():
        for a, gain in enumerate((g0, g1, g2, g3)):
            lift[cols(spot(z, a)), :] = gain[...]
        lay_out(z, (n0, n1, n2, n3), lift.at[pl.ds(states, states)], lift.at[pl.ds(2 * states, TAIL)])


def turn_kernel(where, near, far, b2, t2, t1, t3, t4, t0, out):
    def body(a, parcel):
        out[a] = parcel[...]

    @pl.when(where[1] == 1)
    def _():
        each_parcel(by_relay(where[0], t0, t1, t2, t3, t4), body)


def ahead_kernel(where, event, lift, gain, step_gain, block_1, block_2, left, base, through, beside, block_1_on, block_2_on):
    seg = where[1]
    states = gain.shape[1]

    @pl.when(seg > 1)
    def _():
        block_1_on[...] = block_1[...]
        block_2_on[...] = block_2[...]

    @pl.when(seg == 0)
    def _():
        through[...] = dot(gain[...], lift[:states, :]).astype(BF16)
        beside[...] = dot(gain[...], lift[states : 2 * states, :])

        def one(k, carry):
            rows = step_gain[k]
            left[k] = dot(rows, lift[:states, :]).astype(BF16)
            value = dot(rows, lift[states : 2 * states, :]) * rows.astype(F32)
            base[pl.ds(k, 1), :] = row_sums(value)
            return carry

        lax.fori_loop(0, step_gain.shape[0], one, 0, unroll=4)


def row_sums(value):
    total = value[:, :128]
    for at in range(128, value.shape[1], 128):
        total = total + value[:, at : at + 128]
    return jnp.sum(total.T, axis=0, keepdims=True)


def moments_kernel(where, ends_1, ends_0, lift, left, base, gain, offset, var, kept, kept_mean, half, half_mean, out_mean, out_spread, out):
    z, seg = where[0], where[1]
    states = gain.shape[2]

    @pl.when(seg == 1)
    def _():
        keep_parcels(z, [ends_1.at[a] for a in range(RING)], half, half_mean)

    @pl.when(seg == 0)
    def _():
        keep_parcels(z, [ends_0.at[a] for a in range(RING)], half, half_mean)
        tail = lift[2 * states :, :].astype(F32)
        half_mean[...] = (dot_nt(half_mean[...], lift[:states, :]) + tail[0:1] + tail[1:2]).astype(BF16)

    def steps(rows_of, more):
        def one(k, carry):
            total = jnp.zeros((BLOCK, BLOCK), F32)
            for b in range(RING):
                blocks = (b + 2, b + 3, b) if b in (1, 2) else (b + 3, b)
                parts = [rows_of[k, :, (r % RING) * BLOCK : (r % RING + 1) * BLOCK] for r in blocks]
                value = dot(jnp.concatenate(parts, axis=1), half[b, (3 - len(blocks)) * BLOCK :, :])
                total = total + value * parts[-1].astype(F32)
            spread = row_sums(total) + var[pl.ds(k, 1), :]
            if more is not None:
                spread = spread + more[pl.ds(k, 1), :]
            means = dot_nt(half_mean[...], gain[k])[0:1] + offset[pl.ds(k, 1), :]
            out[0, pl.ds(k, 1), :] = means
            out[1, pl.ds(k, 1), :] = spread
            out_mean[pl.ds(k, 1), :] = means
            out_spread[pl.ds(k, 1), :] = spread
            return carry

        lax.fori_loop(0, gain.shape[0], one, 0, unroll=4)

    @pl.when(seg == 0)
    def _():
        steps(left, base)

    @pl.when(seg != 0)
    def _():
        steps(gain, None)


def last_kernel(where, g0, a1, a2, a3, ends_1, ends_0, lift, through, beside, noise, offset, means, own, far, near, rows, mean_row, product, full, mean):
    z, seg = where[0], where[1]
    states = g0.shape[1]
    mean_row[...] = (dot_nt(means[...], g0[...]) + offset[...]).astype(BF16)

    @pl.when(seg == 0)
    def _():
        lay_out(z, [ends_0.at[a] for a in range(RING)], full, mean)
        half_way = dot(through[...], full[...]).astype(BF16)
        product[...] = (dot_nt(half_way, lift[:states, :]) + beside[...]).astype(BF16)

    @pl.when(seg == 1)
    def _():
        lay_out(z, [ends_1.at[a] for a in range(RING)], full, mean)
        finish(z, dot(g0[...], full[...]).astype(BF16), (g0, a1, a2, a3), noise, rows)

    @pl.when(seg > 1)
    def _():
        rows[:, cols(z)] = own[:BLOCK, :BLOCK]
        rows[:, cols(spot(z, 1))] = own[:BLOCK, BLOCK : 2 * BLOCK]
        rows[:, cols(spot(z, 3))] = near[...].T

        @pl.when(owns_far(z))
        def _():
            rows[:, cols(spot(z, 2))] = own[:BLOCK, 2 * BLOCK :]

        @pl.when(jnp.logical_not(owns_far(z)))
        def _():
            rows[:, cols(spot(z, 2))] = far[...].T


def finish(z, product, gains, noise, rows):
    for a, gain in enumerate(gains):
        column = cols(spot(z, a))
        rows[:, column] = (dot_nt(product, gain[...]) + noise[:, column].astype(F32)).astype(BF16)


def innovation_kernel(where, tiles, counts, s0, s1, s2, s3, value, noise, mean_1, mean_2, mean_3, product, g0, b1, b2, b3, cov_noise, _, out, mean_row, rows_out, full, rows, sem):
    z, seg = where[0], where[1]
    copy = pltpu.make_async_copy(rows, rows_out, sem)

    @pl.when(seg == 0)
    def _():
        finish(z, product[...], (g0, b1, b2, b3), cov_noise, rows)
        copy.start()

    mean = mean_1[0:1].astype(F32)
    for at, source in ((2, mean_2), (3, mean_3)):
        mean = jnp.where(seg == at, source[0:1].astype(F32), mean)
    mean_row[...] = mean.astype(BF16)
    for a, part in enumerate((s0, s1, s2, s3)):
        full[:, :, cols(spot(z, a))] = part[...]
    full[1] = full[1] + noise[...]
    for k in range(value.shape[0]):
        for j in range(SLOTS):
            at = pl.ds(pl.multiple_of(tiles[j, k] * TILE_STATES, TILE_STATES), TILE_STATES)
            result = (value[k, j : j + 1, :] - full[0, k : k + 1, at]) / full[1, k : k + 1, at]
            out[k, j : j + 1, :] = jnp.where(j < counts[k], result, 0.0)

    @pl.when(seg == 0)
    def _():
        copy.wait()


def smem():
    return pl.BlockSpec(memory_space=pltpu.SMEM)


def vmem():
    return pl.BlockSpec(memory_space=pltpu.VMEM)


def params():
    return pltpu.CompilerParams(vmem_limit_bytes=VMEM)


def cost(flops, moved):
    return pl.CostEstimate(flops=int(flops), bytes_accessed=int(moved), transcendentals=0)


def shape(dims, kind=BF16):
    return jax.ShapeDtypeStruct(dims, kind)


def ring_shards(groups, seg_gain, seg_offset, seg_noise, end_mean, end_cov, step_gain, step_offset, step_var, obs_tiles, obs_count, obs_value, obs_noise):
    position = lax.axis_index("tm")
    z = lax.axis_index("tile")
    where = jnp.stack([z, position % GROUP_SEGS, position // GROUP_SEGS]).astype(jnp.int32)
    gain, noise = seg_gain[0], seg_noise[0]
    states = gain.shape[1]
    steps = step_gain.shape[0]
    parcel_shape = shape((BLOCK + TAIL, 3 * BLOCK))

    def route(block, moves):
        table = []
        for g in range(groups):
            for (source, start), (target, end) in moves:
                table.append(((g * GROUP_SEGS + source) * RING + start, (g * GROUP_SEGS + target) * RING + end))
        return lax.ppermute(block, ("tm", "tile"), table)

    def send(block, pairs, shift):
        return route(block, [((a, (to + shift) % RING), (b, to)) for a, b in pairs for to in range(RING)])

    def exchange(block, pairs, own=None):
        others = [send(block, pairs, a) for a in (2, 1, 3)]
        return [send(block, pairs, 0) if own is None else own, others[1], others[0], others[2]]

    def within(segments, steps):
        return [((a, start), (a, to)) for a in segments for start, to in steps]

    def call(kernel, name, out_shape, operands, scratch, flops, aliases={}):
        moved = sum(x.size * x.dtype.itemsize for x in list(operands) + list(out_shape))
        return pl.pallas_call(
            kernel,
            out_shape=out_shape,
            in_specs=[smem()] + [vmem()] * len(operands),
            out_specs=(vmem(),) * len(out_shape),
            scratch_shapes=scratch,
            input_output_aliases=aliases,
            compiler_params=params(),
            cost_estimate=cost(flops, moved),
            name=name,
        )(where, *operands)

    def pack(kernel, name, out_shape, far_operands, near_operands, sems, limit):
        return pl.pallas_call(
            kernel,
            out_shape=out_shape,
            in_specs=[smem()] + [pl.BlockSpec(memory_space=pl.ANY)] * len(far_operands) + [vmem()] * len(near_operands),
            out_specs=jax.tree.map(lambda _: vmem(), out_shape),
            scratch_shapes=[sems],
            compiler_params=pltpu.CompilerParams(vmem_limit_bytes=limit),
            cost_estimate=cost(0, 1e6),
            name=name,
        )(where, *far_operands, *near_operands)

    full_and_mean = [pltpu.VMEM((states, states), BF16), pltpu.VMEM((TAIL, states), BF16)]
    row_shape, mean_shape, block_shape = shape((BLOCK, states)), shape((TAIL, BLOCK)), shape((BLOCK, BLOCK))
    half_shapes = (shape((RING, 3 * BLOCK, BLOCK)), shape((TAIL, states)))

    back, two_on, on = ((1, 0), (2, 1), (3, 2), (0, 3)), ((0, 2), (1, 3), (2, 0), (3, 1)), ((0, 1), (1, 2), (2, 3), (3, 0))
    pair_gains = [route(gain, within((3, 2, 1), back)), route(gain, within((3, 2), ((2, 0), (1, 3))) + within((1,), on))]
    parcel = pack(pack_kernel, "pack", parcel_shape, (end_cov, noise), (end_mean, seg_offset), pltpu.SemaphoreType.DMA((3,)), ALL_VMEM)
    first = [send(parcel, ((0 if a == 2 else 3, 3), (1, 1)), a) for a in range(1, RING)]

    def hand(segment, event):
        kernel = functools.partial(hand_kernel, segment)
        return pack(kernel, f"hand_{segment}", row_shape, (event, gain), (), pltpu.SemaphoreType.DMA, VMEM)

    gains_1 = [pair_gains[0], route(hand(1, first[1]), within((1,), two_on)), pair_gains[1]]

    flops = 4 * BLOCK * states * states
    *kept, parcel_3, mean_3 = call(
        functools.partial(pairs_kernel, 3),
        "pairs_3",
        (*half_shapes, parcel_shape, mean_shape),
        (gain, *pair_gains, noise, seg_offset, end_cov, end_mean, *first),
        full_and_mean + [pltpu.VMEM(parcel_shape.shape, BF16)],
        flops,
    )
    second = exchange(parcel_3, ((3, 2),))

    *kept, parcel_2, mean_2, beside_block, far_block = call(
        functools.partial(pairs_kernel, 2),
        "pairs_2",
        (*half_shapes, parcel_shape, mean_shape, block_shape, block_shape),
        (gain, *pair_gains, noise, seg_offset, second[2], second[1], second[3], second[0], parcel_3, *kept),
        full_and_mean,
        flops,
        {11: 0, 12: 1},
    )
    own = send(parcel_2, ((2, 1),), 0)
    across = send(parcel_2, ((2, 1),), 2)
    sides = [
        route(parcel_2, [((2, start), (1, to)) for start, to in moves])
        for moves in (((1, 0), (2, 1), (3, 2), (0, 3)), ((0, 1), (1, 2), (2, 3)))
    ]
    third = [own, sides[0], across, sides[1], route(across, within((1,), ((1, 0),)))]
    (lift,) = call(stack_kernel, "stack", (shape((2 * states + TAIL, states)),), (parcel_2, gain, *gains_1, parcel, *first), [], 0)
    lift = send(lift, ((1, 0),), 0)
    gain_0 = hand(0, lift)
    left, base, through, beside, beside_block, far_block = call(
        ahead_kernel,
        "ahead",
        (shape(step_gain.shape), shape((steps, BLOCK), F32), row_shape, shape((BLOCK, states), F32), block_shape, block_shape),
        (gain_0, lift, gain, step_gain, beside_block, far_block),
        [],
        4 * (steps + 1) * BLOCK * states * states,
    )
    gains_0 = [route(gain_0, within((0,), moves)) for moves in (back, two_on, on)]
    near, far = route(beside_block, within((3, 2), on)), route(far_block, within((3, 2), ((0, 2), (3, 1))))
    (ends_1,) = call(turn_kernel, "turn", (shape((RING, *parcel_shape.shape)),), (near, far, gains_0[1], third[2], third[1], third[3], third[4], third[0]), [], 0)
    ends_0 = send(ends_1, ((1, 0),), 0)
    out_steps = shape((steps, BLOCK), F32)
    _, means, step_mean, step_spread, stats = call(
        moments_kernel,
        "moments",
        (*half_shapes, out_steps, out_steps, shape((2, steps, BLOCK), F32)),
        (ends_1, ends_0, lift, left, base, step_gain, step_offset, step_var, *kept),
        [],
        2 * steps * BLOCK * states * states,
        {9: 0, 10: 1},
    )
    everyone = tuple((s, s) for s in range(GROUP_SEGS))
    all_stats = [stats] + [send(stats, everyone, a) for a in range(1, RING)]
    rows, mean_1, product = call(
        last_kernel,
        "last",
        (row_shape, mean_shape, row_shape),
        (gain, *gains_1, ends_1, ends_0, lift, through, beside, noise, seg_offset, means, parcel_2, far, near),
        full_and_mean,
        flops,
    )
    innovation, out_mean, out_cov = pl.pallas_call(
        innovation_kernel,
        out_shape=(shape(obs_value.shape, F32), shape((1, BLOCK)), row_shape),
        in_specs=[smem()] * 3 + [vmem()] * 15 + [pl.BlockSpec(memory_space=pl.ANY)],
        out_specs=(vmem(), vmem(), pl.BlockSpec(memory_space=pl.ANY)),
        scratch_shapes=[pltpu.VMEM((2, steps, states), F32), pltpu.VMEM(row_shape.shape, BF16), pltpu.SemaphoreType.DMA],
        input_output_aliases={18: 2},
        compiler_params=params(),
        cost_estimate=cost(0, 2e5),
        name="innovation",
    )(where, obs_tiles.T, obs_count, *all_stats, obs_value, obs_noise.reshape(1, states), mean_1, mean_2, mean_3, product, gain, *gains_0, noise, rows)
    return out_cov[None], out_mean, step_mean, step_spread, innovation


def solution(mesh):
    in_specs = (
        P("tm", "tile", None),
        P("tm", "tile"),
        P("tm", "tile", None),
        P(None, "tile"),
        P(None, "tile", None),
        P("tm", "tile", None),
        P("tm", "tile"),
        P("tm", "tile"),
        P("tm", None),
        P("tm"),
        P("tm", None, None),
        P(),
    )
    out_specs = (
        P("tm", "tile", None),
        P("tm", "tile"),
        P("tm", "tile"),
        P("tm", "tile"),
        P("tm", None, None),
    )
    if mesh.shape["tile"] == RING:
        shards = functools.partial(ring_shards, mesh.shape["tm"] // GROUP_SEGS)
    else:
        shards = general_shards
    return jax.shard_map(shards, mesh=mesh, in_specs=in_specs, out_specs=out_specs, check_vma=False)
```

```python
import functools
import jax
import jax.numpy as jnp
from jax import lax
from jax.experimental import pallas as pl
from jax.experimental.pallas import tpu as pltpu
from jax.sharding import PartitionSpec as P

TILE_STATES = 128
SLOTS = 4
GROUP_SEGS = 4


def shifted(block, axis, distance):
    devices = range(lax.axis_size(axis))
    route = [(i - distance, i) for i in devices if i - distance in devices]
    return lax.ppermute(block, axis, route)


def general_shards(
    seg_gain,
    seg_offset,
    seg_noise,
    end_mean,
    end_cov,
    step_gain,
    step_offset,
    step_var,
    obs_tiles,
    obs_count,
    obs_value,
    obs_noise,
):
    position = lax.axis_index("tm")
    slot_place = position % GROUP_SEGS
    group_index = position // GROUP_SEGS
    gain_rows = seg_gain[0]
    offset_rows = seg_offset[0]
    noise_rows = seg_noise[0].astype(jnp.float32)
    row_count = gain_rows.shape[0]
    state_count = gain_rows.shape[1]
    cur_mean = lax.dynamic_index_in_dim(end_mean, group_index, 0, keepdims=False)
    cur_cov = lax.dynamic_index_in_dim(end_cov, group_index, 0, keepdims=False)
    kept_mean = jnp.zeros((state_count,), jnp.bfloat16)
    kept_cov = jnp.zeros((state_count, state_count), jnp.bfloat16)
    out_mean = jnp.zeros((row_count,), jnp.bfloat16)
    out_cov = jnp.zeros((row_count, state_count), jnp.bfloat16)
    for depth_step in range(GROUP_SEGS):
        whole_mean, whole_cov = (
            lax.all_gather(cur_mean, "tile", axis=0, tiled=True),
            lax.all_gather(cur_cov, "tile", axis=0, tiled=True),
        )
        is_mine = slot_place == GROUP_SEGS - 1 - depth_step
        kept_mean = jnp.where(is_mine, whole_mean, kept_mean)
        kept_cov = jnp.where(is_mine, whole_cov, kept_cov)
        product = jnp.dot(gain_rows, whole_cov, preferred_element_type=jnp.float32).astype(
            jnp.bfloat16
        )
        col_block = jnp.einsum(
            "pd,rd->pr",
            lax.all_gather(product, "tile", axis=0, tiled=True),
            gain_rows,
            preferred_element_type=jnp.float32,
        )
        spread_rows = lax.all_to_all(col_block, "tile", split_axis=0, concat_axis=1, tiled=True)
        new_cov = (spread_rows + noise_rows).astype(jnp.bfloat16)
        new_mean = (
            jnp.dot(gain_rows, whole_mean, preferred_element_type=jnp.float32) + offset_rows
        ).astype(jnp.bfloat16)
        out_mean = jnp.where(is_mine, new_mean, out_mean)
        out_cov = jnp.where(is_mine, new_cov, out_cov)
        if depth_step < GROUP_SEGS - 1:
            got_mean, got_cov = shifted((new_mean, new_cov), "tm", -1)
            takes_next = slot_place == GROUP_SEGS - 2 - depth_step
            cur_mean = jnp.where(takes_next, got_mean, cur_mean)
            cur_cov = jnp.where(takes_next, got_cov, cur_cov)
    partial_value = jnp.einsum(
        "krd,de->kre", step_gain, kept_cov, preferred_element_type=jnp.float32
    )
    local_spread = jnp.sum(partial_value * step_gain, axis=2) + step_var
    local_mean = (
        jnp.einsum("krd,d->kr", step_gain, kept_mean, preferred_element_type=jnp.float32)
        + step_offset
    )
    full_mean, full_spread = (
        lax.all_gather(local_mean, "tile", axis=1, tiled=True),
        lax.all_gather(local_spread, "tile", axis=1, tiled=True),
    )
    step_count = full_mean.shape[0]
    tile_total = state_count // TILE_STATES
    tile_mean = full_mean.reshape(step_count, tile_total, TILE_STATES)
    tile_spread = full_spread.reshape(step_count, tile_total, TILE_STATES) + obs_noise.reshape(
        1, tile_total, TILE_STATES
    )
    onehot = (
        obs_tiles[:, :, None] == jnp.arange(tile_total, dtype=jnp.int32)[None, None, :]
    ).astype(jnp.float32)
    picked_mean = jnp.einsum("ksn,kno->kso", onehot, tile_mean, precision=lax.Precision.HIGHEST)
    picked_spread = jnp.einsum("ksn,kno->kso", onehot, tile_spread, precision=lax.Precision.HIGHEST)
    live_slots = jnp.arange(SLOTS, dtype=jnp.int32)[None, :] < obs_count[:, None]
    innovation = jnp.where(
        live_slots[:, :, None], (obs_value - picked_mean) / picked_spread, jnp.float32(0.0)
    )
    return (out_cov[None], out_mean[None], local_mean, local_spread, innovation)


BLOCK = 256
RING = 4
TAIL = 16
VMEM = 12 * 1024 * 1024
ALL_VMEM = 56 * 1024 * 1024
NT = (((1,), (1,)), ((), ()))
F32 = jnp.float32
BF16 = jnp.bfloat16


def cols(index):
    return pl.ds(pl.multiple_of(index * BLOCK, BLOCK), BLOCK)


def spot(z, shift):
    return lax.rem(z + shift, RING)


def dot(a, b):
    return jnp.dot(a, b, preferred_element_type=F32)


def dot_nt(a, b):
    return lax.dot_general(a, b, NT, preferred_element_type=F32)


def owns_far(row):
    return (row == 0) | (row == RING - 1)


def each_parcel(parcels, body):
    for a, entry in enumerate(parcels):
        if isinstance(entry, tuple):
            condition, one, other = entry
            pl.when(condition)(functools.partial(body, a, one))
            pl.when(jnp.logical_not(condition))(functools.partial(body, a, other))
        else:
            body(a, entry)


def by_relay(z, own, after, across, before, handed):
    return own, after, across, (z > 0, before, handed)


def lay_out(z, parcels, full, mean):
    def body(a, parcel):
        at = spot(z, a)
        row, near, far = cols(at), cols(spot(z, a + 1)), cols(spot(z, a + 2))
        full[row, row] = parcel[:BLOCK, :BLOCK]
        beside = parcel[:BLOCK, BLOCK : 2 * BLOCK]
        full[row, near] = beside
        full[near, row] = beside.T
        mean[:, row] = parcel[BLOCK:, :BLOCK]

        @pl.when(owns_far(at))
        def _():
            block = parcel[:BLOCK, 2 * BLOCK :]
            full[row, far] = block
            full[far, row] = block.T

    each_parcel(parcels, body)


def keep_parcels(z, parcels, half, half_mean):
    def body(a, parcel):
        at = spot(z, a)
        half_mean[:, cols(at)] = parcel[BLOCK:, :BLOCK]
        half[at, 2 * BLOCK :, :] = parcel[:BLOCK, :BLOCK]
        half[spot(z, a + 1), BLOCK : 2 * BLOCK, :] = parcel[:BLOCK, BLOCK : 2 * BLOCK] * 2

        @pl.when(owns_far(at))
        def _():
            half[spot(z, a + 2), :BLOCK, :] = parcel[:BLOCK, 2 * BLOCK :] * 2

    each_parcel(parcels, body)


def keep_whole(full, mean, half, half_mean):
    half_mean[...] = mean[...]
    for b in range(RING):
        column = slice(b * BLOCK, (b + 1) * BLOCK)
        for j in range(3):
            if j < 2 or b in (1, 2):
                row = (b - j) % RING * BLOCK
                block = full[row : row + BLOCK, column]
                half[b, (2 - j) * BLOCK : (3 - j) * BLOCK, :] = block * 2 if j else block


def fetch(source, z, tail, parcel, sems):
    copies = []
    for j in range(3):
        target = parcel.at[pl.ds(0, BLOCK), pl.ds(j * BLOCK, BLOCK)]
        copies.append(pltpu.make_async_copy(source.at[:, cols(spot(z, j))], target, sems.at[j]))
    for copy in copies:
        copy.start()
    parcel[BLOCK:, :] = jnp.zeros((TAIL, 3 * BLOCK), BF16)
    parcel[BLOCK:, :BLOCK] = tail.astype(BF16)
    for copy in copies:
        copy.wait()


def group_mean(group, end_mean):
    mean = jnp.zeros((1, BLOCK), F32)
    for g in range(end_mean.shape[0]):
        mean = jnp.where(group == g, end_mean[g : g + 1, :].astype(F32), mean)
    return jnp.broadcast_to(mean, (TAIL, BLOCK))


def pack_kernel(where, end_cov, noise, end_mean, offset, parcel, sems):
    z, seg, group = where[0], where[1], where[2]

    @pl.when(seg == 1)
    def _():
        high = offset[...].astype(BF16).astype(F32)
        first = lax.broadcasted_iota(jnp.int32, (TAIL, BLOCK), 0) == 0
        fetch(noise, z, jnp.where(first, high, offset[...] - high), parcel, sems)

    @pl.when(seg != 1)
    def _():
        fetch(end_cov.at[group], z, group_mean(group, end_mean), parcel, sems)


def pairs_kernel(at_seg, where, g0, g1, g2, noise, offset, *refs):
    z, seg, group = where[0], where[1], where[2]
    if at_seg == GROUP_SEGS - 1:
        end_cov, end_mean, *others, half, half_mean, parcel, mean_row, full, mean, own = refs
        parcels = (own, *others)
    else:
        p2, p1, p3, p0, early, _, _, half, half_mean, parcel, mean_row, beside, far, full, mean = refs
        parcels = (p0, p1, p2, p3)

    @pl.when(seg == at_seg)
    def _():
        if at_seg == GROUP_SEGS - 1:
            for j in range(3):
                own[:BLOCK, j * BLOCK : (j + 1) * BLOCK] = end_cov[group, :, cols(spot(z, j))]
            own[BLOCK:, :BLOCK] = group_mean(group, end_mean).astype(BF16)
        lay_out(z, parcels, full, mean)
        product = dot(g0[...], full[...]).astype(BF16)
        for j, gain in enumerate((g0, g1, g2)):
            block = dot_nt(product, gain[...]) + noise[:, cols(spot(z, j))].astype(F32)
            parcel[:BLOCK, j * BLOCK : (j + 1) * BLOCK] = block.astype(BF16)
        new_mean = (dot_nt(mean[...], g0[...]) + offset[...]).astype(BF16)
        parcel[BLOCK:, :BLOCK] = new_mean
        parcel[BLOCK:, BLOCK:] = jnp.zeros((TAIL, 2 * BLOCK), BF16)
        mean_row[...] = new_mean
        keep_whole(full, mean, half, half_mean)

    if at_seg < GROUP_SEGS - 1:
        @pl.when(seg == GROUP_SEGS - 1)
        def _():
            parcel[...] = early[...]

        beside[...] = parcel[:BLOCK, BLOCK : 2 * BLOCK]
        far[...] = parcel[:BLOCK, 2 * BLOCK :]


def hand_kernel(at_seg, where, event, gain, out, sem):
    @pl.when(where[1] == at_seg)
    def _():
        copy = pltpu.make_async_copy(gain, out, sem)
        copy.start()
        copy.wait()


def stack_kernel(where, event, g0, g1, g2, g3, n0, n1, n2, n3, lift):
    z, seg = where[0], where[1]
    states = g0.shape[1]

    @pl.when(seg == 1)
    def _():
        for a, gain in enumerate((g0, g1, g2, g3)):
            lift[cols(spot(z, a)), :] = gain[...]
        lay_out(z, (n0, n1, n2, n3), lift.at[pl.ds(states, states)], lift.at[pl.ds(2 * states, TAIL)])


def turn_kernel(where, near, far, b2, t2, t1, t3, t4, t0, out):
    def body(a, parcel):
        out[a] = parcel[...]

    @pl.when(where[1] == 1)
    def _():
        each_parcel(by_relay(where[0], t0, t1, t2, t3, t4), body)


def ahead_kernel(where, event, lift, gain, step_gain, block_1, block_2, left, base, through, beside, block_1_on, block_2_on):
    seg = where[1]
    states = gain.shape[1]

    @pl.when(seg > 1)
    def _():
        block_1_on[...] = block_1[...]
        block_2_on[...] = block_2[...]

    @pl.when(seg == 0)
    def _():
        through[...] = dot(gain[...], lift[:states, :]).astype(BF16)
        beside[...] = dot(gain[...], lift[states : 2 * states, :])

        def one(k, carry):
            rows = step_gain[k]
            left[k] = dot(rows, lift[:states, :]).astype(BF16)
            value = dot(rows, lift[states : 2 * states, :]) * rows.astype(F32)
            base[pl.ds(k, 1), :] = row_sums(value)
            return carry

        lax.fori_loop(0, step_gain.shape[0], one, 0, unroll=4)


def row_sums(value):
    total = value[:, :128]
    for at in range(128, value.shape[1], 128):
        total = total + value[:, at : at + 128]
    return jnp.sum(total.T, axis=0, keepdims=True)


def moments_kernel(where, ends_1, ends_0, lift, left, base, gain, offset, var, kept, kept_mean, half, half_mean, out_mean, out_spread, out):
    z, seg = where[0], where[1]
    states = gain.shape[2]

    @pl.when(seg == 1)
    def _():
        keep_parcels(z, [ends_1.at[a] for a in range(RING)], half, half_mean)

    @pl.when(seg == 0)
    def _():
        keep_parcels(z, [ends_0.at[a] for a in range(RING)], half, half_mean)
        tail = lift[2 * states :, :].astype(F32)
        half_mean[...] = (dot_nt(half_mean[...], lift[:states, :]) + tail[0:1] + tail[1:2]).astype(BF16)

    def steps(rows_of, more):
        def one(k, carry):
            total = jnp.zeros((BLOCK, BLOCK), F32)
            for b in range(RING):
                blocks = (b + 2, b + 3, b) if b in (1, 2) else (b + 3, b)
                parts = [rows_of[k, :, (r % RING) * BLOCK : (r % RING + 1) * BLOCK] for r in blocks]
                value = dot(jnp.concatenate(parts, axis=1), half[b, (3 - len(blocks)) * BLOCK :, :])
                total = total + value * parts[-1].astype(F32)
            spread = row_sums(total) + var[pl.ds(k, 1), :]
            if more is not None:
                spread = spread + more[pl.ds(k, 1), :]
            means = dot_nt(half_mean[...], gain[k])[0:1] + offset[pl.ds(k, 1), :]
            out[0, pl.ds(k, 1), :] = means
            out[1, pl.ds(k, 1), :] = spread
            out_mean[pl.ds(k, 1), :] = means
            out_spread[pl.ds(k, 1), :] = spread
            return carry

        lax.fori_loop(0, gain.shape[0], one, 0, unroll=4)

    @pl.when(seg == 0)
    def _():
        steps(left, base)

    @pl.when(seg != 0)
    def _():
        steps(gain, None)


def last_kernel(where, g0, a1, a2, a3, ends_1, ends_0, lift, through, beside, noise, offset, means, own, far, near, rows, mean_row, product, full, mean):
    z, seg = where[0], where[1]
    states = g0.shape[1]
    mean_row[...] = (dot_nt(means[...], g0[...]) + offset[...]).astype(BF16)

    @pl.when(seg == 0)
    def _():
        lay_out(z, [ends_0.at[a] for a in range(RING)], full, mean)
        half_way = dot(through[...], full[...]).astype(BF16)
        product[...] = (dot_nt(half_way, lift[:states, :]) + beside[...]).astype(BF16)

    @pl.when(seg == 1)
    def _():
        lay_out(z, [ends_1.at[a] for a in range(RING)], full, mean)
        finish(z, dot(g0[...], full[...]).astype(BF16), (g0, a1, a2, a3), noise, rows)

    @pl.when(seg > 1)
    def _():
        rows[:, cols(z)] = own[:BLOCK, :BLOCK]
        rows[:, cols(spot(z, 1))] = own[:BLOCK, BLOCK : 2 * BLOCK]
        rows[:, cols(spot(z, 3))] = near[...].T

        @pl.when(owns_far(z))
        def _():
            rows[:, cols(spot(z, 2))] = own[:BLOCK, 2 * BLOCK :]

        @pl.when(jnp.logical_not(owns_far(z)))
        def _():
            rows[:, cols(spot(z, 2))] = far[...].T


def finish(z, product, gains, noise, rows):
    for a, gain in enumerate(gains):
        column = cols(spot(z, a))
        rows[:, column] = (dot_nt(product, gain[...]) + noise[:, column].astype(F32)).astype(BF16)


def innovation_kernel(where, tiles, counts, s0, s1, s2, s3, value, noise, mean_1, mean_2, mean_3, product, g0, b1, b2, b3, cov_noise, _, out, mean_row, rows_out, full, rows, sem):
    z, seg = where[0], where[1]
    copy = pltpu.make_async_copy(rows, rows_out, sem)

    @pl.when(seg == 0)
    def _():
        finish(z, product[...], (g0, b1, b2, b3), cov_noise, rows)
        copy.start()

    mean = mean_1[0:1].astype(F32)
    for at, source in ((2, mean_2), (3, mean_3)):
        mean = jnp.where(seg == at, source[0:1].astype(F32), mean)
    mean_row[...] = mean.astype(BF16)
    for a, part in enumerate((s0, s1, s2, s3)):
        full[:, :, cols(spot(z, a))] = part[...]
    full[1] = full[1] + noise[...]
    for k in range(value.shape[0]):
        for j in range(SLOTS):
            at = pl.ds(pl.multiple_of(tiles[j, k] * TILE_STATES, TILE_STATES), TILE_STATES)
            result = (value[k, j : j + 1, :] - full[0, k : k + 1, at]) / full[1, k : k + 1, at]
            out[k, j : j + 1, :] = jnp.where(j < counts[k], result, 0.0)

    @pl.when(seg == 0)
    def _():
        copy.wait()


def smem():
    return pl.BlockSpec(memory_space=pltpu.SMEM)


def vmem():
    return pl.BlockSpec(memory_space=pltpu.VMEM)


def params():
    return pltpu.CompilerParams(vmem_limit_bytes=VMEM)


def cost(flops, moved):
    return pl.CostEstimate(flops=int(flops), bytes_accessed=int(moved), transcendentals=0)


def shape(dims, kind=BF16):
    return jax.ShapeDtypeStruct(dims, kind)


def ring_shards(groups, seg_gain, seg_offset, seg_noise, end_mean, end_cov, step_gain, step_offset, step_var, obs_tiles, obs_count, obs_value, obs_noise):
    position = lax.axis_index("tm")
    z = lax.axis_index("tile")
    where = jnp.stack([z, position % GROUP_SEGS, position // GROUP_SEGS]).astype(jnp.int32)
    gain, noise = seg_gain[0], seg_noise[0]
    states = gain.shape[1]
    steps = step_gain.shape[0]
    parcel_shape = shape((BLOCK + TAIL, 3 * BLOCK))

    def route(block, moves):
        table = []
        for g in range(groups):
            for (source, start), (target, end) in moves:
                table.append(((g * GROUP_SEGS + source) * RING + start, (g * GROUP_SEGS + target) * RING + end))
        return lax.ppermute(block, ("tm", "tile"), table)

    def send(block, pairs, shift):
        return route(block, [((a, (to + shift) % RING), (b, to)) for a, b in pairs for to in range(RING)])

    def exchange(block, pairs, own=None):
        others = [send(block, pairs, a) for a in (2, 1, 3)]
        return [send(block, pairs, 0) if own is None else own, others[1], others[0], others[2]]

    def within(segments, steps):
        return [((a, start), (a, to)) for a in segments for start, to in steps]

    def call(kernel, name, out_shape, operands, scratch, flops, aliases={}):
        moved = sum(x.size * x.dtype.itemsize for x in list(operands) + list(out_shape))
        return pl.pallas_call(
            kernel,
            out_shape=out_shape,
            in_specs=[smem()] + [vmem()] * len(operands),
            out_specs=(vmem(),) * len(out_shape),
            scratch_shapes=scratch,
            input_output_aliases=aliases,
            compiler_params=params(),
            cost_estimate=cost(flops, moved),
            name=name,
        )(where, *operands)

    def pack(kernel, name, out_shape, far_operands, near_operands, sems, limit):
        return pl.pallas_call(
            kernel,
            out_shape=out_shape,
            in_specs=[smem()] + [pl.BlockSpec(memory_space=pl.ANY)] * len(far_operands) + [vmem()] * len(near_operands),
            out_specs=jax.tree.map(lambda _: vmem(), out_shape),
            scratch_shapes=[sems],
            compiler_params=pltpu.CompilerParams(vmem_limit_bytes=limit),
            cost_estimate=cost(0, 1e6),
            name=name,
        )(where, *far_operands, *near_operands)

    full_and_mean = [pltpu.VMEM((states, states), BF16), pltpu.VMEM((TAIL, states), BF16)]
    row_shape, mean_shape, block_shape = shape((BLOCK, states)), shape((TAIL, BLOCK)), shape((BLOCK, BLOCK))
    half_shapes = (shape((RING, 3 * BLOCK, BLOCK)), shape((TAIL, states)))

    back, two_on, on = ((1, 0), (2, 1), (3, 2), (0, 3)), ((0, 2), (1, 3), (2, 0), (3, 1)), ((0, 1), (1, 2), (2, 3), (3, 0))
    pair_gains = [route(gain, within((3, 2, 1), back)), route(gain, within((3, 2), ((2, 0), (1, 3))) + within((1,), on))]
    parcel = pack(pack_kernel, "pack", parcel_shape, (end_cov, noise), (end_mean, seg_offset), pltpu.SemaphoreType.DMA((3,)), ALL_VMEM)
    far_moves = [((0 if to else 3, start), (3, to)) for start, to in two_on] + within((1,), two_on)
    first = [send(parcel, ((3, 3), (1, 1)), 1), route(parcel, far_moves), send(parcel, ((3, 3), (1, 1)), 3)]

    def hand(segment, event):
        kernel = functools.partial(hand_kernel, segment)
        return pack(kernel, f"hand_{segment}", row_shape, (event, gain), (), pltpu.SemaphoreType.DMA, VMEM)

    gains_1 = [pair_gains[0], route(hand(1, first[1]), within((1,), two_on)), pair_gains[1]]

    flops = 4 * BLOCK * states * states
    *kept, parcel_3, mean_3 = call(
        functools.partial(pairs_kernel, 3),
        "pairs_3",
        (*half_shapes, parcel_shape, mean_shape),
        (gain, *pair_gains, noise, seg_offset, end_cov, end_mean, *first),
        full_and_mean + [pltpu.VMEM(parcel_shape.shape, BF16)],
        flops,
    )
    second = exchange(parcel_3, ((3, 2),))

    *kept, parcel_2, mean_2, beside_block, far_block = call(
        functools.partial(pairs_kernel, 2),
        "pairs_2",
        (*half_shapes, parcel_shape, mean_shape, block_shape, block_shape),
        (gain, *pair_gains, noise, seg_offset, second[2], second[1], second[3], second[0], parcel_3, *kept),
        full_and_mean,
        flops,
        {11: 0, 12: 1},
    )
    own = send(parcel_2, ((2, 1),), 0)
    across = send(parcel_2, ((2, 1),), 2)
    sides = [
        route(parcel_2, [((2, start), (1, to)) for start, to in moves])
        for moves in (((1, 0), (2, 1), (3, 2), (0, 3)), ((0, 1), (1, 2), (2, 3)))
    ]
    third = [own, sides[0], across, sides[1], route(across, within((1,), ((1, 0),)))]
    (lift,) = call(stack_kernel, "stack", (shape((2 * states + TAIL, states)),), (parcel_2, gain, *gains_1, parcel, *first), [], 0)
    lift = send(lift, ((1, 0),), 0)
    gain_0 = hand(0, lift)
    left, base, through, beside, beside_block, far_block = call(
        ahead_kernel,
        "ahead",
        (shape(step_gain.shape), shape((steps, BLOCK), F32), row_shape, shape((BLOCK, states), F32), block_shape, block_shape),
        (gain_0, lift, gain, step_gain, beside_block, far_block),
        [],
        4 * (steps + 1) * BLOCK * states * states,
    )
    gains_0 = [route(gain_0, within((0,), moves)) for moves in (back, two_on, on)]
    near, far = route(beside_block, within((3, 2), on)), route(far_block, within((3, 2), ((0, 2), (3, 1))))
    (ends_1,) = call(turn_kernel, "turn", (shape((RING, *parcel_shape.shape)),), (near, far, gains_0[1], third[2], third[1], third[3], third[4], third[0]), [], 0)
    ends_0 = send(ends_1, ((1, 0),), 0)
    out_steps = shape((steps, BLOCK), F32)
    _, means, step_mean, step_spread, stats = call(
        moments_kernel,
        "moments",
        (*half_shapes, out_steps, out_steps, shape((2, steps, BLOCK), F32)),
        (ends_1, ends_0, lift, left, base, step_gain, step_offset, step_var, *kept),
        [],
        2 * steps * BLOCK * states * states,
        {9: 0, 10: 1},
    )
    everyone = tuple((s, s) for s in range(GROUP_SEGS))
    all_stats = [stats] + [send(stats, everyone, a) for a in range(1, RING)]
    rows, mean_1, product = call(
        last_kernel,
        "last",
        (row_shape, mean_shape, row_shape),
        (gain, *gains_1, ends_1, ends_0, lift, through, beside, noise, seg_offset, means, parcel_2, far, near),
        full_and_mean,
        flops,
    )
    innovation, out_mean, out_cov = pl.pallas_call(
        innovation_kernel,
        out_shape=(shape(obs_value.shape, F32), shape((1, BLOCK)), row_shape),
        in_specs=[smem()] * 3 + [vmem()] * 15 + [pl.BlockSpec(memory_space=pl.ANY)],
        out_specs=(vmem(), vmem(), pl.BlockSpec(memory_space=pl.ANY)),
        scratch_shapes=[pltpu.VMEM((2, steps, states), F32), pltpu.VMEM(row_shape.shape, BF16), pltpu.SemaphoreType.DMA],
        input_output_aliases={18: 2},
        compiler_params=params(),
        cost_estimate=cost(0, 2e5),
        name="innovation",
    )(where, obs_tiles.T, obs_count, *all_stats, obs_value, obs_noise.reshape(1, states), mean_1, mean_2, mean_3, product, gain, *gains_0, noise, rows)
    return out_cov[None], out_mean, step_mean, step_spread, innovation


def solution(mesh):
    in_specs = (
        P("tm", "tile", None),
        P("tm", "tile"),
        P("tm", "tile", None),
        P(None, "tile"),
        P(None, "tile", None),
        P("tm", "tile", None),
        P("tm", "tile"),
        P("tm", "tile"),
        P("tm", None),
        P("tm"),
        P("tm", None, None),
        P(),
    )
    out_specs = (
        P("tm", "tile", None),
        P("tm", "tile"),
        P("tm", "tile"),
        P("tm", "tile"),
        P("tm", None, None),
    )
    if mesh.shape["tile"] == RING:
        shards = functools.partial(ring_shards, mesh.shape["tm"] // GROUP_SEGS)
    else:
        shards = general_shards
    return jax.shard_map(shards, mesh=mesh, in_specs=in_specs, out_specs=out_specs, check_vma=False)
```
